256 devices in a mesh: layer: 4 (over y), shower: 64 (over x, z, core).
Axes of the slice: x: 4, y: 4, z: 8, core: 2. Of those that a mesh axis runs over, the one named last changes fastest.
Arguments:
- showers: bfloat16 [32768, 6336], P('shower', 'layer'), may hold values from -6 to 6
- geometry: bfloat16 [6336, 1024], P('layer'), may hold values from -0.109375 to 0.109375
- pattern: int32 [44, 8], P('layer'), may hold values 0 or 1
- bins: int32 [256], P('shower'), may hold values from 0 to 7, as said below
- sources: int32 [256], P('shower'), may hold values from 0 to 1
Outputs:
- proof: float32 [32768], P('shower')
The draws below stay inside these ranges and needn't reach their ends.
Inputs may be any that keep to these rules, and one draw needn't show every extreme that they name: `bins`: the blocks of one bin are consecutive; the bin of block 0 holds exactly 129 blocks, every other bin 2 or more; every pair of bin and source is held by at least one block.
All inputs are finite; a program needn't handle non-finite values. No bound on the sum of `pattern` on one device may be relied on, other than what follows from the above.
Results may differ from the reference program's by a relative error of at most 0.0046.
Values may be sent and summed in bfloat16 or wider, within the bound.
No kernel may reach another device: no remote copies, remote signals or barrier semaphores. Data moves between devices by JAX's collectives and lax.ppermute only.
A program may use at most 64 MiB of HBM per device.

```python
import math
import jax
import jax.numpy as jnp
from jax import lax

LAYERS = 44
CELLS = 144
FEATURES = 1024
FEAT_BLOCK = 128
BLOCK_ROWS = 128
ENERGY_BINS = 8
ROWS_DEV = 512
VOXELS = 6336
SHOWERS = 32768
BLOCKS = 256
MAX_RUN = 129


def label_layout(key):
    order_key, cut_key, first_key, second_key, source_key = jax.random.split(key, 5)
    spare = BLOCKS - MAX_RUN - 2 * (ENERGY_BINS - 1)
    cuts = jnp.sort(jax.random.randint(cut_key, (ENERGY_BINS - 2,), 0, spare + 1).astype(jnp.int32))
    bounds = jnp.concatenate([jnp.zeros((1,), jnp.int32), cuts, jnp.full((1,), spare, jnp.int32)])
    rest_len = (bounds[1:] - bounds[:-1] + 2).astype(jnp.int32)
    lengths = jnp.concatenate([jnp.full((1,), MAX_RUN, jnp.int32), rest_len]).astype(jnp.int32)
    ends = jnp.cumsum(lengths).astype(jnp.int32)
    starts = ends - lengths
    block_ids = jnp.arange(BLOCKS, dtype=jnp.int32)
    run_index = jnp.sum((block_ids[:, None] >= ends[None, :]).astype(jnp.int32), axis=1)
    order = jax.random.permutation(order_key, ENERGY_BINS).astype(jnp.int32)
    bin_ids = order[run_index]
    source_ids = jax.random.randint(source_key, (BLOCKS,), 0, 2).astype(jnp.int32)
    first_off = jax.random.randint(first_key, (ENERGY_BINS,), 0, lengths).astype(jnp.int32)
    step_off = jax.random.randint(second_key, (ENERGY_BINS,), 0, lengths - 1).astype(jnp.int32) + 1
    first = starts + first_off
    second = starts + (first_off + step_off) % lengths
    source_ids = source_ids.at[first].set(0).at[second].set(1)
    return (bin_ids, source_ids)


def draw_bins(key, part):
    return label_layout(key)[0].astype(jnp.int32)


def draw_sources(key, part):
    return label_layout(key)[1].astype(jnp.int32)


def plant(entries, own_key, low, top_value):
    extent = entries.shape
    index_at = [jax.random.randint(jax.random.fold_in(own_key, axis), (), 0, extent[axis]) for axis in range(len(extent))]
    entries = entries.at[tuple(index_at)].set(low)
    longest = extent.index(max(extent))
    index_at[longest] = (index_at[longest] + 1) % extent[longest]
    return entries.at[tuple(index_at)].set(top_value)


def shard_levels(rng, extent, shards, low, top_value):
    def one(position, shards_of):
        heights = jax.random.uniform(jax.random.fold_in(jax.random.fold_in(rng, 6), position), (shards_of,), jnp.float32, low / len(shards), top_value / len(shards))
        return jnp.repeat(jnp.exp(heights), extent[position] // shards_of).reshape((-1,) + (1,) * (len(extent) - position - 1))

    factor_of = one(*shards[0])
    for cut in shards[1:]:
        factor_of = factor_of * one(*cut)
    return factor_of


def bell_draw(own_key, shape, scale, most, cuts=(), kind=jnp.bfloat16):
    level = shard_levels(own_key, shape, cuts, -0.22, 0.18) if cuts else 1.0
    values = jax.random.normal(own_key, shape, jnp.float32) * scale * level
    return jnp.minimum(jnp.maximum(values, -most), most).astype(kind)


def setup_inputs(seed: int = 0) -> dict:
    arg_keys = jax.random.split(jax.random.key(seed), 6)
    showers = bell_draw(arg_keys[0], (SHOWERS, VOXELS), 1.0, 6.0, ((0, 64), (1, 4)))
    geometry = bell_draw(arg_keys[1], (VOXELS, FEATURES), (VOXELS // 2) ** -0.5, 0.109375, ((0, 4),))
    pattern = plant((jax.random.randint(arg_keys[2], (LAYERS, FEATURES // FEAT_BLOCK), 0, 2) < 1).astype(jnp.int32), jax.random.fold_in(arg_keys[2], 1), 0, 1)
    bins = draw_bins(jax.random.fold_in(arg_keys[5], 71), 0)
    sources = draw_sources(jax.random.fold_in(arg_keys[5], 71), 0)
    return dict(showers=showers, geometry=geometry, pattern=pattern, bins=bins, sources=sources)


def normalize(values):
    scale = lax.rsqrt(lax.optimization_barrier(jnp.mean(values * values, axis=1, keepdims=True)) + 1e-05)
    return (values * scale).astype(jnp.bfloat16)

def reference(showers, geometry, pattern, bins, sources):
    expanded = jnp.repeat(jnp.repeat(pattern.astype(jnp.bfloat16), CELLS, axis=0), FEAT_BLOCK, axis=1)
    feats = normalize(jnp.dot(showers, geometry * expanded, preferred_element_type=jnp.float32))
    codes = bins + ENERGY_BINS * sources
    onehot = (codes[:, None] == jnp.arange(2 * ENERGY_BINS, dtype=jnp.int32)[None, :]).astype(jnp.float32)
    counts = lax.optimization_barrier(jnp.sum(onehot, axis=0)) * BLOCK_ROWS
    signs = jnp.where(jnp.arange(2 * ENERGY_BINS, dtype=jnp.int32) >= ENERGY_BINS, 1.0, -1.0).astype(jnp.float32)
    block_coef = lax.optimization_barrier(jnp.sum(jnp.where(onehot > 0.5, (signs / counts)[None, :], 0.0), axis=1))
    row_bin = jnp.repeat(bins, BLOCK_ROWS)
    row_coef = jnp.repeat(block_coef, BLOCK_ROWS)
    positions = jnp.arange(SHOWERS, dtype=jnp.int32)
    inv_root = 1.0 / math.sqrt(FEATURES)

    def one_block(index):
        first_row = (index * ROWS_DEV).astype(jnp.int32)
        block_feats = lax.dynamic_slice_in_dim(feats, first_row, ROWS_DEV, 0)
        block_bin = lax.dynamic_slice_in_dim(row_bin, first_row, ROWS_DEV, 0)
        block_pos = lax.dynamic_slice_in_dim(positions, first_row, ROWS_DEV, 0)
        products = lax.dot_general(block_feats.astype(jnp.float32), feats.astype(jnp.float32), (((1,), (1,)), ((), ())))
        shifted = products * inv_root + 1.0
        kernel_vals = shifted * shifted * shifted
        matches = (block_bin[:, None] == row_bin[None, :]) & (block_pos[:, None] != positions[None, :])
        return lax.optimization_barrier(jnp.sum(jnp.where(matches, kernel_vals * row_coef[None, :], 0.0), axis=1))
    proof = lax.map(one_block, jnp.arange(SHOWERS // ROWS_DEV, dtype=jnp.int32))
    return proof.reshape(SHOWERS)
```

```python
import functools

import jax
import jax.numpy as jnp
from jax import lax
from jax.experimental import pallas as pl
from jax.experimental.pallas import tpu as pltpu
from jax.sharding import PartitionSpec as P

BLOCK = 128
TAG = 16
AXES = ("layer", "shower")
NY, NX, NZ, NC = 4, 4, 8, 2


def flat(y, x, z, c):
    return y * (NX * NZ * NC) + (x * NZ + z) * NC + c


def permute(value, move, keep=lambda y, x, z, c: True):
    pairs = [
        (flat(y, x, z, c), flat(*move(y, x, z, c)))
        for y in range(NY)
        for x in range(NX)
        for z in range(NZ)
        for c in range(NC)
        if keep(y, x, z, c)
    ]
    return lax.ppermute(value, AXES, pairs)


def along_y(step):
    return lambda y, x, z, c: ((y + step) % NY, x, z, c)


def swap_x(y, x, z, c):
    return (y, x ^ 1, z, c)


def raw_kernel(pattern, showers, geometry, out, masked):
    step = pl.program_id(0)
    cells = geometry.shape[0] // pattern.shape[0]
    per = geometry.shape[1] // BLOCK
    for layer in range(pattern.shape[0]):
        for part in range(per):
            rows = pl.ds(layer * cells, cells)
            cols = pl.ds(part * BLOCK, BLOCK)
            on = pattern[layer, step * per + part].astype(jnp.float32).astype(jnp.bfloat16)
            masked[rows, cols] = geometry[rows, cols] * on
    out[...] = jnp.dot(showers[...], masked[...], preferred_element_type=jnp.float32)


def raw_partial(showers, geometry, pattern):
    rows, depth = showers.shape
    feats = geometry.shape[1]
    width = 256
    return pl.pallas_call(
        raw_kernel,
        grid=(feats // width,),
        in_specs=[
            pl.BlockSpec(memory_space=pltpu.SMEM),
            pl.BlockSpec((rows, depth), lambda i: (0, 0)),
            pl.BlockSpec((depth, width), lambda i: (0, i)),
        ],
        out_specs=pl.BlockSpec((rows, width), lambda i: (0, i)),
        out_shape=jax.ShapeDtypeStruct((rows, feats), jnp.float32),
        scratch_shapes=[pltpu.VMEM((depth, width), jnp.bfloat16)],
        compiler_params=pltpu.CompilerParams(vmem_limit_bytes=40 * 2**20),
        cost_estimate=pl.CostEstimate(
            flops=2 * rows * depth * feats, bytes_accessed=8 * 2**20, transcendentals=0
        ),
        name="raw",
    )(pattern, showers, geometry)


def pair_kernel(
    place, bins, own, x1, ya, yb, xx, y2a, y2b, w2a, w2b, extra, cols, before, out, rows_at, diag_on
):
    step = pl.program_id(0)
    y, z, c = place[0], place[1], place[2]
    half = BLOCK // 2
    main = 2 * NY * BLOCK

    @pl.when(step == 0)
    def _():
        def put(side, turn, ref, start, size, shift):
            row = side * NY * BLOCK + lax.rem(y + turn, NY) * BLOCK + shift
            rows_at[pl.ds(pl.multiple_of(row, half), size), :] = ref[pl.ds(start, size), :]

        put(0, 0, own, 0, BLOCK, 0)
        put(0, 3, ya, 0, BLOCK, 0)
        put(0, 1, yb, 0, BLOCK, 0)
        put(0, 2, y2a, 0, half, 0)
        put(0, 2, y2b, 0, half, half)
        put(1, 0, x1, 0, BLOCK, 0)
        put(1, 3, xx, 0, BLOCK, 0)
        put(1, 1, xx, BLOCK, BLOCK, 0)
        put(1, 2, w2a, 0, half, 0)
        put(1, 2, w2b, 0, half, half)
        rows_at[pl.ds(main, BLOCK), :] = extra[...]
        out[...] = before[...]

    def work(with_diag):
        count = cols.shape[0] // (BLOCK + TAG)
        for part in range(count):
            block = cols[pl.ds(part * (BLOCK + TAG), BLOCK), :]
            tag = cols[pl.ds(part * (BLOCK + TAG) + BLOCK, TAG), :].astype(jnp.float32)
            code = jnp.max(tag, axis=0, keepdims=True)[:, :BLOCK] - 1.0
            source = (code >= 8.0).astype(jnp.float32)
            bin_id = code - 8.0 * source
            products = lax.dot_general(
                block, rows_at[...], (((1,), (1,)), ((), ())), preferred_element_type=jnp.float32
            )
            shifted = products + 32.0
            cubes = shifted * shifted * shifted
            if with_diag:
                lane = lax.broadcasted_iota(jnp.int32, cubes.shape, 1)
                sub = lax.broadcasted_iota(jnp.int32, cubes.shape, 0)
                same = (lane - y * BLOCK == sub) & (c == part)
                cubes = jnp.where(same, 0.0, cubes)
            sums = jnp.sum(cubes, axis=0, keepdims=True)
            for at in range(cubes.shape[1] // BLOCK):
                lanes = pl.ds(at * BLOCK, BLOCK)
                match = (bins[0:1, lanes] == bin_id).astype(jnp.float32)
                one = match * source
                zero = match - one
                total = sums[:, at * BLOCK : (at + 1) * BLOCK]
                out[0:1, lanes] += one * total
                out[1:2, lanes] += zero * total
                out[2:3, lanes] += one
                out[3:4, lanes] += zero

    if diag_on:

        @pl.when(step == z)
        def _():
            work(True)

        @pl.when(step != z)
        def _():
            work(False)
    else:
        work(False)


def pair_sums(place, bins, parts, cols, before, diag_on):
    size = cols.shape[0] // (BLOCK + TAG)
    per = min(size, NC)
    feats = cols.shape[1]
    rows = bins.shape[1]
    whole = lambda ref: pl.BlockSpec(ref.shape, lambda i: (0, 0))
    return pl.pallas_call(
        functools.partial(pair_kernel, diag_on=diag_on),
        grid=(size // per,),
        in_specs=[
            pl.BlockSpec(memory_space=pltpu.SMEM),
            whole(bins),
            *[whole(part) for part in parts],
            pl.BlockSpec((per * (BLOCK + TAG), feats), lambda i: (i, 0)),
            whole(before),
        ],
        out_specs=pl.BlockSpec((8, rows), lambda i: (0, 0)),
        out_shape=jax.ShapeDtypeStruct((8, rows), jnp.float32),
        scratch_shapes=[pltpu.VMEM((rows, feats), jnp.bfloat16)],
        compiler_params=pltpu.CompilerParams(vmem_limit_bytes=48 * 2**20),
        cost_estimate=pl.CostEstimate(
            flops=2 * rows * size * BLOCK * feats, bytes_accessed=8 * 2**20, transcendentals=0
        ),
        name="pairs",
    )(place, bins, *parts, cols, before)


def shards(showers, geometry, pattern, bins, sources):
    y = lax.axis_index("layer")
    s = lax.axis_index("shower")
    x, z, c = s // (NZ * NC), (s // NC) % NZ, s % NC
    feats = geometry.shape[1]

    partial_sums = raw_partial(showers, geometry, pattern).reshape(NY, BLOCK, feats)
    share = lambda turn: lax.dynamic_index_in_dim(partial_sums, (y + turn) % NY, 0, keepdims=False)
    raw = share(0)
    arrived = [permute(share(turn).astype(jnp.float16), along_y(turn)) for turn in (2, 1, 3)]
    for part in arrived:
        raw = raw + part.astype(jnp.float32)
    scale = lax.rsqrt(jnp.mean(raw * raw, axis=1, keepdims=True) + 1e-05)
    own = (raw * scale).astype(jnp.bfloat16)

    own_code = lax.dynamic_index_in_dim(bins + 8 * sources, y, 0, keepdims=False)
    tag = jnp.full((TAG, feats), own_code + 1, jnp.int32).astype(jnp.bfloat16)
    tagged = jnp.concatenate([own, tag], axis=0)
    lines = [[(i * NZ + j) * NC + k for j in range(NZ) for k in range(NC)] for i in range(NX)]
    cols = lax.all_gather(tagged, "shower", axis_index_groups=lines, axis=0, tiled=True)

    half = BLOCK // 2
    other_bins = permute(bins, swap_x)
    x1 = permute(own, swap_x)
    ya = permute(own, along_y(1))
    yb = permute(own, along_y(3))
    xx = permute(jnp.concatenate([ya, yb], axis=0), swap_x)
    y2a = permute(ya[:half], along_y(1))
    y2b = permute(yb[half:], along_y(3))
    w2a = permute(xx[:half], along_y(1))
    w2b = permute(xx[BLOCK + half :], along_y(3))

    y2 = jnp.concatenate([y2a, y2b], axis=0)
    w2 = jnp.concatenate([w2a, w2b], axis=0)
    near = [own, ya, y2, yb]
    far = [x1, xx[:BLOCK], w2, xx[BLOCK:]]
    odd_row = lax.select_n(y + NY * (x % 2), *near, *far)
    odd_row = permute(
        odd_row,
        lambda y, x, z, c: (y, 3 - x, z, c),
        keep=lambda y, x, z, c: x >= 2 and z == 0 and c == 0,
    )
    odd_col = permute(
        cols[: BLOCK + TAG],
        lambda y, x, z, c: (y, 1, z, c),
        keep=lambda y, x, z, c: y == 0 and x == 2,
    )

    odd_bin = jnp.where((x < 2) & (z == 0) & (c == 0), bins[:1], -2)
    row_bins = jnp.repeat(jnp.concatenate([bins, other_bins, odd_bin]), BLOCK)
    row_bins = jnp.broadcast_to(row_bins.astype(jnp.float32)[None, :], (8, row_bins.shape[0]))
    place = jnp.stack([y, z, c]).astype(jnp.int32)
    parts = (own, x1, ya, yb, xx, y2a, y2b, w2a, w2b, odd_row)
    blank = jnp.zeros((8, row_bins.shape[1]), jnp.float32)
    stats = pair_sums(place, row_bins, parts, cols, blank, True)
    main = 2 * NY * BLOCK
    col_bins = jnp.where(jnp.arange(row_bins.shape[1])[None, :] < main, row_bins, -2.0)
    stats = pair_sums(place, col_bins, parts, odd_col, stats, False)[:4]

    side = NY * BLOCK
    mine = stats[:, :side] + permute(stats[:, side:main], swap_x)
    odd_stats = stats[:, main:]
    for start in (0, 1):
        odd = permute(
            odd_stats,
            lambda y, x, z, c: (y, 2, z, c),
            keep=lambda y, x, z, c, start=start: x == start and z == 0 and c == 0,
        )
        mine = mine + jnp.pad(odd, ((0, 0), (0, side - BLOCK)))
    total = mine
    for turn in (2, 1, 3):
        total = total + permute(mine, along_y(turn))
    weight = 1.0 / (BLOCK * 32.0**3)
    return (total[0] / total[2] - total[1] / total[3]) * weight


def solution(mesh):
    placed = (P("shower", "layer"), P("layer", None), P("layer", None), P("shower"), P("shower"))
    return jax.shard_map(shards, mesh=mesh, in_specs=placed, out_specs=P("shower"), check_vma=False)
```

```python
import functools

import jax
import jax.numpy as jnp
from jax import lax
from jax.experimental import pallas as pl
from jax.experimental.pallas import tpu as pltpu
from jax.sharding import PartitionSpec as P

BLOCK = 128
PIECE = 32
TAG = 16
BINS = 8
CHUNK = 512
AXES = ("layer", "shower")
NY, NX, NZ, NC = 4, 4, 8, 2


def flat(y, x, z, c):
    return y * (NX * NZ * NC) + (x * NZ + z) * NC + c


def permute(value, move, keep=lambda y, x, z, c: True):
    pairs = [
        (flat(y, x, z, c), flat(*move(y, x, z, c)))
        for y in range(NY)
        for x in range(NX)
        for z in range(NZ)
        for c in range(NC)
        if keep(y, x, z, c)
    ]
    return lax.ppermute(value, AXES, pairs)


def along_y(step):
    return lambda y, x, z, c: ((y + step) % NY, x, z, c)


def along_z(step):
    return lambda y, x, z, c: (y, x, (z + step) % NZ, c)


def flip_z(bit):
    return lambda y, x, z, c: (y, x, z ^ bit, c)


def swap_x(y, x, z, c):
    return (y, x ^ 1, z, c)


def swap_core(y, x, z, c):
    return (y, x, z, 1 - c)


def same_core(y, x, z, c):
    return (y, x, (z + 1 - 2 * c) % NZ, c)


def cross_core(y, x, z, c):
    return (y, x, (z - 1 + 2 * c) % NZ, 1 - c)


def raw_kernel(pattern, showers, geometry, out, masked):
    step = pl.program_id(0)
    layers = pattern.shape[1]
    cells = geometry.shape[0] // layers
    per = geometry.shape[1] // BLOCK
    for layer in range(layers):
        for part in range(per):
            rows = pl.ds(layer * cells, cells)
            cols = pl.ds(part * BLOCK, BLOCK)
            on = pattern[step * per + part, layer].astype(jnp.float32).astype(jnp.bfloat16)
            masked[rows, cols] = geometry[rows, cols] * on
    out[...] = lax.dot_general(
        showers[...], masked[...], (((0,), (0,)), ((), ())), preferred_element_type=jnp.float32
    )


def raw_partial(showers, geometry, pattern):
    rows, depth = showers.shape
    feats = geometry.shape[1]
    width = 512
    return pl.pallas_call(
        raw_kernel,
        grid=(feats // width,),
        in_specs=[
            pl.BlockSpec(memory_space=pltpu.SMEM),
            pl.BlockSpec((depth, rows), lambda i: (0, 0)),
            pl.BlockSpec((depth, width), lambda i: (0, i)),
        ],
        out_specs=pl.BlockSpec((rows, width), lambda i: (0, i)),
        out_shape=jax.ShapeDtypeStruct((rows, feats), jnp.float32),
        scratch_shapes=[pltpu.VMEM((depth, width), jnp.bfloat16)],
        compiler_params=pltpu.CompilerParams(vmem_limit_bytes=60 * 2**20),
        cost_estimate=pl.CostEstimate(
            flops=2 * rows * depth * feats, bytes_accessed=8 * 2**20, transcendentals=0
        ),
        name="raw",
    )(pattern.T, showers.T, geometry)


def pair_kernel(*refs, row_sizes, col_sizes, diag, apart):
    n_rows, n_cols = len(row_sizes), len(col_sizes)
    col_bin, col_source, row_bins, before = refs[:4]
    rows = refs[4 : 4 + n_rows]
    cols = refs[4 + n_rows : 4 + n_rows + n_cols]
    out, rows_at, cols_at, row_sems, col_sems = refs[4 + n_rows + n_cols :]

    def copies(sources, sizes, target, sems):
        made, start = [], 0
        for at, (source, size) in enumerate(zip(sources, sizes)):
            copy = pltpu.make_async_copy(
                source.at[pl.ds(0, size), :], target.at[pl.ds(start, size), :], sems.at[at]
            )
            copy.start()
            made.append((copy, start))
            start += size
        return made, start

    col_copies, depth = copies(cols, col_sizes, cols_at, col_sems)
    row_copies, total = copies(rows, row_sizes, rows_at, row_sems)
    for copy, _ in col_copies:
        copy.wait()
    waited = 0
    for start in range(0, total, CHUNK):
        size = min(CHUNK, total - start)
        while waited < n_rows and row_copies[waited][1] < start + size:
            row_copies[waited][0].wait()
            waited += 1
        products = lax.dot_general(
            cols_at[...],
            rows_at[pl.ds(start, size), :],
            (((1,), (1,)), ((), ())),
            preferred_element_type=jnp.float32,
        )
        shifted = products + 32.0
        cubes = shifted * shifted * shifted
        lanes = pl.ds(start, size)
        bins = row_bins[0:1, lanes]
        one = jnp.zeros((8, size), jnp.float32)
        zero = jnp.zeros((8, size), jnp.float32)
        for group in range(depth // PIECE):
            if start >= 16 * BLOCK and group == apart:
                continue
            block = cubes[group * PIECE : (group + 1) * PIECE]
            if diag and start == 0 and group < BLOCK // PIECE:
                lane = lax.broadcasted_iota(jnp.int32, block.shape, 1)
                sub = lax.broadcasted_iota(jnp.int32, block.shape, 0)
                block = jnp.where(lane == sub + group * PIECE, 0.0, block)
            part = block[0:8] + block[8:16] + (block[16:24] + block[24:32])
            match = (bins == col_bin[group]).astype(jnp.float32)
            source = col_source[group]
            one += (match * source) * part
            zero += (match * (1.0 - source)) * part
        out[0:1, lanes] = before[0:1, lanes] + jnp.sum(one, axis=0, keepdims=True)
        out[1:2, lanes] = before[1:2, lanes] + jnp.sum(zero, axis=0, keepdims=True)


def pair_sums(rows, cols, codes, row_bins, before, diag, name, apart=-1):
    row_sizes = tuple(size for _, size in rows)
    col_sizes = tuple(size for _, size in cols)
    total, depth = sum(row_sizes), sum(col_sizes)
    feats = rows[0][0].shape[1]
    col_source = (codes >= BINS).astype(jnp.float32)
    col_bin = codes.astype(jnp.float32) - BINS * col_source
    vmem = pl.BlockSpec(memory_space=pltpu.VMEM)
    smem = pl.BlockSpec(memory_space=pltpu.SMEM)
    hbm = pl.BlockSpec(memory_space=pl.ANY)
    return pl.pallas_call(
        functools.partial(
            pair_kernel, row_sizes=row_sizes, col_sizes=col_sizes, diag=diag, apart=apart
        ),
        in_specs=[smem, smem, vmem, vmem] + [hbm] * (len(rows) + len(cols)),
        out_specs=vmem,
        out_shape=jax.ShapeDtypeStruct((2, total), jnp.float32),
        scratch_shapes=[
            pltpu.VMEM((total, feats), jnp.bfloat16),
            pltpu.VMEM((depth, feats), jnp.bfloat16),
            pltpu.SemaphoreType.DMA((len(rows),)),
            pltpu.SemaphoreType.DMA((len(cols),)),
        ],
        compiler_params=pltpu.CompilerParams(vmem_limit_bytes=58 * 2**20),
        cost_estimate=pl.CostEstimate(
            flops=2 * total * depth * feats,
            bytes_accessed=2 * (total + depth) * feats,
            transcendentals=0,
        ),
        name=name,
    )(col_bin, col_source, row_bins, before, *[r for r, _ in rows], *[c for c, _ in cols])


def line_codes(codes, z, c):
    other = permute(codes, swap_core)
    chip = jnp.where(c == 0, jnp.stack([codes, other]), jnp.stack([other, codes]))
    line = chip[None]
    for bit in (1, 2, 4):
        other = permute(line, flip_z(bit))
        low = (z & bit) == 0
        line = jnp.where(
            low, jnp.concatenate([line, other]), jnp.concatenate([other, line])
        )
    return line, chip


def shards(showers, geometry, pattern, bins, sources):
    y = lax.axis_index("layer")
    s = lax.axis_index("shower")
    x, z, c = s // (NZ * NC), (s // NC) % NZ, s % NC
    feats = geometry.shape[1]
    blocks = bins.shape[0]

    codes = bins + BINS * sources
    line, chip = line_codes(codes, z, c)
    chip_x = permute(chip, swap_x)

    partial_sums = raw_partial(showers, geometry, pattern).reshape(blocks, NY, PIECE, feats)

    def share(turn):
        part = lax.dynamic_index_in_dim(partial_sums, (y + turn) % NY, 1, keepdims=False)
        return part.reshape(BLOCK, feats)

    raw = share(0)
    arrived = [permute(share(turn).astype(jnp.float16), along_y(turn)) for turn in (2, 1, 3)]
    for part in arrived:
        raw = raw + part.astype(jnp.float32)
    scale = lax.rsqrt(jnp.mean(raw * raw, axis=1, keepdims=True) + 1e-05)
    own = (raw * scale).astype(jnp.bfloat16)
    own, line, chip_x = lax.optimization_barrier((own, line, chip_x))

    same, cross = [], []
    for turn in range(4):
        same.append(permute(same[-1] if same else own, same_core))
        if turn < 3:
            cross.append(permute(cross[-1], same_core) if cross else permute(own, cross_core))
        if turn == 0:
            x1 = permute(own, swap_x)
            ya = permute(own, along_y(1))
            yb = permute(own, along_y(3))

    half = BLOCK // 2
    xx = permute(jnp.concatenate([ya, yb], axis=0), swap_x)
    y2a = permute(ya[:half], along_y(1))
    y2b = permute(yb[half:], along_y(3))
    near = permute(jnp.concatenate([own, x1, ya, yb], axis=0), swap_core)
    w2a = permute(xx[:half], along_y(1))
    w2b = permute(xx[BLOCK + half :], along_y(3))
    far = permute(jnp.concatenate([xx, y2a, y2b, w2a, w2b], axis=0), swap_core)

    first_code = jnp.full((TAG, feats), codes[0] + 1, jnp.int32).astype(jnp.bfloat16)
    piece = permute(
        jnp.concatenate([own[:PIECE], first_code], axis=0),
        lambda y, x, z, c: (y, 1, z, c),
        keep=lambda y, x, z, c: x == 2 and z == 0 and c == 0,
    )
    for jump in (4, 2, 1):
        piece = piece + permute(
            piece,
            along_z(jump),
            keep=lambda y, x, z, c, jump=jump: x == 1 and c == 0 and z % (2 * jump) == 0,
        )
    heads = [own[:PIECE], yb[:PIECE], y2a[:PIECE], ya[:PIECE]]
    odd = lax.dynamic_slice_in_dim(
        jnp.concatenate(heads + heads, axis=0), (NY - y) % NY * PIECE, BLOCK, 0
    )
    at_start = lambda y, x, z, c: z == 0 and c == 0
    odd = permute(
        odd, lambda y, x, z, c: (y, 1, z, c), keep=lambda *a: a[1] == 2 and at_start(*a)
    )
    odd = odd + permute(odd, swap_x, keep=lambda *a: a[1] == 1 and at_start(*a))
    odd = odd + permute(odd, swap_core, keep=lambda *a: a[1] < 2 and at_start(*a))

    lines = jnp.concatenate([line, line], axis=0)
    run = lax.dynamic_slice_in_dim(lines, jnp.where(c == 0, z + 4, z + 1), 4, 0)
    run = jnp.where(c == 0, run[::-1], run)
    same_codes = jnp.where(c == 0, run[:, 0], run[:, 1])
    cross_codes = jnp.where(c == 0, run[:, 1], run[:, 0])
    piece_code = piece[PIECE, :1].astype(jnp.int32) - 1
    early_codes = jnp.concatenate(
        [codes, same_codes[0], cross_codes[0], same_codes[1], cross_codes[1]]
    )
    late_codes = jnp.concatenate([same_codes[2], cross_codes[2], piece_code])
    last_codes = same_codes[3]
    all_codes = jnp.concatenate([early_codes, late_codes, last_codes])

    chip_bins = jnp.where(chip >= BINS, chip - BINS, chip)
    chip_x_bins = jnp.where(chip_x >= BINS, chip_x - BINS, chip_x)
    pick = lambda both, core: jnp.repeat(jnp.where(core == 0, both[0], both[1]), PIECE)
    mine, mine_x = pick(chip_bins, c), pick(chip_x_bins, c)
    theirs, theirs_x = pick(chip_bins, 1 - c), pick(chip_x_bins, 1 - c)
    odd_bin = jnp.where((x < 2) & (z == 0), bins[:1], -2)
    row_bins = jnp.concatenate(
        [mine, mine_x, mine, mine]
        + [theirs, theirs_x, theirs, theirs]
        + [mine_x, mine_x, mine, mine_x]
        + [theirs_x, theirs_x, theirs, theirs_x]
        + [jnp.repeat(odd_bin, BLOCK)]
    ).astype(jnp.float32)
    code_source = (all_codes >= BINS).astype(jnp.float32)
    code_bin = all_codes.astype(jnp.float32) - BINS * code_source
    no_odd = jnp.where(jnp.arange(all_codes.shape[0]) == early_codes.shape[0] + 8, 0.0, 1.0)
    match = (code_bin[:, None] == row_bins[None, :]).astype(jnp.float32)
    match = jnp.where(jnp.arange(row_bins.shape[0])[None, :] >= 16 * BLOCK, match * no_odd[:, None], match)
    counts = jnp.stack(
        [jnp.sum(match * code_source[:, None], 0), jnp.sum(match * (1 - code_source[:, None]), 0)]
    )

    row_bins = row_bins[None, :]
    near_rows = [(own, BLOCK), (x1, BLOCK), (ya, BLOCK), (yb, BLOCK), (near, 4 * BLOCK)]
    far_rows = [(xx, 2 * BLOCK), (y2a, half), (y2b, half), (w2a, half), (w2b, half)]
    far_rows = far_rows + [(far, 4 * BLOCK)]
    odd_rows = [(odd, BLOCK)]
    size = lambda rows: sum(n for _, n in rows)
    blank = lambda rows: jnp.zeros((2, size(rows)), jnp.float32)
    early = [(own, BLOCK), (same[0], BLOCK), (cross[0], BLOCK), (same[1], BLOCK), (cross[1], BLOCK)]
    late = [(same[2], BLOCK), (cross[2], BLOCK), (piece, PIECE)]
    last = [(same[3], BLOCK)]
    first = size(near_rows)
    sums_near = pair_sums(
        near_rows, early, early_codes, row_bins[:, :first], blank(near_rows), True, "near"
    )
    far_odd = far_rows + odd_rows
    sums_far = pair_sums(
        far_odd, early, early_codes, row_bins[:, first:], blank(far_odd), False, "far"
    )
    sums = jnp.concatenate([sums_near, sums_far], axis=1)
    every = near_rows + far_odd
    apart = 2 * BLOCK // PIECE
    sums = pair_sums(every, late, late_codes, row_bins, sums, False, "late", apart)
    sums = pair_sums(every, last, last_codes, row_bins, sums, False, "last")

    stats = jnp.concatenate([sums, counts], axis=0).reshape(4, 17, BLOCK)
    core_mine = jnp.concatenate([stats[:, 0:4], stats[:, 8:12]], axis=1)
    core_theirs = jnp.concatenate([stats[:, 4:8], stats[:, 12:16]], axis=1)
    core_mine = core_mine + permute(core_theirs, swap_core)
    to_x = jnp.stack([core_mine[:, i] for i in (1, 4, 5, 7)], axis=1)
    keep = jnp.stack([core_mine[:, i] for i in (0, 2, 3, 6)], axis=1)
    keep = keep + permute(to_x, swap_x)
    odd_stats = stats[:, 16]
    odd_total = jnp.zeros_like(odd_stats)
    for core in (0, 1):
        for start in (0, 1):
            odd_total = odd_total + permute(
                odd_stats,
                lambda y, x, z, c: (y, 2, z, 0),
                keep=lambda y, x, z, c, k=(core, start): (c, x) == k and z == 0,
            )
    turned = jnp.stack([keep[:, 0], keep[:, 2], keep[:, 3], keep[:, 1]], axis=1)
    turned = jnp.concatenate([turned, turned], axis=1)
    ordered = lax.dynamic_slice_in_dim(turned, (NY - y) % NY, NY, 1)
    ordered = ordered.reshape(4, NY, blocks, PIECE)
    ordered = ordered.at[:, :, 0].add(odd_total.reshape(4, NY, PIECE))
    total = ordered
    for turn in (2, 1, 3):
        total = total + permute(ordered, along_y(turn))
    weight = 1.0 / (BLOCK * 32.0**3)
    proof = (total[0] / total[2] - total[1] / total[3]) * weight * (BLOCK // PIECE)
    return jnp.transpose(proof, (1, 0, 2)).reshape(-1)


def solution(mesh):
    placed = (P("shower", "layer"), P("layer", None), P("layer", None), P("shower"), P("shower"))
    return jax.shard_map(shards, mesh=mesh, in_specs=placed, out_specs=P("shower"), check_vma=False)
```

```python
import functools

import jax
import jax.numpy as jnp
from jax import lax
from jax.experimental import pallas as pl
from jax.experimental.pallas import tpu as pltpu
from jax.sharding import PartitionSpec as P

BLOCK = 128
PIECE = 32
TAG = 16
BINS = 8
CHUNK = 512
AXES = ("layer", "shower")
NY, NX, NZ, NC = 4, 4, 8, 2


def flat(y, x, z, c):
    return y * (NX * NZ * NC) + (x * NZ + z) * NC + c


def permute(value, move, keep=lambda y, x, z, c: True):
    pairs = [
        (flat(y, x, z, c), flat(*move(y, x, z, c)))
        for y in range(NY)
        for x in range(NX)
        for z in range(NZ)
        for c in range(NC)
        if keep(y, x, z, c)
    ]
    return lax.ppermute(value, AXES, pairs)


def along_y(step):
    return lambda y, x, z, c: ((y + step) % NY, x, z, c)


def along_z(step):
    return lambda y, x, z, c: (y, x, (z + step) % NZ, c)


def flip_z(bit):
    return lambda y, x, z, c: (y, x, z ^ bit, c)


def swap_x(y, x, z, c):
    return (y, x ^ 1, z, c)


def swap_core(y, x, z, c):
    return (y, x, z, 1 - c)


def same_core(y, x, z, c):
    return (y, x, (z + 1 - 2 * c) % NZ, c)


def cross_core(y, x, z, c):
    return (y, x, (z - 1 + 2 * c) % NZ, 1 - c)


def raw_kernel(pattern, showers, geometry, out, masked):
    step = pl.program_id(0)
    layers = pattern.shape[1]
    cells = geometry.shape[0] // layers
    per = geometry.shape[1] // BLOCK
    for layer in range(layers):
        for part in range(per):
            rows = pl.ds(layer * cells, cells)
            cols = pl.ds(part * BLOCK, BLOCK)
            on = pattern[step * per + part, layer].astype(jnp.float32).astype(jnp.bfloat16)
            masked[rows, cols] = geometry[rows, cols] * on
    out[...] = lax.dot_general(
        showers[...], masked[...], (((0,), (0,)), ((), ())), preferred_element_type=jnp.float32
    )


def raw_partial(showers, geometry, pattern):
    rows, depth = showers.shape
    feats = geometry.shape[1]
    width = 512
    return pl.pallas_call(
        raw_kernel,
        grid=(feats // width,),
        in_specs=[
            pl.BlockSpec(memory_space=pltpu.SMEM),
            pl.BlockSpec((depth, rows), lambda i: (0, 0)),
            pl.BlockSpec((depth, width), lambda i: (0, i)),
        ],
        out_specs=pl.BlockSpec((rows, width), lambda i: (0, i)),
        out_shape=jax.ShapeDtypeStruct((rows, feats), jnp.float32),
        scratch_shapes=[pltpu.VMEM((depth, width), jnp.bfloat16)],
        compiler_params=pltpu.CompilerParams(vmem_limit_bytes=60 * 2**20),
        cost_estimate=pl.CostEstimate(
            flops=2 * rows * depth * feats, bytes_accessed=8 * 2**20, transcendentals=0
        ),
        name="raw",
    )(pattern.T, showers.T, geometry)


def pair_kernel(*refs, row_cuts, tag_cuts, col_sizes, n_args, apart):
    n_cols = len(col_sizes)
    odd_here = refs[0]
    args = refs[1 : 1 + n_args]
    cols = refs[1 + n_args : 1 + n_args + n_cols]
    out, rows_at, cols_at, row_tags, col_tags, row_sems, col_sems, tag_sems = refs[1 + n_args + n_cols :]

    def start(source, first, size, target, place, sem):
        copy = pltpu.make_async_copy(
            source.at[pl.ds(first, size), :], target.at[pl.ds(place, size), :], sem
        )
        copy.start()
        return copy

    waits, depth = [], 0
    for at, (source, size) in enumerate(zip(cols, col_sizes)):
        waits.append(start(source, TAG, size, cols_at, depth, col_sems.at[at]))
        waits.append(start(source, 0, TAG, col_tags, at * TAG, tag_sems.at[at]))
        depth += size
    for at, (arg, first) in enumerate(tag_cuts):
        waits.append(start(args[arg], first, TAG, row_tags, at * TAG, tag_sems.at[n_cols + at]))
    row_copies, total = [], 0
    for at, (arg, first, size) in enumerate(row_cuts):
        row_copies.append((total, start(args[arg], first, size, rows_at, total, row_sems.at[at])))
        total += size
    for copy in waits:
        copy.wait()

    def bin_of(code):
        source = (code >= BINS).astype(jnp.float32)
        return code - BINS * source, source

    waited = 0
    for first in range(0, total, CHUNK):
        size = min(CHUNK, total - first)
        while waited < len(row_copies) and row_copies[waited][0] < first + size:
            row_copies[waited][1].wait()
            waited += 1
        odd = first >= 4 * CHUNK
        set_of = 0 if odd else first // CHUNK
        tag = row_tags[pl.ds(set_of * TAG + 4, 1), pl.ds(0, BLOCK)].astype(jnp.float32) - 1.0
        bins, _ = bin_of(tag)
        if odd:
            bins = jnp.where(odd_here[0] > 0, bins, -2.0)
        bins = jnp.concatenate([bins] * (size // BLOCK), axis=1)
        one = jnp.zeros((8, size), jnp.float32)
        zero = jnp.zeros((8, size), jnp.float32)
        n_one = jnp.zeros((1, size), jnp.float32)
        n_zero = jnp.zeros((1, size), jnp.float32)
        for low in range(0, depth, 2 * BLOCK):
            high = depth if depth - low < 4 * BLOCK and depth % (2 * BLOCK) else low + 2 * BLOCK
            if low and high == depth and low > high - 2 * BLOCK and depth % (2 * BLOCK):
                break
            products = lax.dot_general(
                cols_at[pl.ds(low, high - low), :],
                rows_at[pl.ds(first, size), :],
                (((1,), (1,)), ((), ())),
                preferred_element_type=jnp.float32,
            )
            shifted = products + 32.0
            cubes = shifted * shifted * shifted
            for group in range(low // PIECE, high // PIECE):
                if odd and group == apart:
                    continue
                block = cubes[group * PIECE - low : (group + 1) * PIECE - low]
                if first == 0 and group < BLOCK // PIECE:
                    lane = lax.broadcasted_iota(jnp.int32, block.shape, 1)
                    sub = lax.broadcasted_iota(jnp.int32, block.shape, 0)
                    block = jnp.where(lane == sub + group * PIECE, 0.0, block)
                part = (block[0:8] + block[8:16]) + (block[16:24] + block[24:32])
                row = group // 4 * TAG + group % 4
                code = col_tags[pl.ds(row, 1), pl.ds(0, size)].astype(jnp.float32) - 1.0
                bin_id, source = bin_of(code)
                match = (bins == bin_id).astype(jnp.float32)
                is_one = match * source
                is_zero = match - is_one
                one += is_one * part
                zero += is_zero * part
                n_one += is_one
                n_zero += is_zero
        lanes = pl.ds(first, size)
        out[0:1, lanes] = jnp.sum(one, axis=0, keepdims=True)
        out[1:2, lanes] = jnp.sum(zero, axis=0, keepdims=True)
        out[2:3, lanes] = n_one
        out[3:4, lanes] = n_zero


def pair_sums(odd_here, args, row_cuts, tag_cuts, cols, apart):
    col_sizes = tuple(size for _, size in cols)
    total, depth = sum(size for _, _, size in row_cuts), sum(col_sizes)
    feats = args[0].shape[1]
    hbm = pl.BlockSpec(memory_space=pl.ANY)
    return pl.pallas_call(
        functools.partial(
            pair_kernel,
            row_cuts=tuple(row_cuts),
            tag_cuts=tuple(tag_cuts),
            col_sizes=col_sizes,
            n_args=len(args),
            apart=apart,
        ),
        in_specs=[pl.BlockSpec(memory_space=pltpu.SMEM)] + [hbm] * (len(args) + len(cols)),
        out_specs=pl.BlockSpec(memory_space=pltpu.VMEM),
        out_shape=jax.ShapeDtypeStruct((4, total), jnp.float32),
        scratch_shapes=[
            pltpu.VMEM((total, feats), jnp.bfloat16),
            pltpu.VMEM((depth, feats), jnp.bfloat16),
            pltpu.VMEM((TAG * len(tag_cuts), feats), jnp.bfloat16),
            pltpu.VMEM((TAG * len(cols), feats), jnp.bfloat16),
            pltpu.SemaphoreType.DMA((len(row_cuts),)),
            pltpu.SemaphoreType.DMA((len(cols),)),
            pltpu.SemaphoreType.DMA((len(cols) + len(tag_cuts),)),
        ],
        compiler_params=pltpu.CompilerParams(vmem_limit_bytes=58 * 2**20),
        cost_estimate=pl.CostEstimate(
            flops=2 * total * depth * feats,
            bytes_accessed=2 * (total + depth) * feats,
            transcendentals=0,
        ),
        name="pairs",
    )(odd_here, *args, *[c for c, _ in cols])


def shards(showers, geometry, pattern, bins, sources):
    y = lax.axis_index("layer")
    s = lax.axis_index("shower")
    x, z, c = s // (NZ * NC), (s // NC) % NZ, s % NC
    feats = geometry.shape[1]
    blocks = bins.shape[0]

    codes = (bins + BINS * sources + 1).astype(jnp.float32)
    line = lax.broadcasted_iota(jnp.int32, (TAG, feats), 0)
    lane = lax.broadcasted_iota(jnp.int32, (TAG, feats), 1) // PIECE
    which = jnp.where(line == blocks, lane, line)
    tag = jnp.zeros((TAG, feats), jnp.float32)
    for group in range(blocks):
        tag = jnp.where(which == group, codes[group], tag)
    tag = tag.astype(jnp.bfloat16)

    partial_sums = raw_partial(showers, geometry, pattern).reshape(blocks, NY, PIECE, feats)

    def share(turn):
        part = lax.dynamic_index_in_dim(partial_sums, (y + turn) % NY, 1, keepdims=False)
        return part.reshape(BLOCK, feats)

    raw = share(0)
    arrived = [permute(share(turn).astype(jnp.float16), along_y(turn)) for turn in (2, 1, 3)]
    for part in arrived:
        raw = raw + part.astype(jnp.float32)
    scale = lax.rsqrt(jnp.mean(raw * raw, axis=1, keepdims=True) + 1e-05)
    own = jnp.concatenate([tag, (raw * scale).astype(jnp.bfloat16)], axis=0)

    rows_of = lambda value: value[TAG:]
    same = [permute(own, same_core)]
    cross = [permute(own, cross_core)]
    x1 = permute(own, swap_x)
    ya = permute(rows_of(own), along_y(1))
    yb = permute(rows_of(own), along_y(3))
    same.append(permute(same[0], same_core))
    cross.append(permute(cross[0], same_core))
    y_way = lambda y, x, z, c: ((y + 1 - 2 * c) % NY, x, z, c)
    y2 = permute(jnp.where(c == 0, ya, yb), y_way)
    xx = permute(jnp.concatenate([ya, yb], axis=0), swap_x)
    near = permute(jnp.concatenate([own, x1, ya, yb], axis=0), swap_core)
    same.append(permute(same[1], same_core))
    cross.append(permute(cross[1], same_core))
    w2 = permute(jnp.where(c == 0, xx[:BLOCK], xx[BLOCK:]), y_way)
    far = permute(jnp.concatenate([xx, y2, w2], axis=0), swap_core)
    same.append(permute(same[2], same_core))

    head = TAG + PIECE
    held = [own, same[0], same[1], same[2], same[2], cross[2], cross[1], cross[0]]
    piece = lax.select_n(z, *[value[:head] for value in held])
    to_one = lambda y, x, z, c: (y, 1, z, c)
    side = lambda z: 0 if z < 4 else 1
    piece_near = permute(
        piece, to_one, keep=lambda y, x, z, c: x == 2 and z != 4 and c == side(z)
    )
    piece_far = permute(
        piece,
        lambda y, x, z, c: (y, 1, z + 1, c),
        keep=lambda y, x, z, c: x == 2 and z == 3 and c == 0,
    )
    piece = piece_near + piece_far
    odd = jnp.concatenate(
        [own[TAG:head], yb[:PIECE], y2[:PIECE], ya[:PIECE]], axis=0
    )
    at_start = lambda y, x, z, c: z == 0 and c == 0
    odd = permute(odd, to_one, keep=lambda *a: a[1] == 2 and at_start(*a))
    odd = odd + permute(odd, swap_x, keep=lambda *a: a[1] == 1 and at_start(*a))
    odd = odd + permute(odd, swap_core, keep=lambda *a: a[1] < 2 and at_start(*a))

    args = [own, x1, ya, yb, y2, xx, w2, near, far, odd]
    tagged = BLOCK + TAG
    tag_cuts = [(0, 0), (1, 0), (7, 0), (7, tagged)]
    row_cuts = [(0, TAG, BLOCK), (3, 0, BLOCK), (4, 0, BLOCK), (2, 0, BLOCK)]
    row_cuts += [(1, TAG, BLOCK), (5, BLOCK, BLOCK), (6, 0, BLOCK), (5, 0, BLOCK)]
    row_cuts += [(7, TAG, BLOCK), (7, 2 * tagged + BLOCK, BLOCK)]
    row_cuts += [(8, 2 * BLOCK, BLOCK), (7, 2 * tagged, BLOCK)]
    row_cuts += [(7, tagged + TAG, BLOCK), (8, BLOCK, BLOCK)]
    row_cuts += [(8, 3 * BLOCK, BLOCK), (8, 0, BLOCK), (9, 0, BLOCK)]
    cols = [own, same[0], cross[0], same[1], cross[1], same[2], cross[2], same[3]]
    cols = [(value, BLOCK) for value in cols] + [(piece, PIECE)]
    odd_here = ((x < 2) & (z == 0)).astype(jnp.int32).reshape(1)
    stats = pair_sums(odd_here, args, row_cuts, tag_cuts, cols, 8 * BLOCK // PIECE)

    theirs = permute(stats[:, 2 * CHUNK :], swap_core)
    mine = stats[:, : 2 * CHUNK] + theirs[:, : 2 * CHUNK]
    odd_stats = stats[:, 4 * CHUNK :] + theirs[:, 2 * CHUNK :]
    kept = mine[:, :CHUNK] + permute(mine[:, CHUNK:], swap_x)
    odd_total = jnp.zeros_like(odd_stats)
    for start in (0, 1):
        odd_total = odd_total + permute(
            odd_stats,
            lambda y, x, z, c: (y, 2, z, c),
            keep=lambda *a, start=start: a[1] == start and at_start(*a),
        )
    odd_total = odd_total.reshape(4, NY, PIECE)
    kept = kept.reshape(4, NY, BLOCK) + jnp.pad(odd_total, ((0, 0), (0, 0), (0, BLOCK - PIECE)))
    total = kept
    for turn in (2, 1, 3):
        total = total + jnp.roll(permute(kept, along_y(turn)), -turn, axis=1)
    weight = 1.0 / (PIECE * 32.0**3)
    proof = (total[0] / total[2] - total[1] / total[3]) * weight
    proof = jnp.concatenate([proof, proof], axis=0)
    proof = lax.dynamic_slice_in_dim(proof, (NY - y) % NY, NY, 0).reshape(NY, blocks, PIECE)
    return jnp.transpose(proof, (1, 0, 2)).reshape(-1)


def solution(mesh):
    placed = (P("shower", "layer"), P("layer", None), P("layer", None), P("shower"), P("shower"))
    return jax.shard_map(shards, mesh=mesh, in_specs=placed, out_specs=P("shower"), check_vma=False)
```

```python
import functools

import jax
import jax.numpy as jnp
from jax import lax
from jax.experimental import pallas as pl
from jax.experimental.pallas import tpu as pltpu
from jax.sharding import PartitionSpec as P

BLOCK = 128
PIECE = 32
TAG = 16
BINS = 8
CHUNK = 512
AXES = ("layer", "shower")
NY, NX, NZ, NC = 4, 4, 8, 2


def flat(y, x, z, c):
    return y * (NX * NZ * NC) + (x * NZ + z) * NC + c


def permute(value, move, keep=lambda y, x, z, c: True):
    pairs = [
        (flat(y, x, z, c), flat(*move(y, x, z, c)))
        for y in range(NY)
        for x in range(NX)
        for z in range(NZ)
        for c in range(NC)
        if keep(y, x, z, c)
    ]
    return lax.ppermute(value, AXES, pairs)


def along_y(step):
    return lambda y, x, z, c: ((y + step) % NY, x, z, c)


def along_z(step):
    return lambda y, x, z, c: (y, x, (z + step) % NZ, c)


def flip_z(bit):
    return lambda y, x, z, c: (y, x, z ^ bit, c)


def swap_x(y, x, z, c):
    return (y, x ^ 1, z, c)


def swap_core(y, x, z, c):
    return (y, x, z, 1 - c)


def same_core(y, x, z, c):
    return (y, x, (z + 1 - 2 * c) % NZ, c)


def cross_core(y, x, z, c):
    return (y, x, (z - 1 + 2 * c) % NZ, 1 - c)


def raw_kernel(pattern, showers, geometry, out, masked):
    step = pl.program_id(0)
    layers = pattern.shape[1]
    cells = geometry.shape[0] // layers
    per = geometry.shape[1] // BLOCK
    for layer in range(layers):
        for part in range(per):
            rows = pl.ds(layer * cells, cells)
            cols = pl.ds(part * BLOCK, BLOCK)
            on = pattern[step * per + part, layer].astype(jnp.float32).astype(jnp.bfloat16)
            masked[rows, cols] = geometry[rows, cols] * on
    out[...] = lax.dot_general(
        showers[...], masked[...], (((0,), (0,)), ((), ())), preferred_element_type=jnp.float32
    )


def raw_partial(showers, geometry, pattern):
    rows, depth = showers.shape
    feats = geometry.shape[1]
    width = 512
    return pl.pallas_call(
        raw_kernel,
        grid=(feats // width,),
        in_specs=[
            pl.BlockSpec(memory_space=pltpu.SMEM),
            pl.BlockSpec((depth, rows), lambda i: (0, 0)),
            pl.BlockSpec((depth, width), lambda i: (0, i)),
        ],
        out_specs=pl.BlockSpec((rows, width), lambda i: (0, i)),
        out_shape=jax.ShapeDtypeStruct((rows, feats), jnp.float32),
        scratch_shapes=[pltpu.VMEM((depth, width), jnp.bfloat16)],
        compiler_params=pltpu.CompilerParams(vmem_limit_bytes=60 * 2**20),
        cost_estimate=pl.CostEstimate(
            flops=2 * rows * depth * feats, bytes_accessed=8 * 2**20, transcendentals=0
        ),
        name="raw",
    )(pattern.T, showers.T, geometry)


def pair_kernel(*refs, row_cuts, tag_cuts, col_sizes, n_args, apart, diag):
    n_cols = len(col_sizes)
    odd_here, before = refs[:2]
    args = refs[2 : 2 + n_args]
    cols = refs[2 + n_args : 2 + n_args + n_cols]
    out, rows_at, cols_at, row_tags, col_tags, row_sems, col_sems, tag_sems = refs[2 + n_args + n_cols :]

    def start(source, first, size, target, place, sem):
        copy = pltpu.make_async_copy(
            source.at[pl.ds(first, size), :], target.at[pl.ds(place, size), :], sem
        )
        copy.start()
        return copy

    waits, depth = [], 0
    for at, (source, size) in enumerate(zip(cols, col_sizes)):
        waits.append(start(source, TAG, size, cols_at, depth, col_sems.at[at]))
        waits.append(start(source, 0, TAG, col_tags, at * TAG, tag_sems.at[at]))
        depth += size
    for at, (arg, first) in enumerate(tag_cuts):
        waits.append(start(args[arg], first, TAG, row_tags, at * TAG, tag_sems.at[n_cols + at]))
    row_copies, total = [], 0
    for at, (arg, first, size) in enumerate(row_cuts):
        row_copies.append((total, start(args[arg], first, size, rows_at, total, row_sems.at[at])))
        total += size
    for copy in waits:
        copy.wait()

    def bin_of(code):
        source = (code >= BINS).astype(jnp.float32)
        return code - BINS * source, source

    waited = 0
    for first in range(0, total, CHUNK):
        size = min(CHUNK, total - first)
        while waited < len(row_copies) and row_copies[waited][0] < first + size:
            row_copies[waited][1].wait()
            waited += 1
        odd = first >= 2 * CHUNK
        set_of = 0 if odd else first // CHUNK
        tag = row_tags[pl.ds(set_of * TAG + 4, 1), pl.ds(0, BLOCK)].astype(jnp.float32) - 1.0
        bins, _ = bin_of(tag)
        if odd:
            bins = jnp.where(odd_here[0] > 0, bins, -2.0)
        bins = jnp.concatenate([bins] * (size // BLOCK), axis=1)
        one = jnp.zeros((8, size), jnp.float32)
        zero = jnp.zeros((8, size), jnp.float32)
        n_one = jnp.zeros((1, size), jnp.float32)
        n_zero = jnp.zeros((1, size), jnp.float32)
        for low in range(0, depth, 2 * BLOCK):
            high = depth if depth - low < 4 * BLOCK and depth % (2 * BLOCK) else low + 2 * BLOCK
            if low and high == depth and low > high - 2 * BLOCK and depth % (2 * BLOCK):
                break
            products = lax.dot_general(
                cols_at[pl.ds(low, high - low), :],
                rows_at[pl.ds(first, size), :],
                (((1,), (1,)), ((), ())),
                preferred_element_type=jnp.float32,
            )
            shifted = products + 32.0
            cubes = shifted * shifted * shifted
            for group in range(low // PIECE, high // PIECE):
                if odd and group == apart:
                    continue
                block = cubes[group * PIECE - low : (group + 1) * PIECE - low]
                if diag and first == 0 and group < BLOCK // PIECE:
                    lane = lax.broadcasted_iota(jnp.int32, block.shape, 1)
                    sub = lax.broadcasted_iota(jnp.int32, block.shape, 0)
                    block = jnp.where(lane == sub + group * PIECE, 0.0, block)
                part = (block[0:8] + block[8:16]) + (block[16:24] + block[24:32])
                row = group // 4 * TAG + group % 4
                code = col_tags[pl.ds(row, 1), pl.ds(0, size)].astype(jnp.float32) - 1.0
                bin_id, source = bin_of(code)
                match = (bins == bin_id).astype(jnp.float32)
                is_one = match * source
                is_zero = match - is_one
                one += is_one * part
                zero += is_zero * part
                n_one += is_one
                n_zero += is_zero
        lanes = pl.ds(first, size)
        out[0:1, lanes] = before[0:1, lanes] + jnp.sum(one, axis=0, keepdims=True)
        out[1:2, lanes] = before[1:2, lanes] + jnp.sum(zero, axis=0, keepdims=True)
        out[2:3, lanes] = before[2:3, lanes] + n_one
        out[3:4, lanes] = before[3:4, lanes] + n_zero


def pair_sums(odd_here, before, args, row_cuts, tag_cuts, cols, apart, diag, name):
    col_sizes = tuple(size for _, size in cols)
    total, depth = sum(size for _, _, size in row_cuts), sum(col_sizes)
    feats = args[0].shape[1]
    hbm = pl.BlockSpec(memory_space=pl.ANY)
    return pl.pallas_call(
        functools.partial(
            pair_kernel,
            row_cuts=tuple(row_cuts),
            tag_cuts=tuple(tag_cuts),
            col_sizes=col_sizes,
            n_args=len(args),
            apart=apart,
            diag=diag,
        ),
        in_specs=[pl.BlockSpec(memory_space=pltpu.SMEM), pl.BlockSpec(memory_space=pltpu.VMEM)]
        + [hbm] * (len(args) + len(cols)),
        out_specs=pl.BlockSpec(memory_space=pltpu.VMEM),
        out_shape=jax.ShapeDtypeStruct((4, total), jnp.float32),
        scratch_shapes=[
            pltpu.VMEM((total, feats), jnp.bfloat16),
            pltpu.VMEM((depth, feats), jnp.bfloat16),
            pltpu.VMEM((TAG * len(tag_cuts), feats), jnp.bfloat16),
            pltpu.VMEM((TAG * len(cols), feats), jnp.bfloat16),
            pltpu.SemaphoreType.DMA((len(row_cuts),)),
            pltpu.SemaphoreType.DMA((len(cols),)),
            pltpu.SemaphoreType.DMA((len(cols) + len(tag_cuts),)),
        ],
        compiler_params=pltpu.CompilerParams(vmem_limit_bytes=58 * 2**20),
        cost_estimate=pl.CostEstimate(
            flops=2 * total * depth * feats,
            bytes_accessed=2 * (total + depth) * feats,
            transcendentals=0,
        ),
        name=name,
    )(odd_here, before, *args, *[c for c, _ in cols])


def shards(showers, geometry, pattern, bins, sources):
    y = lax.axis_index("layer")
    s = lax.axis_index("shower")
    x, z, c = s // (NZ * NC), (s // NC) % NZ, s % NC
    feats = geometry.shape[1]
    blocks = bins.shape[0]

    codes = (bins + BINS * sources + 1).astype(jnp.float32)
    line = lax.broadcasted_iota(jnp.int32, (TAG, feats), 0)
    lane = lax.broadcasted_iota(jnp.int32, (TAG, feats), 1) // PIECE
    which = jnp.where(line == blocks, lane, line)
    tag = jnp.zeros((TAG, feats), jnp.float32)
    for group in range(blocks):
        tag = jnp.where(which == group, codes[group], tag)
    tag = tag.astype(jnp.bfloat16)

    partial_sums = raw_partial(showers, geometry, pattern).reshape(blocks, NY, PIECE, feats)

    def share(turn):
        part = lax.dynamic_index_in_dim(partial_sums, (y + turn) % NY, 1, keepdims=False)
        return part.reshape(BLOCK, feats)

    raw = share(0)
    arrived = [permute(share(turn).astype(jnp.float16), along_y(turn)) for turn in (2, 1, 3)]
    for part in arrived:
        raw = raw + part.astype(jnp.float32)
    scale = lax.rsqrt(jnp.mean(raw * raw, axis=1, keepdims=True) + 1e-05)
    own = jnp.concatenate([tag, (raw * scale).astype(jnp.bfloat16)], axis=0)

    rows_of = lambda value: value[TAG:]
    same, cross = [], []
    for turn in range(4):
        same.append(permute(same[-1] if same else own, same_core))
        if turn < 3:
            cross.append(permute(cross[-1], same_core) if cross else permute(own, cross_core))
    own_other = permute(own, swap_core)
    same_other = [permute(value, swap_core) for value in same]
    cross_other = [permute(value, swap_core) for value in cross]

    y_way = lambda y, x, z, c: ((y + 1 - 2 * c) % NY, x, z, c)
    x1 = permute(own, swap_x)
    ya = permute(rows_of(own), along_y(1))
    yb = permute(rows_of(own), along_y(3))
    y2 = permute(jnp.where(c == 0, ya, yb), y_way)
    xa = permute(ya, swap_x)
    xb = permute(yb, swap_x)
    w2 = permute(jnp.where(c == 0, xa, xb), y_way)

    head = TAG + PIECE
    held = [own, same[0], same[1], same[2], same[2], cross[2], cross[1], cross[0]]
    piece = lax.select_n(z, *[value[:head] for value in held])
    to_one = lambda y, x, z, c: (y, 1, z, c)
    side = lambda z: 0 if z < 4 else 1
    piece_near = permute(
        piece, to_one, keep=lambda y, x, z, c: x == 2 and z != 4 and c == side(z)
    )
    piece_far = permute(
        piece,
        lambda y, x, z, c: (y, 1, z + 1, c),
        keep=lambda y, x, z, c: x == 2 and z == 3 and c == 0,
    )
    piece = piece_near + piece_far
    piece = piece + permute(piece, swap_core)
    odd = jnp.concatenate([own[TAG:head], yb[:PIECE], y2[:PIECE], ya[:PIECE]], axis=0)
    at_start = lambda y, x, z, c: z == 0 and c == 0
    odd = permute(odd, to_one, keep=lambda *a: a[1] == 2 and at_start(*a))
    odd = odd + permute(odd, swap_x, keep=lambda *a: a[1] == 1 and at_start(*a))

    args = [own, x1, ya, yb, y2, xa, xb, w2, odd]
    tag_cuts = [(0, 0), (1, 0)]
    row_cuts = [(0, TAG), (3, 0), (4, 0), (2, 0), (1, TAG), (6, 0), (7, 0), (5, 0), (8, 0)]
    row_cuts = [(arg, first, BLOCK) for arg, first in row_cuts]
    whole = lambda values: [(value, BLOCK) for value in values]
    early = whole([own, own_other])
    for turn in range(2):
        early += whole([same[turn], cross[turn], same_other[turn], cross_other[turn]])
    late = whole([same[2], cross[2], same_other[2], cross_other[2], same[3], same_other[3]])
    late = late + [(piece, PIECE)]
    odd_here = ((x < 2) & (z == 0) & (c == 0)).astype(jnp.int32).reshape(1)
    blank = jnp.zeros((4, 2 * CHUNK + BLOCK), jnp.float32)
    stats = pair_sums(odd_here, blank, args, row_cuts, tag_cuts, early, -1, True, "early")
    apart = 6 * BLOCK // PIECE
    stats = pair_sums(odd_here, stats, args, row_cuts, tag_cuts, late, apart, False, "late")

    kept = stats[:, :CHUNK] + permute(stats[:, CHUNK : 2 * CHUNK], swap_x)
    odd_stats = stats[:, 2 * CHUNK :]
    odd_total = jnp.zeros_like(odd_stats)
    for start in (0, 1):
        odd_total = odd_total + permute(
            odd_stats,
            lambda y, x, z, c: (y, 2, z, c),
            keep=lambda *a, start=start: a[1] == start and at_start(*a),
        )
    odd_total = odd_total.reshape(4, NY, PIECE)
    kept = kept.reshape(4, NY, BLOCK) + jnp.pad(odd_total, ((0, 0), (0, 0), (0, BLOCK - PIECE)))
    total = kept
    for turn in (2, 1, 3):
        total = total + jnp.roll(permute(kept, along_y(turn)), -turn, axis=1)
    weight = 1.0 / (PIECE * 32.0**3)
    proof = (total[0] / total[2] - total[1] / total[3]) * weight
    proof = jnp.concatenate([proof, proof], axis=0)
    proof = lax.dynamic_slice_in_dim(proof, (NY - y) % NY, NY, 0).reshape(NY, blocks, PIECE)
    return jnp.transpose(proof, (1, 0, 2)).reshape(-1)


def solution(mesh):
    placed = (P("shower", "layer"), P("layer", None), P("layer", None), P("shower"), P("shower"))
    return jax.shard_map(shards, mesh=mesh, in_specs=placed, out_specs=P("shower"), check_vma=False)
```

```python
import functools

import jax
import jax.numpy as jnp
from jax import lax
from jax.experimental import pallas as pl
from jax.experimental.pallas import tpu as pltpu
from jax.sharding import PartitionSpec as P

BLOCK = 128
PIECE = 32
TAG = 16
BINS = 8
CHUNK = 512
AXES = ("layer", "shower")
NY, NX, NZ, NC = 4, 4, 8, 2


def flat(y, x, z, c):
    return y * (NX * NZ * NC) + (x * NZ + z) * NC + c


def permute(value, move, keep=lambda y, x, z, c: True):
    pairs = [
        (flat(y, x, z, c), flat(*move(y, x, z, c)))
        for y in range(NY)
        for x in range(NX)
        for z in range(NZ)
        for c in range(NC)
        if keep(y, x, z, c)
    ]
    return lax.ppermute(value, AXES, pairs)


def along_y(step):
    return lambda y, x, z, c: ((y + step) % NY, x, z, c)


def along_z(step):
    return lambda y, x, z, c: (y, x, (z + step) % NZ, c)


def flip_z(bit):
    return lambda y, x, z, c: (y, x, z ^ bit, c)


def swap_x(y, x, z, c):
    return (y, x ^ 1, z, c)


def swap_core(y, x, z, c):
    return (y, x, z, 1 - c)


def same_core(y, x, z, c):
    return (y, x, (z + 1 - 2 * c) % NZ, c)


def cross_core(y, x, z, c):
    return (y, x, (z - 1 + 2 * c) % NZ, 1 - c)


def raw_kernel(pattern, showers, geometry, out, masked, *, part_of):
    layers = pattern.shape[1]
    cells = geometry.shape[0] // layers
    per = geometry.shape[1] // BLOCK
    for layer in range(layers):
        for part in range(per):
            rows = pl.ds(layer * cells, cells)
            cols = pl.ds(part * BLOCK, BLOCK)
            on = pattern[part_of * per + part, layer].astype(jnp.float32).astype(jnp.bfloat16)
            masked[rows, cols] = geometry[rows, cols] * on
    out[...] = lax.dot_general(
        showers[...], masked[...], (((0,), (0,)), ((), ())), preferred_element_type=jnp.float32
    )


def raw_partial(showers, geometry, pattern, part_of):
    rows, depth = showers.shape
    width = CHUNK
    return pl.pallas_call(
        functools.partial(raw_kernel, part_of=part_of),
        grid=(1,),
        in_specs=[
            pl.BlockSpec(memory_space=pltpu.SMEM),
            pl.BlockSpec((depth, rows), lambda i: (0, 0)),
            pl.BlockSpec((depth, width), lambda i: (0, part_of)),
        ],
        out_specs=pl.BlockSpec((rows, width), lambda i: (0, 0)),
        out_shape=jax.ShapeDtypeStruct((rows, width), jnp.float32),
        scratch_shapes=[pltpu.VMEM((depth, width), jnp.bfloat16)],
        compiler_params=pltpu.CompilerParams(vmem_limit_bytes=60 * 2**20),
        cost_estimate=pl.CostEstimate(
            flops=2 * rows * depth * width, bytes_accessed=5 * 2**20, transcendentals=0
        ),
        name="raw",
    )(pattern.T, showers.T, geometry)


def pair_kernel(*refs, row_cuts, tag_cuts, col_sizes, n_args):
    n_cols = len(col_sizes)
    odd_here = refs[0]
    args = refs[1 : 1 + n_args]
    cols = refs[1 + n_args : 1 + n_args + n_cols]
    outs = refs[1 + n_args + n_cols : 4 + n_args + n_cols]
    (
        rows_at, cols_at, row_tags, col_tags, sums, counts, row_sems, col_sems, tag_sems, row_tag_sems,
    ) = refs[4 + n_args + n_cols :]

    def start(source, first, size, target, place, sem):
        copy = pltpu.make_async_copy(
            source.at[pl.ds(first, size), :], target.at[pl.ds(place, size), :], sem
        )
        copy.start()
        return copy

    starts = [sum(col_sizes[:at]) for at in range(n_cols)]
    depth = sum(col_sizes)

    def col_copies(at):
        return [
            start(cols[at], TAG, col_sizes[at], cols_at, starts[at], col_sems.at[at]),
            start(cols[at], 0, TAG, col_tags, at * TAG, tag_sems.at[at]),
        ]

    held = {at: col_copies(at) for at in range(2)}
    tag_copies = [
        start(args[arg], first, TAG, row_tags, at * TAG, row_tag_sems.at[at])
        for at, (arg, first) in enumerate(tag_cuts)
    ]
    row_copies, total = [], 0
    for at, (arg, first, size) in enumerate(row_cuts):
        row_copies.append((total, start(args[arg], first, size, rows_at, total, row_sems.at[at])))
        total += size
    for at in range(2, n_cols):
        held[at] = col_copies(at)
    sums[...] = jnp.zeros_like(sums)
    counts[...] = jnp.zeros_like(counts)
    for copy in tag_copies:
        copy.wait()

    def bin_of(code):
        source = (code >= BINS).astype(jnp.float32)
        return code - BINS * source, source

    waited_rows = waited_cols = 0
    low = 0
    while low < depth:
        high = depth if depth - low < 3 * BLOCK else low + 2 * BLOCK
        while waited_cols < n_cols and starts[waited_cols] < high:
            for copy in held[waited_cols]:
                copy.wait()
            waited_cols += 1
        for first in range(0, total, CHUNK):
            size = min(CHUNK, total - first)
            while waited_rows < len(row_copies) and row_copies[waited_rows][0] < first + size:
                row_copies[waited_rows][1].wait()
                waited_rows += 1
            odd = first >= 2 * CHUNK
            set_of = 0 if odd else first // CHUNK
            tag = row_tags[pl.ds(set_of * TAG + 4, 1), pl.ds(0, BLOCK)].astype(jnp.float32) - 1.0
            bins, _ = bin_of(tag)
            if odd:
                bins = jnp.where(odd_here[0] > 0, bins, -2.0)
            bins = jnp.concatenate([bins] * (size // BLOCK), axis=1)
            lanes = pl.ds(first, size)
            products = lax.dot_general(
                cols_at[pl.ds(low, high - low), :],
                rows_at[lanes, :],
                (((1,), (1,)), ((), ())),
                preferred_element_type=jnp.float32,
            )
            shifted = products + 32.0
            cubes = shifted * shifted * shifted
            one = jnp.zeros((8, size), jnp.float32)
            zero = jnp.zeros((8, size), jnp.float32)
            n_one = jnp.zeros((1, size), jnp.float32)
            n_zero = jnp.zeros((1, size), jnp.float32)
            for group in range(low // PIECE, high // PIECE):
                at = group * PIECE // BLOCK
                if odd and col_sizes[at] == PIECE:
                    continue
                block = cubes[group * PIECE - low : (group + 1) * PIECE - low]
                if first == 0 and at == 0:
                    lane = lax.broadcasted_iota(jnp.int32, block.shape, 1)
                    sub = lax.broadcasted_iota(jnp.int32, block.shape, 0)
                    block = jnp.where(lane == sub + group * PIECE, 0.0, block)
                part = (block[0:8] + block[8:16]) + (block[16:24] + block[24:32])
                row = at * TAG + group % 4
                code = col_tags[pl.ds(row, 1), pl.ds(0, size)].astype(jnp.float32) - 1.0
                bin_id, source = bin_of(code)
                match = (bins == bin_id).astype(jnp.float32)
                is_one = match * source
                is_zero = match - is_one
                one += is_one * part
                zero += is_zero * part
                n_one += is_one
                n_zero += is_zero
            sums[0:8, lanes] += one
            sums[8:16, lanes] += zero
            counts[0:1, lanes] += n_one
            counts[1:2, lanes] += n_zero
        low = high
    for out, first in zip(outs, range(0, total, CHUNK)):
        lanes = pl.ds(first, out.shape[1])
        out[0:1, :] = jnp.sum(sums[0:8, lanes], axis=0, keepdims=True)
        out[1:2, :] = jnp.sum(sums[8:16, lanes], axis=0, keepdims=True)
        out[2:4, :] = counts[0:2, lanes]


def pair_sums(odd_here, args, row_cuts, tag_cuts, cols):
    col_sizes = tuple(size for _, size in cols)
    total, depth = sum(size for _, _, size in row_cuts), sum(col_sizes)
    feats = args[0].shape[1]
    hbm = pl.BlockSpec(memory_space=pl.ANY)
    vmem = pl.BlockSpec(memory_space=pltpu.VMEM)
    widths = [min(CHUNK, total - first) for first in range(0, total, CHUNK)]
    dma = pltpu.SemaphoreType.DMA
    return pl.pallas_call(
        functools.partial(
            pair_kernel,
            row_cuts=tuple(row_cuts),
            tag_cuts=tuple(tag_cuts),
            col_sizes=col_sizes,
            n_args=len(args),
        ),
        in_specs=[pl.BlockSpec(memory_space=pltpu.SMEM)] + [hbm] * (len(args) + len(cols)),
        out_specs=[vmem] * len(widths),
        out_shape=[jax.ShapeDtypeStruct((4, width), jnp.float32) for width in widths],
        scratch_shapes=[
            pltpu.VMEM((total, feats), jnp.bfloat16),
            pltpu.VMEM((depth, feats), jnp.bfloat16),
            pltpu.VMEM((TAG * len(tag_cuts), feats), jnp.bfloat16),
            pltpu.VMEM((TAG * len(cols), feats), jnp.bfloat16),
            pltpu.VMEM((16, total), jnp.float32),
            pltpu.VMEM((8, total), jnp.float32),
            dma((len(row_cuts),)),
            dma((len(cols),)),
            dma((len(cols),)),
            dma((len(tag_cuts),)),
        ],
        compiler_params=pltpu.CompilerParams(vmem_limit_bytes=58 * 2**20),
        cost_estimate=pl.CostEstimate(
            flops=2 * total * depth * feats,
            bytes_accessed=2 * (total + depth) * feats,
            transcendentals=0,
        ),
        name="pairs",
    )(odd_here, *args, *[c for c, _ in cols])


def shards(showers, geometry, pattern, bins, sources):
    y = lax.axis_index("layer")
    s = lax.axis_index("shower")
    x, z, c = s // (NZ * NC), (s // NC) % NZ, s % NC
    feats = geometry.shape[1]
    blocks = bins.shape[0]

    codes = (bins + BINS * sources + 1).astype(jnp.float32)
    line = lax.broadcasted_iota(jnp.int32, (TAG, feats), 0)
    lane = lax.broadcasted_iota(jnp.int32, (TAG, feats), 1) // PIECE
    which = jnp.where(line == blocks, lane, line)
    tag = jnp.zeros((TAG, feats), jnp.float32)
    for group in range(blocks):
        tag = jnp.where(which == group, codes[group], tag)
    tag = tag.astype(jnp.bfloat16)

    halves = []
    for part_of in range(feats // CHUNK):
        partial_sums = raw_partial(showers, geometry, pattern, part_of)
        partial_sums = partial_sums.reshape(blocks, NY, PIECE, CHUNK)

        def share(turn):
            part = lax.dynamic_index_in_dim(partial_sums, (y + turn) % NY, 1, keepdims=False)
            return part.reshape(BLOCK, CHUNK)

        raw = share(0)
        arrived = [permute(share(turn).astype(jnp.float16), along_y(turn)) for turn in (2, 1, 3)]
        halves.append((raw, arrived))
    raws = []
    for raw, arrived in halves:
        for part in arrived:
            raw = raw + part.astype(jnp.float32)
        raws.append(raw)
    square = sum(jnp.sum(raw * raw, axis=1, keepdims=True) for raw in raws)
    scale = lax.rsqrt(square / feats + 1e-05)
    own = jnp.concatenate([(raw * scale).astype(jnp.bfloat16) for raw in raws], axis=1)
    own = lax.optimization_barrier(jnp.concatenate([tag, own], axis=0))

    y_way = lambda y, x, z, c: ((y + 1 - 2 * c) % NY, x, z, c)
    fence = lambda *values: lax.optimization_barrier(values)
    same, cross = [permute(own, same_core)], [permute(own, cross_core)]
    ya = permute(own[TAG:], along_y(1))
    yb = permute(own[TAG:], along_y(3))
    x1 = permute(own, swap_x)
    same[0], cross[0], ya, yb, x1, own = fence(same[0], cross[0], ya, yb, x1, own)

    same.append(permute(same[0], same_core))
    cross.append(permute(cross[0], same_core))
    y2 = permute(jnp.where(c == 0, ya, yb), y_way)
    xa = permute(ya, swap_x)
    own_other = permute(own, swap_core)
    same[1], cross[1], y2, xa, own_other, yb, same[0], cross[0] = fence(
        same[1], cross[1], y2, xa, own_other, yb, same[0], cross[0]
    )

    same.append(permute(same[1], same_core))
    cross.append(permute(cross[1], same_core))
    xb = permute(yb, swap_x)
    same_other, cross_other = [permute(same[0], swap_core)], [permute(cross[0], swap_core)]
    same[2], cross[2], xb, same_other[0], cross_other[0], same[1], cross[1], y2, yb, ya = fence(
        same[2], cross[2], xb, same_other[0], cross_other[0], same[1], cross[1], y2, yb, ya
    )

    same.append(permute(same[2], same_core))
    w2 = permute(jnp.where(c == 0, xa, xb), y_way)
    for turn in (1, 2):
        same_other.append(permute(same[turn], swap_core))
        cross_other.append(permute(cross[turn], swap_core))
    same_other.append(permute(same[3], swap_core))

    head = TAG + PIECE
    held = [own, same[0], same[1], same[2], same[2], cross[2], cross[1], cross[0]]
    piece = lax.select_n(z, *[value[:head] for value in held])
    to_one = lambda y, x, z, c: (y, 1, z, c)
    side = lambda z: 0 if z < 4 else 1
    piece_near = permute(
        piece, to_one, keep=lambda y, x, z, c: x == 2 and z != 4 and c == side(z)
    )
    piece_far = permute(
        piece,
        lambda y, x, z, c: (y, 1, z + 1, c),
        keep=lambda y, x, z, c: x == 2 and z == 3 and c == 0,
    )
    piece = piece_near + piece_far
    piece = piece + permute(piece, swap_core)
    odd = jnp.concatenate([own[TAG:head], yb[:PIECE], y2[:PIECE], ya[:PIECE]], axis=0)
    at_start = lambda y, x, z, c: z == 0 and c == 0
    odd = permute(odd, to_one, keep=lambda *a: a[1] == 2 and at_start(*a))
    odd = odd + permute(odd, swap_x, keep=lambda *a: a[1] == 1 and at_start(*a))

    args = [own, x1, ya, yb, y2, xa, xb, w2, odd]
    tag_cuts = [(0, 0), (1, 0)]
    row_cuts = [(0, TAG), (3, 0), (4, 0), (2, 0), (1, TAG), (6, 0), (7, 0), (5, 0), (8, 0)]
    row_cuts = [(arg, first, BLOCK) for arg, first in row_cuts]
    cols = [own, own_other]
    for turn in range(3):
        cols += [same[turn], cross[turn], same_other[turn], cross_other[turn]]
    cols += [same[3], same_other[3]]
    cols = [(value, BLOCK) for value in cols] + [(piece, PIECE)]
    odd_here = ((x < 2) & (z == 0) & (c == 0)).astype(jnp.int32).reshape(1)
    stats, stats_x, odd_stats = pair_sums(odd_here, args, row_cuts, tag_cuts, cols)

    kept = stats + permute(stats_x, swap_x)
    odd_total = jnp.zeros_like(odd_stats)
    for start in (0, 1):
        odd_total = odd_total + permute(
            odd_stats,
            lambda y, x, z, c: (y, 2, z, c),
            keep=lambda *a, start=start: a[1] == start and at_start(*a),
        )
    odd_total = odd_total.reshape(4, NY, PIECE)
    kept = kept.reshape(4, NY, BLOCK) + jnp.pad(odd_total, ((0, 0), (0, 0), (0, BLOCK - PIECE)))
    total = kept
    for turn in (2, 1, 3):
        total = total + jnp.roll(permute(kept, along_y(turn)), -turn, axis=1)
    weight = 1.0 / (PIECE * 32.0**3)
    proof = (total[0] / total[2] - total[1] / total[3]) * weight
    proof = jnp.concatenate([proof, proof], axis=0)
    proof = lax.dynamic_slice_in_dim(proof, (NY - y) % NY, NY, 0).reshape(NY, blocks, PIECE)
    return jnp.transpose(proof, (1, 0, 2)).reshape(-1)


def solution(mesh):
    placed = (P("shower", "layer"), P("layer", None), P("layer", None), P("shower"), P("shower"))
    return jax.shard_map(shards, mesh=mesh, in_specs=placed, out_specs=P("shower"), check_vma=False)
```

```python
import functools

import jax
import jax.numpy as jnp
from jax import lax
from jax.experimental import pallas as pl
from jax.experimental.pallas import tpu as pltpu
from jax.sharding import PartitionSpec as P

BLOCK = 128
PIECE = 32
TAG = 16
BINS = 8
CHUNK = 512
AXES = ("layer", "shower")
NY, NX, NZ, NC = 4, 4, 8, 2


def flat(y, x, z, c):
    return y * (NX * NZ * NC) + (x * NZ + z) * NC + c


def permute(value, move, keep=lambda y, x, z, c: True):
    pairs = [
        (flat(y, x, z, c), flat(*move(y, x, z, c)))
        for y in range(NY)
        for x in range(NX)
        for z in range(NZ)
        for c in range(NC)
        if keep(y, x, z, c)
    ]
    return lax.ppermute(value, AXES, pairs)


def along_y(step):
    return lambda y, x, z, c: ((y + step) % NY, x, z, c)


def along_z(step):
    return lambda y, x, z, c: (y, x, (z + step) % NZ, c)


def flip_z(bit):
    return lambda y, x, z, c: (y, x, z ^ bit, c)


def swap_x(y, x, z, c):
    return (y, x ^ 1, z, c)


def swap_core(y, x, z, c):
    return (y, x, z, 1 - c)


def same_core(y, x, z, c):
    return (y, x, (z + 1 - 2 * c) % NZ, c)


def cross_core(y, x, z, c):
    return (y, x, (z - 1 + 2 * c) % NZ, 1 - c)


def raw_kernel(pattern, showers, geometry, out, masked):
    step = pl.program_id(0)
    layers = pattern.shape[1]
    cells = geometry.shape[0] // layers
    per = geometry.shape[1] // BLOCK
    for layer in range(layers):
        for part in range(per):
            rows = pl.ds(layer * cells, cells)
            cols = pl.ds(part * BLOCK, BLOCK)
            on = pattern[step * per + part, layer].astype(jnp.float32).astype(jnp.bfloat16)
            masked[rows, cols] = geometry[rows, cols] * on
    out[...] = lax.dot_general(
        showers[...], masked[...], (((0,), (0,)), ((), ())), preferred_element_type=jnp.float32
    )


def raw_partial(showers, geometry, pattern):
    rows, depth = showers.shape
    feats = geometry.shape[1]
    width = 512
    return pl.pallas_call(
        raw_kernel,
        grid=(feats // width,),
        in_specs=[
            pl.BlockSpec(memory_space=pltpu.SMEM),
            pl.BlockSpec((depth, rows), lambda i: (0, 0)),
            pl.BlockSpec((depth, width), lambda i: (0, i)),
        ],
        out_specs=pl.BlockSpec((rows, width), lambda i: (0, i)),
        out_shape=jax.ShapeDtypeStruct((rows, feats), jnp.float32),
        scratch_shapes=[pltpu.VMEM((depth, width), jnp.bfloat16)],
        compiler_params=pltpu.CompilerParams(vmem_limit_bytes=60 * 2**20),
        cost_estimate=pl.CostEstimate(
            flops=2 * rows * depth * feats, bytes_accessed=8 * 2**20, transcendentals=0
        ),
        name="raw",
    )(pattern.T, showers.T, geometry)


def pair_kernel(*refs, tag_cuts, col_cuts, n_args):
    n_cols = len(col_cuts)
    place = refs[0]
    args = refs[1 : 1 + n_args]
    out_near, out_far, out_theirs, out_odd = refs[1 + n_args : 5 + n_args]
    rows_at, cols_at, row_tags, col_tags, row_sems, col_sems, tag_sems = refs[5 + n_args :]
    odd_here, core = place[0], place[1]
    tagged = BLOCK + TAG
    row_args = args[n_cols_args(col_cuts) :]

    def start(source, first, size, target, at, sem):
        copy = pltpu.make_async_copy(
            source.at[pl.ds(first, size), :], target.at[pl.ds(at, size), :], sem
        )
        copy.start()
        return copy

    waits, depth = [], 0
    for at, (arg, first, size) in enumerate(col_cuts):
        waits.append(start(args[arg], first, size, cols_at, depth, col_sems.at[at]))
        waits.append(start(args[arg], first - TAG, TAG, col_tags, at * TAG, tag_sems.at[at]))
        depth += size
    for at, (arg, first) in enumerate(tag_cuts):
        waits.append(start(args[arg], first, TAG, row_tags, at * TAG, tag_sems.at[n_cols + at]))

    own, own_t, x1, x1_t, y1, y1_t, y2, y2_t, xx, xx_t, w2, w2_t, odd_rows = row_args
    turn = jnp.where(core == 0, 3, 1)
    side = [4 * CHUNK // 2 * jnp.where(core == b, 0, 1) for b in range(NC)]
    made = []

    def rows(source, first, at):
        at = at if isinstance(at, int) else pl.multiple_of(at, BLOCK)
        made.append(start(source, first, BLOCK, rows_at, at, row_sems.at[len(made)]))

    rows(own, TAG, 0)
    rows(y2, 0, 2 * BLOCK)
    for b in range(NC):
        rows(y1, TAG + b * tagged, side[b] + turn * BLOCK)
        rows(y1_t, TAG + b * tagged, side[b] + (NY - turn) * BLOCK)
    rows(own_t, TAG, 2 * CHUNK)
    rows(y2_t, 0, 2 * CHUNK + 2 * BLOCK)
    n_near = len(made)
    rows(x1, TAG, CHUNK)
    rows(w2, 0, CHUNK + 2 * BLOCK)
    for b in range(NC):
        rows(xx, TAG + b * tagged, CHUNK + side[b] + turn * BLOCK)
        rows(xx_t, TAG + b * tagged, CHUNK + side[b] + (NY - turn) * BLOCK)
    rows(x1_t, TAG, 3 * CHUNK)
    rows(w2_t, 0, 3 * CHUNK + 2 * BLOCK)
    rows(odd_rows, 0, 4 * CHUNK)
    for copy in waits:
        copy.wait()

    def bin_of(code):
        source = (code >= BINS).astype(jnp.float32)
        return code - BINS * source, source

    for chunk in (0, 2, 1, 3, 4):
        if chunk == 0:
            for copy in made[:n_near]:
                copy.wait()
        if chunk == 1:
            for copy in made[n_near:]:
                copy.wait()
        first = chunk * CHUNK
        odd = chunk == 4
        size = BLOCK if odd else CHUNK
        set_of = 0 if odd else chunk
        tag = row_tags[pl.ds(set_of * TAG + 4, 1), pl.ds(0, BLOCK)].astype(jnp.float32) - 1.0
        bins, _ = bin_of(tag)
        if odd:
            bins = jnp.where(odd_here > 0, bins, -2.0)
        bins = jnp.concatenate([bins] * (size // BLOCK), axis=1)
        one = jnp.zeros((8, size), jnp.float32)
        zero = jnp.zeros((8, size), jnp.float32)
        n_one = jnp.zeros((1, size), jnp.float32)
        n_zero = jnp.zeros((1, size), jnp.float32)
        low = 0
        while low < depth:
            high = depth if depth - low < 3 * BLOCK else low + 2 * BLOCK
            products = lax.dot_general(
                cols_at[pl.ds(low, high - low), :],
                rows_at[pl.ds(first, size), :],
                (((1,), (1,)), ((), ())),
                preferred_element_type=jnp.float32,
            )
            shifted = products + 32.0
            cubes = shifted * shifted * shifted
            for group in range(low // PIECE, high // PIECE):
                at = group * PIECE // BLOCK
                if odd and col_cuts[at][2] == PIECE:
                    continue
                block = cubes[group * PIECE - low : (group + 1) * PIECE - low]
                if first == 0 and at == 0:
                    lane = lax.broadcasted_iota(jnp.int32, block.shape, 1)
                    sub = lax.broadcasted_iota(jnp.int32, block.shape, 0)
                    block = jnp.where(lane == sub + group * PIECE, 0.0, block)
                part = (block[0:8] + block[8:16]) + (block[16:24] + block[24:32])
                row = at * TAG + group % 4
                code = col_tags[pl.ds(row, 1), pl.ds(0, size)].astype(jnp.float32) - 1.0
                bin_id, source = bin_of(code)
                match = (bins == bin_id).astype(jnp.float32)
                is_one = match * source
                is_zero = match - is_one
                one += is_one * part
                zero += is_zero * part
                n_one += is_one
                n_zero += is_zero
            low = high
        targets = {0: [(out_near, 0)], 1: [(out_far, 0)], 2: [(out_theirs, 0)]}
        targets |= {3: [(out_theirs, CHUNK)], 4: [(out_theirs, 2 * CHUNK), (out_odd, 0)]}
        for out, place_at in targets[chunk]:
            lanes = pl.ds(place_at, size)
            out[0:1, lanes] = jnp.sum(one, axis=0, keepdims=True)
            out[1:2, lanes] = jnp.sum(zero, axis=0, keepdims=True)
            out[2:3, lanes] = n_one
            out[3:4, lanes] = n_zero


def n_cols_args(col_cuts):
    return 1 + max(arg for arg, _, _ in col_cuts)


def pair_sums(place, col_args, row_args, col_cuts, tag_cuts):
    args = col_args + row_args
    total, depth = 4 * CHUNK + BLOCK, sum(size for _, _, size in col_cuts)
    feats = args[0].shape[1]
    hbm = pl.BlockSpec(memory_space=pl.ANY)
    vmem = pl.BlockSpec(memory_space=pltpu.VMEM)
    dma = pltpu.SemaphoreType.DMA
    widths = [CHUNK, CHUNK, 2 * CHUNK + BLOCK, BLOCK]
    return pl.pallas_call(
        functools.partial(
            pair_kernel, tag_cuts=tuple(tag_cuts), col_cuts=tuple(col_cuts), n_args=len(args)
        ),
        in_specs=[pl.BlockSpec(memory_space=pltpu.SMEM)] + [hbm] * len(args),
        out_specs=[vmem] * len(widths),
        out_shape=[jax.ShapeDtypeStruct((4, width), jnp.float32) for width in widths],
        scratch_shapes=[
            pltpu.VMEM((total, feats), jnp.bfloat16),
            pltpu.VMEM((depth, feats), jnp.bfloat16),
            pltpu.VMEM((TAG * len(tag_cuts), feats), jnp.bfloat16),
            pltpu.VMEM((TAG * len(col_cuts), feats), jnp.bfloat16),
            dma((17,)),
            dma((len(col_cuts),)),
            dma((len(col_cuts) + len(tag_cuts),)),
        ],
        compiler_params=pltpu.CompilerParams(vmem_limit_bytes=58 * 2**20),
        cost_estimate=pl.CostEstimate(
            flops=2 * total * depth * feats,
            bytes_accessed=2 * (total + depth) * feats,
            transcendentals=0,
        ),
        name="pairs",
    )(place, *args)


def shards(showers, geometry, pattern, bins, sources):
    y = lax.axis_index("layer")
    s = lax.axis_index("shower")
    x, z, c = s // (NZ * NC), (s // NC) % NZ, s % NC
    feats = geometry.shape[1]
    blocks = bins.shape[0]

    codes = (bins + BINS * sources + 1).astype(jnp.float32)
    line = lax.broadcasted_iota(jnp.int32, (TAG, feats), 0)
    lane = lax.broadcasted_iota(jnp.int32, (TAG, feats), 1) // PIECE
    which = jnp.where(line == blocks, lane, line)
    tag = jnp.zeros((TAG, feats), jnp.float32)
    for group in range(blocks):
        tag = jnp.where(which == group, codes[group], tag)
    tag = tag.astype(jnp.bfloat16)

    partial_sums = raw_partial(showers, geometry, pattern).reshape(blocks, NY, PIECE, feats)

    def share(turn):
        part = lax.dynamic_index_in_dim(partial_sums, (y + turn) % NY, 1, keepdims=False)
        return part.reshape(BLOCK, feats)

    raw = share(0)
    arrived = [permute(share(turn).astype(jnp.float16), along_y(turn)) for turn in (2, 1, 3)]
    for part in arrived:
        raw = raw + part.astype(jnp.float32)
    scale = lax.rsqrt(jnp.mean(raw * raw, axis=1, keepdims=True) + 1e-05)
    own = jnp.concatenate([tag, (raw * scale).astype(jnp.bfloat16)], axis=0)

    fence = lambda *values: lax.optimization_barrier(values)
    tagged = BLOCK + TAG
    y_way = lambda y, x, z, c: ((y + 1 - 2 * c) % NY, x, z, c)
    own_t = permute(own, swap_core)
    chip = jnp.where(c == 0, jnp.concatenate([own, own_t]), jnp.concatenate([own_t, own]))
    z1 = permute(chip, same_core)
    y1 = permute(chip, y_way)
    x1 = permute(own, swap_x)
    z1, y1, x1 = fence(z1, y1, x1)

    z2 = permute(z1, same_core)
    y2 = permute(jnp.where(c == 0, y1[TAG:tagged], y1[tagged + TAG :]), y_way)
    xx = permute(y1, swap_x)
    y1_t = permute(y1, swap_core)
    x1_t = permute(x1, swap_core)
    z1, z2, y2, xx, y1_t, x1_t = fence(z1, z2, y2, xx, y1_t, x1_t)

    z3 = permute(z2, same_core)
    w2 = permute(y2, swap_x)
    head = TAG + PIECE
    odd_rows = jnp.concatenate([own[TAG:head], y1_t[TAG:head], y2[:PIECE], y1[TAG:head]], axis=0)
    at_start = lambda y, x, z, c: z == 0 and c == 0
    odd_at = [
        permute(
            odd_rows,
            lambda y, x, z, c, to=to: (y, to, z, c),
            keep=lambda *a: a[1] == 2 and at_start(*a),
        )
        for to in (1, 0)
    ]
    y2_t = permute(y2, swap_core)
    z2, z3, w2, y2_t, *odd_at = fence(z2, z3, w2, y2_t, *odd_at)

    z4 = permute(jnp.where(c == 0, z3[:tagged], z3[tagged:]), same_core)
    held = [own, z1, z2, z3, z3, z3, z2, z1]
    piece = lax.select_n(z, *[value[:head] for value in held])
    side = lambda z: 0 if z < 4 else 1
    piece_near = permute(
        piece,
        lambda y, x, z, c: (y, 1, z, c),
        keep=lambda y, x, z, c: x == 2 and z != 4 and c == side(z),
    )
    piece_far = permute(
        piece,
        lambda y, x, z, c: (y, 1, z + 1, c),
        keep=lambda y, x, z, c: x == 2 and z == 3 and c == 0,
    )
    xx_t = permute(xx, swap_core)
    w2_t = permute(w2, swap_core)
    odd_rows = odd_at[0] + odd_at[1]
    odd_rows = odd_rows + permute(
        odd_rows, swap_core, keep=lambda *a: a[1] < 2 and at_start(*a)
    )
    piece = piece_near + piece_far

    col_args = [own, z1, z2, z3, z4, piece]
    col_cuts = [(0, TAG, BLOCK)]
    for arg in (1, 2, 3):
        col_cuts += [(arg, TAG, BLOCK), (arg, tagged + TAG, BLOCK)]
    col_cuts += [(4, TAG, BLOCK), (5, TAG, PIECE)]
    row_args = [own, own_t, x1, x1_t, y1, y1_t, y2, y2_t, xx, xx_t, w2, w2_t, odd_rows]
    tag_cuts = [(6, 0), (8, 0), (7, 0), (9, 0)]
    place = jnp.stack([((x < 2) & (z == 0)).astype(jnp.int32), c.astype(jnp.int32)])
    near, far, theirs, odd_stats = pair_sums(place, col_args, row_args, col_cuts, tag_cuts)

    theirs = permute(theirs, swap_core)
    kept = near + theirs[:, :CHUNK] + permute(far + theirs[:, CHUNK : 2 * CHUNK], swap_x)
    odd_stats = odd_stats + theirs[:, 2 * CHUNK :]
    odd_total = jnp.zeros_like(odd_stats)
    for start in (0, 1):
        odd_total = odd_total + permute(
            odd_stats,
            lambda y, x, z, c: (y, 2, z, c),
            keep=lambda *a, start=start: a[1] == start and at_start(*a),
        )
    odd_total = odd_total.reshape(4, NY, PIECE)
    kept = kept.reshape(4, NY, BLOCK) + jnp.pad(odd_total, ((0, 0), (0, 0), (0, BLOCK - PIECE)))
    total = kept
    for turn in (2, 1, 3):
        total = total + jnp.roll(permute(kept, along_y(turn)), -turn, axis=1)
    weight = 1.0 / (PIECE * 32.0**3)
    proof = (total[0] / total[2] - total[1] / total[3]) * weight
    proof = jnp.concatenate([proof, proof], axis=0)
    proof = lax.dynamic_slice_in_dim(proof, (NY - y) % NY, NY, 0).reshape(NY, blocks, PIECE)
    return jnp.transpose(proof, (1, 0, 2)).reshape(-1)


def solution(mesh):
    placed = (P("shower", "layer"), P("layer", None), P("layer", None), P("shower"), P("shower"))
    return jax.shard_map(shards, mesh=mesh, in_specs=placed, out_specs=P("shower"), check_vma=False)
```

```python
import functools

import jax
import jax.numpy as jnp
from jax import lax
from jax.experimental import pallas as pl
from jax.experimental.pallas import tpu as pltpu
from jax.sharding import PartitionSpec as P

BLOCK = 128
PIECE = 32
TAG = 16
BINS = 8
CHUNK = 512
AXES = ("layer", "shower")
NY, NX, NZ, NC = 4, 4, 8, 2


def flat(y, x, z, c):
    return y * (NX * NZ * NC) + (x * NZ + z) * NC + c


def permute(value, move, keep=lambda y, x, z, c: True):
    pairs = [
        (flat(y, x, z, c), flat(*move(y, x, z, c)))
        for y in range(NY)
        for x in range(NX)
        for z in range(NZ)
        for c in range(NC)
        if keep(y, x, z, c)
    ]
    return lax.ppermute(value, AXES, pairs)


def along_y(step):
    return lambda y, x, z, c: ((y + step) % NY, x, z, c)


def along_z(step):
    return lambda y, x, z, c: (y, x, (z + step) % NZ, c)


def flip_z(bit):
    return lambda y, x, z, c: (y, x, z ^ bit, c)


def swap_x(y, x, z, c):
    return (y, x ^ 1, z, c)


def swap_core(y, x, z, c):
    return (y, x, z, 1 - c)


def same_core(y, x, z, c):
    return (y, x, (z + 1 - 2 * c) % NZ, c)


def cross_core(y, x, z, c):
    return (y, x, (z - 1 + 2 * c) % NZ, 1 - c)


def raw_kernel(pattern, showers, geometry, out, masked):
    step = pl.program_id(0)
    layers = pattern.shape[1]
    cells = geometry.shape[0] // layers
    per = geometry.shape[1] // BLOCK
    for layer in range(layers):
        for part in range(per):
            rows = pl.ds(layer * cells, cells)
            cols = pl.ds(part * BLOCK, BLOCK)
            on = pattern[step * per + part, layer].astype(jnp.float32).astype(jnp.bfloat16)
            masked[rows, cols] = geometry[rows, cols] * on
    out[...] = lax.dot_general(
        showers[...], masked[...], (((0,), (0,)), ((), ())), preferred_element_type=jnp.float32
    )


def raw_partial(showers, geometry, pattern):
    rows, depth = showers.shape
    feats = geometry.shape[1]
    width = 512
    return pl.pallas_call(
        raw_kernel,
        grid=(feats // width,),
        in_specs=[
            pl.BlockSpec(memory_space=pltpu.SMEM),
            pl.BlockSpec((depth, rows), lambda i: (0, 0)),
            pl.BlockSpec((depth, width), lambda i: (0, i)),
        ],
        out_specs=pl.BlockSpec((rows, width), lambda i: (0, i)),
        out_shape=jax.ShapeDtypeStruct((rows, feats), jnp.float32),
        scratch_shapes=[pltpu.VMEM((depth, width), jnp.bfloat16)],
        compiler_params=pltpu.CompilerParams(vmem_limit_bytes=60 * 2**20),
        cost_estimate=pl.CostEstimate(
            flops=2 * rows * depth * feats, bytes_accessed=8 * 2**20, transcendentals=0
        ),
        name="raw",
    )(pattern.T, showers.T, geometry)


def pair_kernel(*refs, tag_cuts, col_cuts, n_args):
    n_cols = len(col_cuts)
    place = refs[0]
    args = refs[1 : 1 + n_args]
    out_near, out_far, out_theirs, out_odd = refs[1 + n_args : 5 + n_args]
    rows_at, cols_at, row_tags, col_tags, row_sems, col_sems, tag_sems = refs[5 + n_args :]
    odd_here, core = place[0], place[1]
    tagged = BLOCK + TAG
    row_args = args[n_cols_args(col_cuts) :]

    def start(source, first, size, target, at, sem):
        copy = pltpu.make_async_copy(
            source.at[pl.ds(first, size), :], target.at[pl.ds(at, size), :], sem
        )
        copy.start()
        return copy

    starts = [sum(size for _, _, size in col_cuts[:at]) for at in range(n_cols)]
    depth = sum(size for _, _, size in col_cuts)

    def load_col(at):
        arg, first, size = col_cuts[at]
        return [
            start(args[arg], first, size, cols_at, starts[at], col_sems.at[at]),
            start(args[arg], first - TAG, TAG, col_tags, at * TAG, tag_sems.at[at]),
        ]

    held = {at: load_col(at) for at in range(2)}
    waits = []
    for at, (arg, first) in enumerate(tag_cuts):
        waits.append(start(args[arg], first, TAG, row_tags, at * TAG, tag_sems.at[n_cols + at]))

    own, own_t, x1, x1_t, y1, y1_t, y2, y2_t = row_args[:8]
    xa, xb, xa_t, xb_t, w2, w2_t, odd_rows = row_args[8:]
    turn = jnp.where(core == 0, 3, 1)
    side = [4 * CHUNK // 2 * jnp.where(core == b, 0, 1) for b in range(NC)]
    made = []

    def rows(source, first, at):
        at = at if isinstance(at, int) else pl.multiple_of(at, BLOCK)
        made.append(start(source, first, BLOCK, rows_at, at, row_sems.at[len(made)]))

    rows(own, TAG, 0)
    rows(y2, 0, 2 * BLOCK)
    for b in range(NC):
        rows(y1, TAG + b * tagged, side[b] + turn * BLOCK)
        rows(y1_t, TAG + b * tagged, side[b] + (NY - turn) * BLOCK)
    n_near = len(made)
    for copy in waits + made:
        copy.wait()
    for at in range(2, n_cols):
        held[at] = load_col(at)
    rows(own_t, TAG, 2 * CHUNK)
    rows(y2_t, 0, 2 * CHUNK + 2 * BLOCK)
    n_far = len(made)
    rows(x1, TAG, CHUNK)
    rows(w2, 0, CHUNK + 2 * BLOCK)
    for b in range(NC):
        rows((xa, xb)[b], 0, CHUNK + side[b] + turn * BLOCK)
        rows((xa_t, xb_t)[b], 0, CHUNK + side[b] + (NY - turn) * BLOCK)
    rows(x1_t, TAG, 3 * CHUNK)
    rows(w2_t, 0, 3 * CHUNK + 2 * BLOCK)
    rows(odd_rows, 0, 4 * CHUNK)
    waited = 0

    def bin_of(code):
        source = (code >= BINS).astype(jnp.float32)
        return code - BINS * source, source

    for chunk in (0, 2, 1, 3, 4):
        for copy in {2: made[n_near:n_far], 1: made[n_far:]}.get(chunk, []):
            copy.wait()
        first = chunk * CHUNK
        odd = chunk == 4
        size = BLOCK if odd else CHUNK
        set_of = 0 if odd else chunk
        tag = row_tags[pl.ds(set_of * TAG + 4, 1), pl.ds(0, BLOCK)].astype(jnp.float32) - 1.0
        bins, _ = bin_of(tag)
        if odd:
            bins = jnp.where(odd_here > 0, bins, -2.0)
        bins = jnp.concatenate([bins] * (size // BLOCK), axis=1)
        one = jnp.zeros((8, size), jnp.float32)
        zero = jnp.zeros((8, size), jnp.float32)
        n_one = jnp.zeros((1, size), jnp.float32)
        n_zero = jnp.zeros((1, size), jnp.float32)
        low = 0
        while low < depth:
            high = depth if depth - low < 3 * BLOCK else low + 2 * BLOCK
            while waited < n_cols and starts[waited] < high:
                for copy in held[waited]:
                    copy.wait()
                waited += 1
            products = lax.dot_general(
                cols_at[pl.ds(low, high - low), :],
                rows_at[pl.ds(first, size), :],
                (((1,), (1,)), ((), ())),
                preferred_element_type=jnp.float32,
            )
            shifted = products + 32.0
            cubes = shifted * shifted * shifted
            for group in range(low // PIECE, high // PIECE):
                at = group * PIECE // BLOCK
                if odd and col_cuts[at][2] == PIECE:
                    continue
                block = cubes[group * PIECE - low : (group + 1) * PIECE - low]
                if first == 0 and at == 0:
                    lane = lax.broadcasted_iota(jnp.int32, block.shape, 1)
                    sub = lax.broadcasted_iota(jnp.int32, block.shape, 0)
                    block = jnp.where(lane == sub + group * PIECE, 0.0, block)
                part = (block[0:8] + block[8:16]) + (block[16:24] + block[24:32])
                row = at * TAG + group % 4
                code = col_tags[pl.ds(row, 1), pl.ds(0, size)].astype(jnp.float32) - 1.0
                bin_id, source = bin_of(code)
                match = (bins == bin_id).astype(jnp.float32)
                is_one = match * source
                is_zero = match - is_one
                one += is_one * part
                zero += is_zero * part
                n_one += is_one
                n_zero += is_zero
            low = high
        targets = {0: [(out_near, 0)], 1: [(out_far, 0)], 2: [(out_theirs, 0)]}
        targets |= {3: [(out_theirs, CHUNK)], 4: [(out_theirs, 2 * CHUNK), (out_odd, 0)]}
        for out, place_at in targets[chunk]:
            lanes = pl.ds(place_at, size)
            out[0:1, lanes] = jnp.sum(one, axis=0, keepdims=True)
            out[1:2, lanes] = jnp.sum(zero, axis=0, keepdims=True)
            out[2:3, lanes] = n_one
            out[3:4, lanes] = n_zero


def n_cols_args(col_cuts):
    return 1 + max(arg for arg, _, _ in col_cuts)


def pair_sums(place, col_args, row_args, col_cuts, tag_cuts):
    args = col_args + row_args
    total, depth = 4 * CHUNK + BLOCK, sum(size for _, _, size in col_cuts)
    feats = args[0].shape[1]
    hbm = pl.BlockSpec(memory_space=pl.ANY)
    vmem = pl.BlockSpec(memory_space=pltpu.VMEM)
    dma = pltpu.SemaphoreType.DMA
    widths = [CHUNK, CHUNK, 2 * CHUNK + BLOCK, BLOCK]
    return pl.pallas_call(
        functools.partial(
            pair_kernel, tag_cuts=tuple(tag_cuts), col_cuts=tuple(col_cuts), n_args=len(args)
        ),
        in_specs=[pl.BlockSpec(memory_space=pltpu.SMEM)] + [hbm] * len(args),
        out_specs=[vmem] * len(widths),
        out_shape=[jax.ShapeDtypeStruct((4, width), jnp.float32) for width in widths],
        scratch_shapes=[
            pltpu.VMEM((total, feats), jnp.bfloat16),
            pltpu.VMEM((depth, feats), jnp.bfloat16),
            pltpu.VMEM((TAG * len(tag_cuts), feats), jnp.bfloat16),
            pltpu.VMEM((TAG * len(col_cuts), feats), jnp.bfloat16),
            dma((17,)),
            dma((len(col_cuts),)),
            dma((len(col_cuts) + len(tag_cuts),)),
        ],
        compiler_params=pltpu.CompilerParams(vmem_limit_bytes=58 * 2**20),
        cost_estimate=pl.CostEstimate(
            flops=2 * total * depth * feats,
            bytes_accessed=2 * (total + depth) * feats,
            transcendentals=0,
        ),
        name="pairs",
    )(place, *args)


def shards(showers, geometry, pattern, bins, sources):
    y = lax.axis_index("layer")
    s = lax.axis_index("shower")
    x, z, c = s // (NZ * NC), (s // NC) % NZ, s % NC
    feats = geometry.shape[1]
    blocks = bins.shape[0]

    codes = (bins + BINS * sources + 1).astype(jnp.float32)
    line = lax.broadcasted_iota(jnp.int32, (TAG, feats), 0)
    lane = lax.broadcasted_iota(jnp.int32, (TAG, feats), 1) // PIECE
    which = jnp.where(line == blocks, lane, line)
    tag = jnp.zeros((TAG, feats), jnp.float32)
    for group in range(blocks):
        tag = jnp.where(which == group, codes[group], tag)
    tag = tag.astype(jnp.bfloat16)

    partial_sums = raw_partial(showers, geometry, pattern).reshape(blocks, NY, PIECE, feats)

    def share(turn):
        part = lax.dynamic_index_in_dim(partial_sums, (y + turn) % NY, 1, keepdims=False)
        return part.reshape(BLOCK, feats)

    raw = share(0)
    arrived = [permute(share(turn).astype(jnp.float16), along_y(turn)) for turn in (2, 1, 3)]
    for part in arrived:
        raw = raw + part.astype(jnp.float32)
    scale = lax.rsqrt(jnp.mean(raw * raw, axis=1, keepdims=True) + 1e-05)
    own = jnp.concatenate([tag, (raw * scale).astype(jnp.bfloat16)], axis=0)

    fence = lambda *values: lax.optimization_barrier(values)
    tagged = BLOCK + TAG
    y_way = lambda y, x, z, c: ((y + 1 - 2 * c) % NY, x, z, c)
    own_t = permute(own, swap_core)
    chip = jnp.where(c == 0, jnp.concatenate([own, own_t]), jnp.concatenate([own_t, own]))
    z1 = permute(chip, same_core)
    y1 = permute(chip, y_way)
    x1 = permute(own, swap_x)
    z1, y1, x1 = fence(z1, y1, x1)

    z2 = permute(z1, same_core)
    y2 = permute(jnp.where(c == 0, y1[TAG:tagged], y1[tagged + TAG :]), y_way)
    xa = permute(y1[TAG:tagged], swap_x)
    y1_t = permute(y1, swap_core)
    x1_t = permute(x1, swap_core)
    z1, z2, y2, xa, y1_t, x1_t, y1 = fence(z1, z2, y2, xa, y1_t, x1_t, y1)

    z3 = permute(z2, same_core)
    xb = permute(y1[tagged + TAG :], swap_x)
    head = TAG + PIECE
    odd_rows = jnp.concatenate([own[TAG:head], y1_t[TAG:head], y2[:PIECE], y1[TAG:head]], axis=0)
    at_start = lambda y, x, z, c: z == 0 and c == 0
    odd_at = [
        permute(
            odd_rows,
            lambda y, x, z, c, to=to: (y, to, z, c),
            keep=lambda *a: a[1] == 2 and at_start(*a),
        )
        for to in (1, 0)
    ]
    y2_t = permute(y2, swap_core)
    z2, z3, y2, xb, xa, y2_t, *odd_at = fence(z2, z3, y2, xb, xa, y2_t, *odd_at)

    z4 = permute(jnp.where(c == 0, z3[:tagged], z3[tagged:]), same_core)
    held = [chip, z1, z2, z3, z3, z3, z2, z1]
    piece = permute(
        lax.select_n(z, *[value[:head] for value in held]),
        lambda y, x, z, c: (y, 1, z + 1 - c, c),
        keep=lambda y, x, z, c: x == 2 and (z < 4 if c == 0 else z == 0 or z > 4),
    )
    w2 = permute(y2, swap_x)
    xa_t = permute(xa, swap_core)
    xb_t = permute(xb, swap_core)
    w2_t = permute(w2, swap_core)
    odd_rows = odd_at[0] + odd_at[1]
    odd_rows = odd_rows + permute(
        odd_rows, swap_core, keep=lambda *a: a[1] < 2 and at_start(*a)
    )

    col_args = [own, z1, z2, z3, z4, piece]
    col_cuts = [(0, TAG, BLOCK)]
    for arg in (1, 2, 3):
        col_cuts += [(arg, TAG, BLOCK), (arg, tagged + TAG, BLOCK)]
    col_cuts += [(4, TAG, BLOCK), (5, TAG, PIECE)]
    row_args = [own, own_t, x1, x1_t, y1, y1_t, y2, y2_t]
    row_args += [xa, xb, xa_t, xb_t, w2, w2_t, odd_rows]
    tag_cuts = [(6, 0), (8, 0), (7, 0), (9, 0)]
    place = jnp.stack([((x < 2) & (z == 0)).astype(jnp.int32), c.astype(jnp.int32)])
    near, far, theirs, odd_stats = pair_sums(place, col_args, row_args, col_cuts, tag_cuts)

    theirs = permute(theirs, swap_core)
    kept = near + theirs[:, :CHUNK] + permute(far + theirs[:, CHUNK : 2 * CHUNK], swap_x)
    odd_stats = odd_stats + theirs[:, 2 * CHUNK :]
    odd_total = jnp.zeros_like(odd_stats)
    for start in (0, 1):
        odd_total = odd_total + permute(
            odd_stats,
            lambda y, x, z, c: (y, 2, z, c),
            keep=lambda *a, start=start: a[1] == start and at_start(*a),
        )
    odd_total = odd_total.reshape(4, NY, PIECE)
    kept = kept.reshape(4, NY, BLOCK) + jnp.pad(odd_total, ((0, 0), (0, 0), (0, BLOCK - PIECE)))
    total = kept
    for turn in (1, 2):
        total = total + jnp.roll(permute(total, along_y(turn)), -turn, axis=1)
    weight = 1.0 / (PIECE * 32.0**3)
    proof = (total[0] / total[2] - total[1] / total[3]) * weight
    proof = jnp.concatenate([proof, proof], axis=0)
    proof = lax.dynamic_slice_in_dim(proof, (NY - y) % NY, NY, 0).reshape(NY, blocks, PIECE)
    return jnp.transpose(proof, (1, 0, 2)).reshape(-1)


def solution(mesh):
    placed = (P("shower", "layer"), P("layer", None), P("layer", None), P("shower"), P("shower"))
    return jax.shard_map(shards, mesh=mesh, in_specs=placed, out_specs=P("shower"), check_vma=False)
```

```python
import functools

import jax
import jax.numpy as jnp
from jax import lax
from jax.experimental import pallas as pl
from jax.experimental.pallas import tpu as pltpu
from jax.sharding import PartitionSpec as P

BLOCK = 128
PIECE = 32
TAG = 16
BINS = 8
CHUNK = 512
EARLY = 7
AXES = ("layer", "shower")
NY, NX, NZ, NC = 4, 4, 8, 2


def flat(y, x, z, c):
    return y * (NX * NZ * NC) + (x * NZ + z) * NC + c


def permute(value, move, keep=lambda y, x, z, c: True):
    pairs = [
        (flat(y, x, z, c), flat(*move(y, x, z, c)))
        for y in range(NY)
        for x in range(NX)
        for z in range(NZ)
        for c in range(NC)
        if keep(y, x, z, c)
    ]
    return lax.ppermute(value, AXES, pairs)


def along_y(step):
    return lambda y, x, z, c: ((y + step) % NY, x, z, c)


def along_z(step):
    return lambda y, x, z, c: (y, x, (z + step) % NZ, c)


def flip_z(bit):
    return lambda y, x, z, c: (y, x, z ^ bit, c)


def swap_x(y, x, z, c):
    return (y, x ^ 1, z, c)


def swap_core(y, x, z, c):
    return (y, x, z, 1 - c)


def same_core(y, x, z, c):
    return (y, x, (z + 1 - 2 * c) % NZ, c)


def cross_core(y, x, z, c):
    return (y, x, (z - 1 + 2 * c) % NZ, 1 - c)


def raw_kernel(pattern, showers, geometry, out, masked):
    step = pl.program_id(0)
    layers = pattern.shape[1]
    cells = geometry.shape[0] // layers
    per = geometry.shape[1] // BLOCK
    for layer in range(layers):
        for part in range(per):
            rows = pl.ds(layer * cells, cells)
            cols = pl.ds(part * BLOCK, BLOCK)
            on = pattern[step * per + part, layer].astype(jnp.float32).astype(jnp.bfloat16)
            masked[rows, cols] = geometry[rows, cols] * on
    out[...] = lax.dot_general(
        showers[...], masked[...], (((0,), (0,)), ((), ())), preferred_element_type=jnp.float32
    )


def raw_partial(showers, geometry, pattern):
    rows, depth = showers.shape
    feats = geometry.shape[1]
    width = 512
    return pl.pallas_call(
        raw_kernel,
        grid=(feats // width,),
        in_specs=[
            pl.BlockSpec(memory_space=pltpu.SMEM),
            pl.BlockSpec((depth, rows), lambda i: (0, 0)),
            pl.BlockSpec((depth, width), lambda i: (0, i)),
        ],
        out_specs=pl.BlockSpec((rows, width), lambda i: (0, i)),
        out_shape=jax.ShapeDtypeStruct((rows, feats), jnp.float32),
        scratch_shapes=[pltpu.VMEM((depth, width), jnp.bfloat16)],
        compiler_params=pltpu.CompilerParams(vmem_limit_bytes=60 * 2**20),
        cost_estimate=pl.CostEstimate(
            flops=2 * rows * depth * feats, bytes_accessed=8 * 2**20, transcendentals=0
        ),
        name="raw",
    )(pattern.T, showers.T, geometry)


NAMES = ("own", "own_t", "y1", "y1_t", "y2", "y2_t", "x1", "x1_t", "xa", "xb", "xa_t", "xb_t", "w2", "w2_t", "odd")
TAG_OF = ("own", "x1", "own_t", "x1_t", "own")


def pair_kernel(*refs, col_cuts, n_cols_args, late):
    n_cols = len(col_cuts)
    names = NAMES if late else NAMES[:6]
    place, refs = refs[0], refs[1:]
    before, refs = refs[: 2 * late], refs[2 * late :]
    col_args, refs = refs[:n_cols_args], refs[n_cols_args:]
    held, refs = dict(zip(names, refs)), refs[len(names) :]
    outs, refs = refs[: 4 if late else 2], refs[4 if late else 2 :]
    rows_at, cols_at, row_tags, col_tags, row_sems, col_sems, tag_sems = refs
    odd_here, core = place[0], place[1]
    tagged = BLOCK + TAG

    def start(source, first, size, target, at, sem):
        copy = pltpu.make_async_copy(
            source.at[pl.ds(first, size), :], target.at[pl.ds(at, size), :], sem
        )
        copy.start()
        return copy

    starts = [sum(size for _, _, size in col_cuts[:at]) for at in range(n_cols)]
    depth = sum(size for _, _, size in col_cuts)
    loads = []
    for at, (arg, first, size) in enumerate(col_cuts):
        source = col_args[arg]
        loads.append(
            [
                start(source, first, size, cols_at, starts[at], col_sems.at[at]),
                start(source, first - TAG, TAG, col_tags, at * TAG, tag_sems.at[at]),
            ]
        )
    chunks = (0, 2, 1, 3, 4) if late else (0, 2)
    tags = {
        chunk: start(
            held[TAG_OF[chunk]], 0, TAG, row_tags, chunk * TAG, tag_sems.at[n_cols + chunk]
        )
        for chunk in chunks
    }
    turn = jnp.where(core == 0, 3, 1)
    side = [2 * CHUNK * jnp.where(core == b, 0, 1) for b in range(NC)]
    made = []

    def rows(name, first, at):
        at = at if isinstance(at, int) else pl.multiple_of(at, BLOCK)
        made.append(start(held[name], first, BLOCK, rows_at, at, row_sems.at[len(made)]))

    rows("own", TAG, 0)
    rows("y2", 0, 2 * BLOCK)
    for b in range(NC):
        rows("y1", TAG + b * tagged, side[b] + turn * BLOCK)
        rows("y1_t", TAG + b * tagged, side[b] + (NY - turn) * BLOCK)
    n_near = len(made)
    rows("own_t", TAG, 2 * CHUNK)
    rows("y2_t", 0, 2 * CHUNK + 2 * BLOCK)
    n_far = len(made)
    if late:
        rows("x1", TAG, CHUNK)
        rows("w2", 0, CHUNK + 2 * BLOCK)
        for b in range(NC):
            rows(("xa", "xb")[b], 0, CHUNK + side[b] + turn * BLOCK)
            rows(("xa_t", "xb_t")[b], 0, CHUNK + side[b] + (NY - turn) * BLOCK)
        rows("x1_t", TAG, 3 * CHUNK)
        rows("w2_t", 0, 3 * CHUNK + 2 * BLOCK)
        rows("odd", 0, 4 * CHUNK)
    waited = set()

    def bin_of(code):
        source = (code >= BINS).astype(jnp.float32)
        return code - BINS * source, source

    for chunk in chunks:
        tags[chunk].wait()
        for copy in {0: made[:n_near], 2: made[n_near:n_far], 1: made[n_far:]}.get(chunk, []):
            copy.wait()
        first = chunk * CHUNK
        odd = chunk == 4
        size = BLOCK if odd else CHUNK
        tag = row_tags[pl.ds(chunk * TAG + 4, 1), pl.ds(0, BLOCK)].astype(jnp.float32) - 1.0
        bins, _ = bin_of(tag)
        if odd:
            bins = jnp.where(odd_here > 0, bins, -2.0)
        bins = jnp.concatenate([bins] * (size // BLOCK), axis=1)
        one = jnp.zeros((8, size), jnp.float32)
        zero = jnp.zeros((8, size), jnp.float32)
        n_one = jnp.zeros((1, size), jnp.float32)
        n_zero = jnp.zeros((1, size), jnp.float32)
        low = EARLY * BLOCK if late and chunk in (0, 2) else 0
        while low < depth:
            high = depth if depth - low < 3 * BLOCK else low + 2 * BLOCK
            for at in range(n_cols):
                if low <= starts[at] < high and at not in waited:
                    waited.add(at)
                    for copy in loads[at]:
                        copy.wait()
            products = lax.dot_general(
                cols_at[pl.ds(low, high - low), :],
                rows_at[pl.ds(first, size), :],
                (((1,), (1,)), ((), ())),
                preferred_element_type=jnp.float32,
            )
            shifted = products + 32.0
            cubes = shifted * shifted * shifted
            for group in range(low // PIECE, high // PIECE):
                at = group * PIECE // BLOCK
                if odd and col_cuts[at][2] == PIECE:
                    continue
                block = cubes[group * PIECE - low : (group + 1) * PIECE - low]
                if first == 0 and at == 0:
                    lane = lax.broadcasted_iota(jnp.int32, block.shape, 1)
                    sub = lax.broadcasted_iota(jnp.int32, block.shape, 0)
                    block = jnp.where(lane == sub + group * PIECE, 0.0, block)
                part = (block[0:8] + block[8:16]) + (block[16:24] + block[24:32])
                row = at * TAG + group % 4
                code = col_tags[pl.ds(row, 1), pl.ds(0, size)].astype(jnp.float32) - 1.0
                bin_id, source = bin_of(code)
                match = (bins == bin_id).astype(jnp.float32)
                is_one = match * source
                is_zero = match - is_one
                one += is_one * part
                zero += is_zero * part
                n_one += is_one
                n_zero += is_zero
            low = high
        one = jnp.sum(one, axis=0, keepdims=True)
        zero = jnp.sum(zero, axis=0, keepdims=True)
        if late:
            targets = {0: [(outs[0], 0)], 1: [(outs[1], 0)], 2: [(outs[2], 0)]}
            targets |= {3: [(outs[2], CHUNK)], 4: [(outs[2], 2 * CHUNK), (outs[3], 0)]}
            earlier = {0: before[0], 2: before[1]}.get(chunk)
        else:
            targets, earlier = {0: [(outs[0], 0)], 2: [(outs[1], 0)]}, None
        values = [one, zero, n_one, n_zero]
        if earlier is not None:
            values = [earlier[i : i + 1, :] + value for i, value in enumerate(values)]
        for out, place_at in targets[chunk]:
            for i, value in enumerate(values):
                out[i : i + 1, pl.ds(place_at, size)] = value


def pair_sums(place, col_args, row_args, col_cuts, before):
    late = before is not None
    total = 4 * CHUNK + BLOCK if late else 3 * CHUNK
    used, depth = (5 if late else 2) * CHUNK, sum(size for _, _, size in col_cuts)
    feats = col_args[0].shape[1]
    hbm = pl.BlockSpec(memory_space=pl.ANY)
    vmem = pl.BlockSpec(memory_space=pltpu.VMEM)
    dma = pltpu.SemaphoreType.DMA
    widths = [CHUNK, CHUNK, 2 * CHUNK + BLOCK, BLOCK] if late else [CHUNK, CHUNK]
    names = NAMES if late else NAMES[:6]
    before = list(before or [])
    return pl.pallas_call(
        functools.partial(
            pair_kernel, col_cuts=tuple(col_cuts), n_cols_args=len(col_args), late=late
        ),
        in_specs=[pl.BlockSpec(memory_space=pltpu.SMEM)]
        + [vmem] * len(before)
        + [hbm] * (len(col_args) + len(names)),
        out_specs=[vmem] * len(widths),
        out_shape=[jax.ShapeDtypeStruct((4, width), jnp.float32) for width in widths],
        scratch_shapes=[
            pltpu.VMEM((total, feats), jnp.bfloat16),
            pltpu.VMEM((depth, feats), jnp.bfloat16),
            pltpu.VMEM((TAG * 5, feats), jnp.bfloat16),
            pltpu.VMEM((TAG * len(col_cuts), feats), jnp.bfloat16),
            dma((17,)),
            dma((len(col_cuts),)),
            dma((len(col_cuts) + 5,)),
        ],
        compiler_params=pltpu.CompilerParams(vmem_limit_bytes=58 * 2**20),
        cost_estimate=pl.CostEstimate(
            flops=6 * used * depth * feats,
            bytes_accessed=6 * (used + depth) * feats,
            transcendentals=0,
        ),
        name="late" if late else "early",
    )(place, *before, *col_args, *[row_args[name] for name in names])


def shards(showers, geometry, pattern, bins, sources):
    y = lax.axis_index("layer")
    s = lax.axis_index("shower")
    x, z, c = s // (NZ * NC), (s // NC) % NZ, s % NC
    feats = geometry.shape[1]
    blocks = bins.shape[0]

    codes = (bins + BINS * sources + 1).astype(jnp.float32)
    line = lax.broadcasted_iota(jnp.int32, (TAG, feats), 0)
    lane = lax.broadcasted_iota(jnp.int32, (TAG, feats), 1) // PIECE
    which = jnp.where(line == blocks, lane, line)
    tag = jnp.zeros((TAG, feats), jnp.float32)
    for group in range(blocks):
        tag = jnp.where(which == group, codes[group], tag)
    tag = tag.astype(jnp.bfloat16)

    partial_sums = raw_partial(showers, geometry, pattern).reshape(blocks, NY, PIECE, feats)

    def share(turn):
        part = lax.dynamic_index_in_dim(partial_sums, (y + turn) % NY, 1, keepdims=False)
        return part.reshape(BLOCK, feats)

    raw = share(0)
    arrived = [permute(share(turn).astype(jnp.float16), along_y(turn)) for turn in (2, 1, 3)]
    for part in arrived:
        raw = raw + part.astype(jnp.float32)
    scale = lax.rsqrt(jnp.mean(raw * raw, axis=1, keepdims=True) + 1e-05)
    own = jnp.concatenate([tag, (raw * scale).astype(jnp.bfloat16)], axis=0)

    fence = lambda *values: lax.optimization_barrier(values)
    tagged = BLOCK + TAG
    y_way = lambda y, x, z, c: ((y + 1 - 2 * c) % NY, x, z, c)
    own_t = permute(own, swap_core)
    chip = jnp.where(c == 0, jnp.concatenate([own, own_t]), jnp.concatenate([own_t, own]))
    z1 = permute(chip, same_core)
    y1 = permute(chip, y_way)
    x1 = permute(own, swap_x)
    z1, y1, x1 = fence(z1, y1, x1)

    z2 = permute(z1, same_core)
    y2 = permute(jnp.where(c == 0, y1[TAG:tagged], y1[tagged + TAG :]), y_way)
    xa = permute(y1[TAG:tagged], swap_x)
    y1_t = permute(y1, swap_core)
    x1_t = permute(x1, swap_core)
    z1, z2, y2, xa, y1_t, x1_t, y1 = fence(z1, z2, y2, xa, y1_t, x1_t, y1)

    z3 = permute(z2, same_core)
    xb = permute(y1[tagged + TAG :], swap_x)
    head = TAG + PIECE
    odd_rows = jnp.concatenate([own[TAG:head], y1_t[TAG:head], y2[:PIECE], y1[TAG:head]], axis=0)
    at_start = lambda y, x, z, c: z == 0 and c == 0
    odd_at = [
        permute(
            odd_rows,
            lambda y, x, z, c, to=to: (y, to, z, c),
            keep=lambda *a: a[1] == 2 and at_start(*a),
        )
        for to in (1, 0)
    ]
    y2_t = permute(y2, swap_core)
    xa_t = permute(xa, swap_core)
    z2, z3, y2, xb, xa_t, y2_t, *odd_at = fence(z2, z3, y2, xb, xa_t, y2_t, *odd_at)

    z4 = permute(jnp.where(c == 0, z3[:tagged], z3[tagged:]), same_core)
    held = [chip, z1, z2, z3, z3, z3, z2, z1]
    piece = permute(
        lax.select_n(z, *[value[:head] for value in held]),
        lambda y, x, z, c: (y, 1, z + 1 - c, c),
        keep=lambda y, x, z, c: x == 2 and (z < 4 if c == 0 else z == 0 or z > 4),
    )
    w2 = permute(y2, swap_x)
    xb_t = permute(xb, swap_core)
    col_args = [own, z1, z2, z3]
    col_cuts = [(0, TAG, BLOCK)]
    for arg in (1, 2, 3):
        col_cuts += [(arg, TAG, BLOCK), (arg, tagged + TAG, BLOCK)]
    row_args = dict(own=own, own_t=own_t, y1=y1, y1_t=y1_t, y2=y2, y2_t=y2_t)
    place = jnp.stack([((x < 2) & (z == 0)).astype(jnp.int32), c.astype(jnp.int32)])
    early = pair_sums(place, col_args, row_args, col_cuts, None)
    w2, odd_at[0], odd_at[1], early, piece = fence(w2, odd_at[0], odd_at[1], early, piece)
    w2_t = permute(w2, swap_core)
    odd_rows = odd_at[0] + odd_at[1]
    odd_rows = odd_rows + permute(
        odd_rows, swap_core, keep=lambda *a: a[1] < 2 and at_start(*a)
    )
    row_args |= dict(x1=x1, x1_t=x1_t, xa=xa, xb=xb, xa_t=xa_t, xb_t=xb_t, w2=w2, w2_t=w2_t)
    row_args["odd"] = odd_rows
    col_cuts += [(4, TAG, BLOCK), (5, TAG, PIECE)]
    near, far, theirs, odd_stats = pair_sums(
        place, col_args + [z4, piece], row_args, col_cuts, early
    )

    theirs = permute(theirs, swap_core)
    kept = near + theirs[:, :CHUNK] + permute(far + theirs[:, CHUNK : 2 * CHUNK], swap_x)
    odd_stats = odd_stats + theirs[:, 2 * CHUNK :]
    odd_total = jnp.zeros_like(odd_stats)
    for start in (0, 1):
        odd_total = odd_total + permute(
            odd_stats,
            lambda y, x, z, c: (y, 2, z, c),
            keep=lambda *a, start=start: a[1] == start and at_start(*a),
        )
    odd_total = odd_total.reshape(4, NY, PIECE)
    kept = kept.reshape(4, NY, BLOCK) + jnp.pad(odd_total, ((0, 0), (0, 0), (0, BLOCK - PIECE)))
    total = kept
    for turn in (2, 1, 3):
        total = total + jnp.roll(permute(kept, along_y(turn)), -turn, axis=1)
    weight = 1.0 / (PIECE * 32.0**3)
    proof = (total[0] / total[2] - total[1] / total[3]) * weight
    proof = jnp.concatenate([proof, proof], axis=0)
    proof = lax.dynamic_slice_in_dim(proof, (NY - y) % NY, NY, 0).reshape(NY, blocks, PIECE)
    return jnp.transpose(proof, (1, 0, 2)).reshape(-1)


def solution(mesh):
    placed = (P("shower", "layer"), P("layer", None), P("layer", None), P("shower"), P("shower"))
    return jax.shard_map(shards, mesh=mesh, in_specs=placed, out_specs=P("shower"), check_vma=False)
```

```python
import functools

import jax
import jax.numpy as jnp
from jax import lax
from jax.experimental import pallas as pl
from jax.experimental.pallas import tpu as pltpu
from jax.sharding import PartitionSpec as P

BLOCK = 128
PIECE = 32
TAG = 16
BINS = 8
CHUNK = 512
EARLY = 7
AXES = ("layer", "shower")
NY, NX, NZ, NC = 4, 4, 8, 2


def flat(y, x, z, c):
    return y * (NX * NZ * NC) + (x * NZ + z) * NC + c


def permute(value, move, keep=lambda y, x, z, c: True):
    pairs = [
        (flat(y, x, z, c), flat(*move(y, x, z, c)))
        for y in range(NY)
        for x in range(NX)
        for z in range(NZ)
        for c in range(NC)
        if keep(y, x, z, c)
    ]
    return lax.ppermute(value, AXES, pairs)


def along_y(step):
    return lambda y, x, z, c: ((y + step) % NY, x, z, c)


def along_z(step):
    return lambda y, x, z, c: (y, x, (z + step) % NZ, c)


def flip_z(bit):
    return lambda y, x, z, c: (y, x, z ^ bit, c)


def swap_x(y, x, z, c):
    return (y, x ^ 1, z, c)


def swap_core(y, x, z, c):
    return (y, x, z, 1 - c)


def same_core(y, x, z, c):
    return (y, x, (z + 1 - 2 * c) % NZ, c)


def cross_core(y, x, z, c):
    return (y, x, (z - 1 + 2 * c) % NZ, 1 - c)


def raw_kernel(pattern, showers, geometry, out, masked):
    step = pl.program_id(0)
    layers = pattern.shape[1]
    cells = geometry.shape[0] // layers
    per = geometry.shape[1] // BLOCK
    for layer in range(layers):
        for part in range(per):
            rows = pl.ds(layer * cells, cells)
            cols = pl.ds(part * BLOCK, BLOCK)
            on = pattern[step * per + part, layer].astype(jnp.float32).astype(jnp.bfloat16)
            masked[rows, cols] = geometry[rows, cols] * on
    out[...] = lax.dot_general(
        showers[...], masked[...], (((0,), (0,)), ((), ())), preferred_element_type=jnp.float32
    )


def raw_partial(showers, geometry, pattern):
    rows, depth = showers.shape
    feats = geometry.shape[1]
    width = 512
    return pl.pallas_call(
        raw_kernel,
        grid=(feats // width,),
        in_specs=[
            pl.BlockSpec(memory_space=pltpu.SMEM),
            pl.BlockSpec((depth, rows), lambda i: (0, 0)),
            pl.BlockSpec((depth, width), lambda i: (0, i)),
        ],
        out_specs=pl.BlockSpec((rows, width), lambda i: (0, i)),
        out_shape=jax.ShapeDtypeStruct((rows, feats), jnp.float32),
        scratch_shapes=[pltpu.VMEM((depth, width), jnp.bfloat16)],
        compiler_params=pltpu.CompilerParams(vmem_limit_bytes=60 * 2**20),
        cost_estimate=pl.CostEstimate(
            flops=2 * rows * depth * feats, bytes_accessed=8 * 2**20, transcendentals=0
        ),
        name="raw",
    )(pattern.T, showers.T, geometry)


NAMES = ("own", "own_t", "y1", "y1_t", "y2", "y2_t", "x1", "x1_t", "xa", "xb", "xa_t", "xb_t", "w2", "w2_t", "odd")
TAG_OF = ("own", "x1", "own_t", "x1_t", "own")


def pair_kernel(*refs, col_cuts, n_cols_args, late):
    n_cols = len(col_cuts)
    names = NAMES if late else NAMES[:6]
    place, refs = refs[0], refs[1:]
    before, refs = refs[: 2 * late], refs[2 * late :]
    col_args, refs = refs[:n_cols_args], refs[n_cols_args:]
    held, refs = dict(zip(names, refs)), refs[len(names) :]
    outs, refs = refs[: 4 if late else 2], refs[4 if late else 2 :]
    rows_at, cols_at, row_tags, col_tags, row_sems, col_sems, tag_sems = refs
    odd_here, core = place[0], place[1]
    tagged = BLOCK + TAG

    def start(source, first, size, target, at, sem):
        copy = pltpu.make_async_copy(
            source.at[pl.ds(first, size), :], target.at[pl.ds(at, size), :], sem
        )
        copy.start()
        return copy

    starts = [sum(size for _, _, size in col_cuts[:at]) for at in range(n_cols)]
    depth = sum(size for _, _, size in col_cuts)
    loads = []
    for at, (arg, first, size) in enumerate(col_cuts):
        source = col_args[arg]
        loads.append(
            [
                start(source, first, size, cols_at, starts[at], col_sems.at[at]),
                start(source, first - TAG, TAG, col_tags, at * TAG, tag_sems.at[at]),
            ]
        )
    chunks = (0, 2, 1, 3, 4) if late else (0, 2)
    tags = {
        chunk: start(
            held[TAG_OF[chunk]], 0, TAG, row_tags, chunk * TAG, tag_sems.at[n_cols + chunk]
        )
        for chunk in chunks
    }
    turn = jnp.where(core == 0, 3, 1)
    side = [2 * CHUNK * jnp.where(core == b, 0, 1) for b in range(NC)]
    made = []

    def rows(name, first, at):
        at = at if isinstance(at, int) else pl.multiple_of(at, BLOCK)
        made.append(start(held[name], first, BLOCK, rows_at, at, row_sems.at[len(made)]))

    rows("own", TAG, 0)
    rows("y2", 0, 2 * BLOCK)
    for b in range(NC):
        rows("y1", TAG + b * tagged, side[b] + turn * BLOCK)
        rows("y1_t", TAG + b * tagged, side[b] + (NY - turn) * BLOCK)
    n_near = len(made)
    rows("own_t", TAG, 2 * CHUNK)
    rows("y2_t", 0, 2 * CHUNK + 2 * BLOCK)
    n_far = len(made)
    if late:
        rows("x1", TAG, CHUNK)
        rows("w2", 0, CHUNK + 2 * BLOCK)
        for b in range(NC):
            rows(("xa", "xb")[b], 0, CHUNK + side[b] + turn * BLOCK)
            rows(("xa_t", "xb_t")[b], 0, CHUNK + side[b] + (NY - turn) * BLOCK)
        rows("x1_t", TAG, 3 * CHUNK)
        rows("w2_t", 0, 3 * CHUNK + 2 * BLOCK)
        rows("odd", 0, 4 * CHUNK)
    waited = set()

    def bin_of(code):
        source = (code >= BINS).astype(jnp.float32)
        return code - BINS * source, source

    for chunk in chunks:
        tags[chunk].wait()
        for copy in {0: made[:n_near], 2: made[n_near:n_far], 1: made[n_far:]}.get(chunk, []):
            copy.wait()
        first = chunk * CHUNK
        odd = chunk == 4
        size = BLOCK if odd else CHUNK
        tag = row_tags[pl.ds(chunk * TAG + 4, 1), pl.ds(0, BLOCK)].astype(jnp.float32) - 1.0
        bins, _ = bin_of(tag)
        if odd:
            bins = jnp.where(odd_here > 0, bins, -2.0)
        bins = jnp.concatenate([bins] * (size // BLOCK), axis=1)
        one = jnp.zeros((8, size), jnp.float32)
        zero = jnp.zeros((8, size), jnp.float32)
        n_one = jnp.zeros((1, size), jnp.float32)
        n_zero = jnp.zeros((1, size), jnp.float32)
        low = EARLY * BLOCK if late and chunk in (0, 2) else 0
        while low < depth:
            high = depth if depth - low < 3 * BLOCK else low + 2 * BLOCK
            for at in range(n_cols):
                if low <= starts[at] < high and at not in waited:
                    waited.add(at)
                    for copy in loads[at]:
                        copy.wait()
            products = lax.dot_general(
                cols_at[pl.ds(low, high - low), :],
                rows_at[pl.ds(first, size), :],
                (((1,), (1,)), ((), ())),
                preferred_element_type=jnp.float32,
            )
            shifted = products + 32.0
            cubes = shifted * shifted * shifted
            for group in range(low // PIECE, high // PIECE):
                at = group * PIECE // BLOCK
                if odd and col_cuts[at][2] == PIECE:
                    continue
                block = cubes[group * PIECE - low : (group + 1) * PIECE - low]
                if first == 0 and at == 0:
                    lane = lax.broadcasted_iota(jnp.int32, block.shape, 1)
                    sub = lax.broadcasted_iota(jnp.int32, block.shape, 0)
                    block = jnp.where(lane == sub + group * PIECE, 0.0, block)
                part = (block[0:8] + block[8:16]) + (block[16:24] + block[24:32])
                row = at * TAG + group % 4
                code = col_tags[pl.ds(row, 1), pl.ds(0, size)].astype(jnp.float32) - 1.0
                bin_id, source = bin_of(code)
                match = (bins == bin_id).astype(jnp.float32)
                is_one = match * source
                is_zero = match - is_one
                one += is_one * part
                zero += is_zero * part
                n_one += is_one
                n_zero += is_zero
            low = high
        one = jnp.sum(one, axis=0, keepdims=True)
        zero = jnp.sum(zero, axis=0, keepdims=True)
        if late:
            targets = {0: [(outs[0], 0)], 1: [(outs[1], 0)], 2: [(outs[2], 0)]}
            targets |= {3: [(outs[2], CHUNK)], 4: [(outs[2], 2 * CHUNK), (outs[3], 0)]}
            earlier = {0: before[0], 2: before[1]}.get(chunk)
        else:
            targets, earlier = {0: [(outs[0], 0)], 2: [(outs[1], 0)]}, None
        values = [one, zero, n_one, n_zero]
        if earlier is not None:
            values = [earlier[i : i + 1, :] + value for i, value in enumerate(values)]
        for out, place_at in targets[chunk]:
            for i, value in enumerate(values):
                out[i : i + 1, pl.ds(place_at, size)] = value


def pair_sums(place, col_args, row_args, col_cuts, before):
    late = before is not None
    total = 4 * CHUNK + BLOCK if late else 3 * CHUNK
    used, depth = (5 if late else 2) * CHUNK, sum(size for _, _, size in col_cuts)
    feats = col_args[0].shape[1]
    hbm = pl.BlockSpec(memory_space=pl.ANY)
    vmem = pl.BlockSpec(memory_space=pltpu.VMEM)
    dma = pltpu.SemaphoreType.DMA
    widths = [CHUNK, CHUNK, 2 * CHUNK + BLOCK, BLOCK] if late else [CHUNK, CHUNK]
    names = NAMES if late else NAMES[:6]
    before = list(before or [])
    return pl.pallas_call(
        functools.partial(
            pair_kernel, col_cuts=tuple(col_cuts), n_cols_args=len(col_args), late=late
        ),
        in_specs=[pl.BlockSpec(memory_space=pltpu.SMEM)]
        + [vmem] * len(before)
        + [hbm] * (len(col_args) + len(names)),
        out_specs=[vmem] * len(widths),
        out_shape=[jax.ShapeDtypeStruct((4, width), jnp.float32) for width in widths],
        scratch_shapes=[
            pltpu.VMEM((total, feats), jnp.bfloat16),
            pltpu.VMEM((depth, feats), jnp.bfloat16),
            pltpu.VMEM((TAG * 5, feats), jnp.bfloat16),
            pltpu.VMEM((TAG * len(col_cuts), feats), jnp.bfloat16),
            dma((17,)),
            dma((len(col_cuts),)),
            dma((len(col_cuts) + 5,)),
        ],
        compiler_params=pltpu.CompilerParams(vmem_limit_bytes=18 * 2**20),
        cost_estimate=pl.CostEstimate(
            flops=6 * used * depth * feats,
            bytes_accessed=6 * (used + depth) * feats,
            transcendentals=0,
        ),
        name="late" if late else "early",
    )(place, *before, *col_args, *[row_args[name] for name in names])


def shards(showers, geometry, pattern, bins, sources):
    y = lax.axis_index("layer")
    s = lax.axis_index("shower")
    x, z, c = s // (NZ * NC), (s // NC) % NZ, s % NC
    feats = geometry.shape[1]
    blocks = bins.shape[0]

    codes = (bins + BINS * sources + 1).astype(jnp.float32)
    line = lax.broadcasted_iota(jnp.int32, (TAG, feats), 0)
    lane = lax.broadcasted_iota(jnp.int32, (TAG, feats), 1) // PIECE
    which = jnp.where(line == blocks, lane, line)
    tag = jnp.zeros((TAG, feats), jnp.float32)
    for group in range(blocks):
        tag = jnp.where(which == group, codes[group], tag)
    tag = tag.astype(jnp.bfloat16)

    partial_sums = raw_partial(showers, geometry, pattern).reshape(blocks, NY, PIECE, feats)

    def share(turn):
        part = lax.dynamic_index_in_dim(partial_sums, (y + turn) % NY, 1, keepdims=False)
        return part.reshape(BLOCK, feats)

    raw = share(0)
    arrived = [permute(share(turn).astype(jnp.float16), along_y(turn)) for turn in (2, 1, 3)]
    for part in arrived:
        raw = raw + part.astype(jnp.float32)
    scale = lax.rsqrt(jnp.mean(raw * raw, axis=1, keepdims=True) + 1e-05)
    own = jnp.concatenate([tag, (raw * scale).astype(jnp.bfloat16)], axis=0)

    fence = lambda *values: lax.optimization_barrier(values)
    tagged = BLOCK + TAG
    y_way = lambda y, x, z, c: ((y + 1 - 2 * c) % NY, x, z, c)
    own_t = permute(own, swap_core)
    chip = jnp.where(c == 0, jnp.concatenate([own, own_t]), jnp.concatenate([own_t, own]))
    z1 = permute(chip, same_core)
    y1 = permute(chip, y_way)
    x1 = permute(own, swap_x)
    z1, y1, x1 = fence(z1, y1, x1)

    z2 = permute(z1, same_core)
    y2 = permute(jnp.where(c == 0, y1[TAG:tagged], y1[tagged + TAG :]), y_way)
    xa = permute(y1[TAG:tagged], swap_x)
    y1_t = permute(y1, swap_core)
    x1_t = permute(x1, swap_core)
    z1, z2, y2, xa, y1_t, x1_t, y1 = fence(z1, z2, y2, xa, y1_t, x1_t, y1)

    z3 = permute(z2, same_core)
    xb = permute(y1[tagged + TAG :], swap_x)
    head = TAG + PIECE
    odd_rows = jnp.concatenate([own[TAG:head], y1_t[TAG:head], y2[:PIECE], y1[TAG:head]], axis=0)
    at_start = lambda y, x, z, c: z == 0 and c == 0
    odd_at = [
        permute(
            odd_rows,
            lambda y, x, z, c, to=to: (y, to, z, c),
            keep=lambda *a: a[1] == 2 and at_start(*a),
        )
        for to in (1, 0)
    ]
    y2_t = permute(y2, swap_core)
    xa_t = permute(xa, swap_core)
    z2, z3, y2, xb, xa_t, y2_t, *odd_at = fence(z2, z3, y2, xb, xa_t, y2_t, *odd_at)

    z4 = permute(jnp.where(c == 0, z3[:tagged], z3[tagged:]), same_core)
    held = [chip, z1, z2, z3, z3, z3, z2, z1]
    piece = permute(
        lax.select_n(z, *[value[:head] for value in held]),
        lambda y, x, z, c: (y, 1, z + 1 - c, c),
        keep=lambda y, x, z, c: x == 2 and (z < 4 if c == 0 else z == 0 or z > 4),
    )
    w2 = permute(y2, swap_x)
    xb_t = permute(xb, swap_core)
    col_args = [own, z1, z2, z3]
    col_cuts = [(0, TAG, BLOCK)]
    for arg in (1, 2, 3):
        col_cuts += [(arg, TAG, BLOCK), (arg, tagged + TAG, BLOCK)]
    row_args = dict(own=own, own_t=own_t, y1=y1, y1_t=y1_t, y2=y2, y2_t=y2_t)
    place = jnp.stack([((x < 2) & (z == 0)).astype(jnp.int32), c.astype(jnp.int32)])
    early = pair_sums(place, col_args, row_args, col_cuts, None)
    w2, odd_at[0], odd_at[1], early, piece = fence(w2, odd_at[0], odd_at[1], early, piece)
    w2_t = permute(w2, swap_core)
    odd_rows = odd_at[0] + odd_at[1]
    odd_rows = odd_rows + permute(
        odd_rows, swap_core, keep=lambda *a: a[1] < 2 and at_start(*a)
    )
    row_args |= dict(x1=x1, x1_t=x1_t, xa=xa, xb=xb, xa_t=xa_t, xb_t=xb_t, w2=w2, w2_t=w2_t)
    row_args["odd"] = odd_rows
    col_cuts += [(4, TAG, BLOCK), (5, TAG, PIECE)]
    near, far, theirs, odd_stats = pair_sums(
        place, col_args + [z4, piece], row_args, col_cuts, early
    )

    theirs = permute(theirs, swap_core)
    kept = near + theirs[:, :CHUNK] + permute(far + theirs[:, CHUNK : 2 * CHUNK], swap_x)
    odd_stats = odd_stats + theirs[:, 2 * CHUNK :]
    odd_total = jnp.zeros_like(odd_stats)
    for start in (0, 1):
        odd_total = odd_total + permute(
            odd_stats,
            lambda y, x, z, c: (y, 2, z, c),
            keep=lambda *a, start=start: a[1] == start and at_start(*a),
        )
    odd_total = odd_total.reshape(4, NY, PIECE)
    kept = kept.reshape(4, NY, BLOCK) + jnp.pad(odd_total, ((0, 0), (0, 0), (0, BLOCK - PIECE)))
    total = kept
    for turn in (2, 1, 3):
        total = total + jnp.roll(permute(kept, along_y(turn)), -turn, axis=1)
    weight = 1.0 / (PIECE * 32.0**3)
    proof = (total[0] / total[2] - total[1] / total[3]) * weight
    proof = jnp.concatenate([proof, proof], axis=0)
    proof = lax.dynamic_slice_in_dim(proof, (NY - y) % NY, NY, 0).reshape(NY, blocks, PIECE)
    return jnp.transpose(proof, (1, 0, 2)).reshape(-1)


def solution(mesh):
    placed = (P("shower", "layer"), P("layer", None), P("layer", None), P("shower"), P("shower"))
    return jax.shard_map(shards, mesh=mesh, in_specs=placed, out_specs=P("shower"), check_vma=False)
```

```python
import functools

import jax
import jax.numpy as jnp
from jax import lax
from jax.experimental import pallas as pl
from jax.experimental.pallas import tpu as pltpu
from jax.sharding import PartitionSpec as P

BLOCK = 128
PIECE = 32
TAG = 16
BINS = 8
CHUNK = 512
EARLY = 7
AXES = ("layer", "shower")
NY, NX, NZ, NC = 4, 4, 8, 2


def flat(y, x, z, c):
    return y * (NX * NZ * NC) + (x * NZ + z) * NC + c


def permute(value, move, keep=lambda y, x, z, c: True):
    pairs = [
        (flat(y, x, z, c), flat(*move(y, x, z, c)))
        for y in range(NY)
        for x in range(NX)
        for z in range(NZ)
        for c in range(NC)
        if keep(y, x, z, c)
    ]
    return lax.ppermute(value, AXES, pairs)


def along_y(step):
    return lambda y, x, z, c: ((y + step) % NY, x, z, c)


def along_z(step):
    return lambda y, x, z, c: (y, x, (z + step) % NZ, c)


def flip_z(bit):
    return lambda y, x, z, c: (y, x, z ^ bit, c)


def swap_x(y, x, z, c):
    return (y, x ^ 1, z, c)


def swap_core(y, x, z, c):
    return (y, x, z, 1 - c)


def same_core(y, x, z, c):
    return (y, x, (z + 1 - 2 * c) % NZ, c)


def cross_core(y, x, z, c):
    return (y, x, (z - 1 + 2 * c) % NZ, 1 - c)


def raw_kernel(pattern, showers, geometry, out, masked):
    step = pl.program_id(0)
    layers = pattern.shape[1]
    cells = geometry.shape[0] // layers
    per = geometry.shape[1] // BLOCK
    for layer in range(layers):
        for part in range(per):
            rows = pl.ds(layer * cells, cells)
            cols = pl.ds(part * BLOCK, BLOCK)
            on = pattern[step * per + part, layer].astype(jnp.float32).astype(jnp.bfloat16)
            masked[rows, cols] = geometry[rows, cols] * on
    out[...] = lax.dot_general(
        showers[...], masked[...], (((0,), (0,)), ((), ())), preferred_element_type=jnp.float32
    )


def raw_partial(showers, geometry, pattern):
    rows, depth = showers.shape
    feats = geometry.shape[1]
    width = 512
    return pl.pallas_call(
        raw_kernel,
        grid=(feats // width,),
        in_specs=[
            pl.BlockSpec(memory_space=pltpu.SMEM),
            pl.BlockSpec((depth, rows), lambda i: (0, 0)),
            pl.BlockSpec((depth, width), lambda i: (0, i)),
        ],
        out_specs=pl.BlockSpec((rows, width), lambda i: (0, i)),
        out_shape=jax.ShapeDtypeStruct((rows, feats), jnp.float32),
        scratch_shapes=[pltpu.VMEM((depth, width), jnp.bfloat16)],
        compiler_params=pltpu.CompilerParams(vmem_limit_bytes=60 * 2**20),
        cost_estimate=pl.CostEstimate(
            flops=2 * rows * depth * feats, bytes_accessed=8 * 2**20, transcendentals=0
        ),
        name="raw",
    )(pattern.T, showers.T, geometry)


NAMES = ("own", "own_t", "y1", "y1_t", "y2", "y2_t", "x1", "x1_t", "xa", "xb", "xa_t", "xb_t", "w2", "w2_t", "odd")
TAG_OF = ("own", "x1", "own_t", "x1_t", "own")


def pair_kernel(*refs, col_cuts, n_cols_args, late):
    n_cols = len(col_cuts)
    names = NAMES if late else NAMES[:6]
    place, refs = refs[0], refs[1:]
    before, refs = refs[: 2 * late], refs[2 * late :]
    col_args, refs = refs[:n_cols_args], refs[n_cols_args:]
    held, refs = dict(zip(names, refs)), refs[len(names) :]
    outs, refs = refs[: 4 if late else 2], refs[4 if late else 2 :]
    rows_at, cols_at = refs
    odd_here, core = place[0], place[1]
    tagged = BLOCK + TAG

    starts = [sum(size for _, _, size in col_cuts[:at]) for at in range(n_cols)]
    depth = sum(size for _, _, size in col_cuts)
    for at, (arg, first, size) in enumerate(col_cuts):
        cols_at[pl.ds(starts[at], size), :] = col_args[arg][pl.ds(first, size), :]
    chunks = (0, 2, 1, 3, 4) if late else (0, 2)
    turn = jnp.where(core == 0, 3, 1)
    side = [2 * CHUNK * jnp.where(core == b, 0, 1) for b in range(NC)]

    def rows(name, first, at):
        at = at if isinstance(at, int) else pl.multiple_of(at, BLOCK)
        rows_at[pl.ds(at, BLOCK), :] = held[name][pl.ds(first, BLOCK), :]

    rows("own", TAG, 0)
    rows("y2", 0, 2 * BLOCK)
    for b in range(NC):
        rows("y1", TAG + b * tagged, side[b] + turn * BLOCK)
        rows("y1_t", TAG + b * tagged, side[b] + (NY - turn) * BLOCK)
    rows("own_t", TAG, 2 * CHUNK)
    rows("y2_t", 0, 2 * CHUNK + 2 * BLOCK)
    if late:
        rows("x1", TAG, CHUNK)
        rows("w2", 0, CHUNK + 2 * BLOCK)
        for b in range(NC):
            rows(("xa", "xb")[b], 0, CHUNK + side[b] + turn * BLOCK)
            rows(("xa_t", "xb_t")[b], 0, CHUNK + side[b] + (NY - turn) * BLOCK)
        rows("x1_t", TAG, 3 * CHUNK)
        rows("w2_t", 0, 3 * CHUNK + 2 * BLOCK)
        rows("odd", 0, 4 * CHUNK)

    def bin_of(code):
        source = (code >= BINS).astype(jnp.float32)
        return code - BINS * source, source

    for chunk in chunks:
        first = chunk * CHUNK
        odd = chunk == 4
        size = BLOCK if odd else CHUNK
        tag = held[TAG_OF[chunk]][4:5, pl.ds(0, BLOCK)].astype(jnp.float32) - 1.0
        bins, _ = bin_of(tag)
        if odd:
            bins = jnp.where(odd_here > 0, bins, -2.0)
        bins = jnp.concatenate([bins] * (size // BLOCK), axis=1)
        one = jnp.zeros((8, size), jnp.float32)
        zero = jnp.zeros((8, size), jnp.float32)
        n_one = jnp.zeros((1, size), jnp.float32)
        n_zero = jnp.zeros((1, size), jnp.float32)
        low = EARLY * BLOCK if late and chunk in (0, 2) else 0
        while low < depth:
            high = depth if depth - low < 3 * BLOCK else low + 2 * BLOCK
            products = lax.dot_general(
                cols_at[pl.ds(low, high - low), :],
                rows_at[pl.ds(first, size), :],
                (((1,), (1,)), ((), ())),
                preferred_element_type=jnp.float32,
            )
            shifted = products + 32.0
            cubes = shifted * shifted * shifted
            for group in range(low // PIECE, high // PIECE):
                at = group * PIECE // BLOCK
                if odd and col_cuts[at][2] == PIECE:
                    continue
                block = cubes[group * PIECE - low : (group + 1) * PIECE - low]
                if first == 0 and at == 0:
                    lane = lax.broadcasted_iota(jnp.int32, block.shape, 1)
                    sub = lax.broadcasted_iota(jnp.int32, block.shape, 0)
                    block = jnp.where(lane == sub + group * PIECE, 0.0, block)
                part = (block[0:8] + block[8:16]) + (block[16:24] + block[24:32])
                arg, place_of, _ = col_cuts[at]
                row = place_of - TAG + group % 4
                code = col_args[arg][pl.ds(row, 1), pl.ds(0, size)].astype(jnp.float32) - 1.0
                bin_id, source = bin_of(code)
                match = (bins == bin_id).astype(jnp.float32)
                is_one = match * source
                is_zero = match - is_one
                one += is_one * part
                zero += is_zero * part
                n_one += is_one
                n_zero += is_zero
            low = high
        one = jnp.sum(one, axis=0, keepdims=True)
        zero = jnp.sum(zero, axis=0, keepdims=True)
        if late:
            targets = {0: [(outs[0], 0)], 1: [(outs[1], 0)], 2: [(outs[2], 0)]}
            targets |= {3: [(outs[2], CHUNK)], 4: [(outs[2], 2 * CHUNK), (outs[3], 0)]}
            earlier = {0: before[0], 2: before[1]}.get(chunk)
        else:
            targets, earlier = {0: [(outs[0], 0)], 2: [(outs[1], 0)]}, None
        values = [one, zero, n_one, n_zero]
        if earlier is not None:
            values = [earlier[i : i + 1, :] + value for i, value in enumerate(values)]
        for out, place_at in targets[chunk]:
            for i, value in enumerate(values):
                out[i : i + 1, pl.ds(place_at, size)] = value


def pair_sums(place, col_args, row_args, col_cuts, before):
    late = before is not None
    total = 4 * CHUNK + BLOCK if late else 3 * CHUNK
    used, depth = (5 if late else 2) * CHUNK, sum(size for _, _, size in col_cuts)
    feats = col_args[0].shape[1]
    vmem = pl.BlockSpec(memory_space=pltpu.VMEM)
    widths = [CHUNK, CHUNK, 2 * CHUNK + BLOCK, BLOCK] if late else [CHUNK, CHUNK]
    names = NAMES if late else NAMES[:6]
    before = list(before or [])
    return pl.pallas_call(
        functools.partial(
            pair_kernel, col_cuts=tuple(col_cuts), n_cols_args=len(col_args), late=late
        ),
        in_specs=[pl.BlockSpec(memory_space=pltpu.SMEM)]
        + [vmem] * (len(before) + len(col_args) + len(names)),
        out_specs=[vmem] * len(widths),
        out_shape=[jax.ShapeDtypeStruct((4, width), jnp.float32) for width in widths],
        scratch_shapes=[
            pltpu.VMEM((total, feats), jnp.bfloat16),
            pltpu.VMEM((depth, feats), jnp.bfloat16),
        ],
        compiler_params=pltpu.CompilerParams(vmem_limit_bytes=18 * 2**20),
        cost_estimate=pl.CostEstimate(
            flops=6 * used * depth * feats,
            bytes_accessed=6 * (used + depth) * feats,
            transcendentals=0,
        ),
        name="late" if late else "early",
    )(place, *before, *col_args, *[row_args[name] for name in names])


def shards(showers, geometry, pattern, bins, sources):
    y = lax.axis_index("layer")
    s = lax.axis_index("shower")
    x, z, c = s // (NZ * NC), (s // NC) % NZ, s % NC
    feats = geometry.shape[1]
    blocks = bins.shape[0]

    codes = (bins + BINS * sources + 1).astype(jnp.float32)
    line = lax.broadcasted_iota(jnp.int32, (TAG, feats), 0)
    lane = lax.broadcasted_iota(jnp.int32, (TAG, feats), 1) // PIECE
    which = jnp.where(line == blocks, lane, line)
    tag = jnp.zeros((TAG, feats), jnp.float32)
    for group in range(blocks):
        tag = jnp.where(which == group, codes[group], tag)
    tag = tag.astype(jnp.bfloat16)

    partial_sums = raw_partial(showers, geometry, pattern).reshape(blocks, NY, PIECE, feats)

    def share(turn):
        part = lax.dynamic_index_in_dim(partial_sums, (y + turn) % NY, 1, keepdims=False)
        return part.reshape(BLOCK, feats)

    raw = share(0)
    arrived = [permute(share(turn).astype(jnp.float16), along_y(turn)) for turn in (2, 1, 3)]
    for part in arrived:
        raw = raw + part.astype(jnp.float32)
    scale = lax.rsqrt(jnp.mean(raw * raw, axis=1, keepdims=True) + 1e-05)
    own = jnp.concatenate([tag, (raw * scale).astype(jnp.bfloat16)], axis=0)

    fence = lambda *values: lax.optimization_barrier(values)
    tagged = BLOCK + TAG
    y_way = lambda y, x, z, c: ((y + 1 - 2 * c) % NY, x, z, c)
    own_t = permute(own, swap_core)
    chip = jnp.where(c == 0, jnp.concatenate([own, own_t]), jnp.concatenate([own_t, own]))
    z1 = permute(chip, same_core)
    y1 = permute(chip, y_way)
    x1 = permute(own, swap_x)
    z1, y1, x1 = fence(z1, y1, x1)

    z2 = permute(z1, same_core)
    y2 = permute(jnp.where(c == 0, y1[TAG:tagged], y1[tagged + TAG :]), y_way)
    xa = permute(y1[TAG:tagged], swap_x)
    y1_t = permute(y1, swap_core)
    x1_t = permute(x1, swap_core)
    z1, z2, y2, xa, y1_t, x1_t, y1 = fence(z1, z2, y2, xa, y1_t, x1_t, y1)

    z3 = permute(z2, same_core)
    xb = permute(y1[tagged + TAG :], swap_x)
    head = TAG + PIECE
    odd_rows = jnp.concatenate([own[TAG:head], y1_t[TAG:head], y2[:PIECE], y1[TAG:head]], axis=0)
    at_start = lambda y, x, z, c: z == 0 and c == 0
    odd_at = [
        permute(
            odd_rows,
            lambda y, x, z, c, to=to: (y, to, z, c),
            keep=lambda *a: a[1] == 2 and at_start(*a),
        )
        for to in (1, 0)
    ]
    y2_t = permute(y2, swap_core)
    xa_t = permute(xa, swap_core)
    z2, z3, y2, xb, xa_t, y2_t, *odd_at = fence(z2, z3, y2, xb, xa_t, y2_t, *odd_at)

    z4 = permute(jnp.where(c == 0, z3[:tagged], z3[tagged:]), same_core)
    held = [chip, z1, z2, z3, z3, z3, z2, z1]
    piece = permute(
        lax.select_n(z, *[value[:head] for value in held]),
        lambda y, x, z, c: (y, 1, z + 1 - c, c),
        keep=lambda y, x, z, c: x == 2 and (z < 4 if c == 0 else z == 0 or z > 4),
    )
    w2 = permute(y2, swap_x)
    xb_t = permute(xb, swap_core)
    col_args = [own, z1, z2, z3]
    col_cuts = [(0, TAG, BLOCK)]
    for arg in (1, 2, 3):
        col_cuts += [(arg, TAG, BLOCK), (arg, tagged + TAG, BLOCK)]
    row_args = dict(own=own, own_t=own_t, y1=y1, y1_t=y1_t, y2=y2, y2_t=y2_t)
    place = jnp.stack([((x < 2) & (z == 0)).astype(jnp.int32), c.astype(jnp.int32)])
    early = pair_sums(place, col_args, row_args, col_cuts, None)
    w2, odd_at[0], odd_at[1], early, piece = fence(w2, odd_at[0], odd_at[1], early, piece)
    w2_t = permute(w2, swap_core)
    odd_rows = odd_at[0] + odd_at[1]
    odd_rows = odd_rows + permute(
        odd_rows, swap_core, keep=lambda *a: a[1] < 2 and at_start(*a)
    )
    row_args |= dict(x1=x1, x1_t=x1_t, xa=xa, xb=xb, xa_t=xa_t, xb_t=xb_t, w2=w2, w2_t=w2_t)
    row_args["odd"] = odd_rows
    col_cuts += [(4, TAG, BLOCK), (5, TAG, PIECE)]
    near, far, theirs, odd_stats = pair_sums(
        place, col_args + [z4, piece], row_args, col_cuts, early
    )

    theirs = permute(theirs, swap_core)
    kept = near + theirs[:, :CHUNK] + permute(far + theirs[:, CHUNK : 2 * CHUNK], swap_x)
    odd_stats = odd_stats + theirs[:, 2 * CHUNK :]
    odd_total = jnp.zeros_like(odd_stats)
    for start in (0, 1):
        odd_total = odd_total + permute(
            odd_stats,
            lambda y, x, z, c: (y, 2, z, c),
            keep=lambda *a, start=start: a[1] == start and at_start(*a),
        )
    odd_total = odd_total.reshape(4, NY, PIECE)
    kept = kept.reshape(4, NY, BLOCK) + jnp.pad(odd_total, ((0, 0), (0, 0), (0, BLOCK - PIECE)))
    total = kept
    for turn in (2, 1, 3):
        total = total + jnp.roll(permute(kept, along_y(turn)), -turn, axis=1)
    weight = 1.0 / (PIECE * 32.0**3)
    proof = (total[0] / total[2] - total[1] / total[3]) * weight
    proof = jnp.concatenate([proof, proof], axis=0)
    proof = lax.dynamic_slice_in_dim(proof, (NY - y) % NY, NY, 0).reshape(NY, blocks, PIECE)
    return jnp.transpose(proof, (1, 0, 2)).reshape(-1)


def solution(mesh):
    placed = (P("shower", "layer"), P("layer", None), P("layer", None), P("shower"), P("shower"))
    return jax.shard_map(shards, mesh=mesh, in_specs=placed, out_specs=P("shower"), check_vma=False)
```

```python
import functools

import jax
import jax.numpy as jnp
from jax import lax
from jax.experimental import pallas as pl
from jax.experimental.pallas import tpu as pltpu
from jax.sharding import PartitionSpec as P

BLOCK = 128
PIECE = 32
TAG = 16
BINS = 8
CHUNK = 512
EARLY = 7
AXES = ("layer", "shower")
NY, NX, NZ, NC = 4, 4, 8, 2


def flat(y, x, z, c):
    return y * (NX * NZ * NC) + (x * NZ + z) * NC + c


def permute(value, move, keep=lambda y, x, z, c: True):
    pairs = [
        (flat(y, x, z, c), flat(*move(y, x, z, c)))
        for y in range(NY)
        for x in range(NX)
        for z in range(NZ)
        for c in range(NC)
        if keep(y, x, z, c)
    ]
    return lax.ppermute(value, AXES, pairs)


def along_y(step):
    return lambda y, x, z, c: ((y + step) % NY, x, z, c)


def along_z(step):
    return lambda y, x, z, c: (y, x, (z + step) % NZ, c)


def flip_z(bit):
    return lambda y, x, z, c: (y, x, z ^ bit, c)


def swap_x(y, x, z, c):
    return (y, x ^ 1, z, c)


def swap_core(y, x, z, c):
    return (y, x, z, 1 - c)


def same_core(y, x, z, c):
    return (y, x, (z + 1 - 2 * c) % NZ, c)


def cross_core(y, x, z, c):
    return (y, x, (z - 1 + 2 * c) % NZ, 1 - c)


def raw_kernel(pattern, showers, geometry, out, masked):
    step = pl.program_id(0)
    layers = pattern.shape[1]
    cells = geometry.shape[0] // layers
    per = geometry.shape[1] // BLOCK
    for layer in range(layers):
        for part in range(per):
            rows = pl.ds(layer * cells, cells)
            cols = pl.ds(part * BLOCK, BLOCK)
            on = pattern[step * per + part, layer].astype(jnp.float32).astype(jnp.bfloat16)
            masked[rows, cols] = geometry[rows, cols] * on
    out[...] = lax.dot_general(
        showers[...], masked[...], (((0,), (0,)), ((), ())), preferred_element_type=jnp.float32
    )


def raw_partial(showers, geometry, pattern):
    rows, depth = showers.shape
    feats = geometry.shape[1]
    width = 512
    return pl.pallas_call(
        raw_kernel,
        grid=(feats // width,),
        in_specs=[
            pl.BlockSpec(memory_space=pltpu.SMEM),
            pl.BlockSpec((depth, rows), lambda i: (0, 0)),
            pl.BlockSpec((depth, width), lambda i: (0, i)),
        ],
        out_specs=pl.BlockSpec((rows, width), lambda i: (0, i)),
        out_shape=jax.ShapeDtypeStruct((rows, feats), jnp.float32),
        scratch_shapes=[pltpu.VMEM((depth, width), jnp.bfloat16)],
        compiler_params=pltpu.CompilerParams(vmem_limit_bytes=60 * 2**20),
        cost_estimate=pl.CostEstimate(
            flops=2 * rows * depth * feats, bytes_accessed=8 * 2**20, transcendentals=0
        ),
        name="raw",
    )(pattern.T, showers.T, geometry)


NAMES = ("own", "own_t", "y1", "y1_t", "y2", "y2_t", "x1", "x1_t", "xa", "xb", "xa_t", "xb_t", "w2", "w2_t", "odd")
TAG_OF = ("own", "x1", "own_t", "x1_t", "own")


def pair_kernel(*refs, col_cuts, n_cols_args, late):
    n_cols = len(col_cuts)
    names = NAMES if late else NAMES[:6]
    place, refs = refs[0], refs[1:]
    before, refs = refs[: 2 * late], refs[2 * late :]
    col_args, refs = refs[:n_cols_args], refs[n_cols_args:]
    held, refs = dict(zip(names, refs)), refs[len(names) :]
    outs, refs = refs[: 4 if late else 2], refs[4 if late else 2 :]
    rows_at, cols_at = refs
    odd_here, core = place[0], place[1]
    tagged = BLOCK + TAG

    starts = [sum(size for _, _, size in col_cuts[:at]) for at in range(n_cols)]
    depth = sum(size for _, _, size in col_cuts)
    for at, (arg, first, size) in enumerate(col_cuts):
        cols_at[pl.ds(starts[at], size), :] = col_args[arg][pl.ds(first, size), :]
    chunks = (0, 2, 1, 3, 4) if late else (0, 2)
    turn = jnp.where(core == 0, 3, 1)
    side = [2 * CHUNK * jnp.where(core == b, 0, 1) for b in range(NC)]

    def rows(name, first, at):
        at = at if isinstance(at, int) else pl.multiple_of(at, BLOCK)
        rows_at[pl.ds(at, BLOCK), :] = held[name][pl.ds(first, BLOCK), :]

    rows("own", TAG, 0)
    rows("y2", 0, 2 * BLOCK)
    for b in range(NC):
        rows("y1", TAG + b * tagged, side[b] + turn * BLOCK)
        rows("y1_t", TAG + b * tagged, side[b] + (NY - turn) * BLOCK)
    rows("own_t", TAG, 2 * CHUNK)
    rows("y2_t", 0, 2 * CHUNK + 2 * BLOCK)
    if late:
        rows("x1", TAG, CHUNK)
        rows("w2", 0, CHUNK + 2 * BLOCK)
        for b in range(NC):
            rows(("xa", "xb")[b], 0, CHUNK + side[b] + turn * BLOCK)
            rows(("xa_t", "xb_t")[b], 0, CHUNK + side[b] + (NY - turn) * BLOCK)
        rows("x1_t", TAG, 3 * CHUNK)
        rows("w2_t", 0, 3 * CHUNK + 2 * BLOCK)
        rows("odd", 0, 4 * CHUNK)

    def bin_of(code):
        source = (code >= BINS).astype(jnp.float32)
        return code - BINS * source, source

    for chunk in chunks:
        first = chunk * CHUNK
        odd = chunk == 4
        size = BLOCK if odd else CHUNK
        tag = held[TAG_OF[chunk]][4:5, pl.ds(0, BLOCK)].astype(jnp.float32) - 1.0
        bins, _ = bin_of(tag)
        if odd:
            bins = jnp.where(odd_here > 0, bins, -2.0)
        bins = jnp.concatenate([bins] * (size // BLOCK), axis=1)
        one = jnp.zeros((8, size), jnp.float32)
        zero = jnp.zeros((8, size), jnp.float32)
        n_one = jnp.zeros((1, size), jnp.float32)
        n_zero = jnp.zeros((1, size), jnp.float32)
        low = EARLY * BLOCK if late and chunk in (0, 2) else 0
        while low < depth:
            high = depth if depth - low < 3 * BLOCK else low + 2 * BLOCK
            products = lax.dot_general(
                cols_at[pl.ds(low, high - low), :],
                rows_at[pl.ds(first, size), :],
                (((1,), (1,)), ((), ())),
                preferred_element_type=jnp.float32,
            )
            shifted = products + 32.0
            cubes = shifted * shifted * shifted
            for group in range(low // PIECE, high // PIECE):
                at = group * PIECE // BLOCK
                if odd and col_cuts[at][2] == PIECE:
                    continue
                block = cubes[group * PIECE - low : (group + 1) * PIECE - low]
                if first == 0 and at == 0:
                    lane = lax.broadcasted_iota(jnp.int32, block.shape, 1)
                    sub = lax.broadcasted_iota(jnp.int32, block.shape, 0)
                    block = jnp.where(lane == sub + group * PIECE, 0.0, block)
                part = (block[0:8] + block[8:16]) + (block[16:24] + block[24:32])
                arg, place_of, _ = col_cuts[at]
                row = place_of - TAG + group % 4
                code = col_args[arg][pl.ds(row, 1), pl.ds(0, size)].astype(jnp.float32) - 1.0
                bin_id, source = bin_of(code)
                match = (bins == bin_id).astype(jnp.float32)
                is_one = match * source
                is_zero = match - is_one
                one += is_one * part
                zero += is_zero * part
                n_one += is_one
                n_zero += is_zero
            low = high
        one = jnp.sum(one, axis=0, keepdims=True)
        zero = jnp.sum(zero, axis=0, keepdims=True)
        if late:
            targets = {0: [(outs[0], 0)], 1: [(outs[1], 0)], 2: [(outs[2], 0)]}
            targets |= {3: [(outs[2], CHUNK)], 4: [(outs[2], 2 * CHUNK), (outs[3], 0)]}
            earlier = {0: before[0], 2: before[1]}.get(chunk)
        else:
            targets, earlier = {0: [(outs[0], 0)], 2: [(outs[1], 0)]}, None
        values = [one, zero, n_one, n_zero]
        if earlier is not None:
            values = [earlier[i : i + 1, :] + value for i, value in enumerate(values)]
        for out, place_at in targets[chunk]:
            for i, value in enumerate(values):
                out[i : i + 1, pl.ds(place_at, size)] = value


def pair_sums(place, col_args, row_args, col_cuts, before):
    late = before is not None
    total = 4 * CHUNK + BLOCK if late else 3 * CHUNK
    used, depth = (5 if late else 2) * CHUNK, sum(size for _, _, size in col_cuts)
    feats = col_args[0].shape[1]
    vmem = pl.BlockSpec(memory_space=pltpu.VMEM)
    widths = [CHUNK, CHUNK, 2 * CHUNK + BLOCK, BLOCK] if late else [CHUNK, CHUNK]
    names = NAMES if late else NAMES[:6]
    before = list(before or [])
    return pl.pallas_call(
        functools.partial(
            pair_kernel, col_cuts=tuple(col_cuts), n_cols_args=len(col_args), late=late
        ),
        in_specs=[pl.BlockSpec(memory_space=pltpu.SMEM)]
        + [vmem] * (len(before) + len(col_args) + len(names)),
        out_specs=[vmem] * len(widths),
        out_shape=[jax.ShapeDtypeStruct((4, width), jnp.float32) for width in widths],
        scratch_shapes=[
            pltpu.VMEM((total, feats), jnp.bfloat16),
            pltpu.VMEM((depth, feats), jnp.bfloat16),
        ],
        compiler_params=pltpu.CompilerParams(vmem_limit_bytes=18 * 2**20),
        cost_estimate=pl.CostEstimate(
            flops=6 * used * depth * feats,
            bytes_accessed=6 * (used + depth) * feats,
            transcendentals=0,
        ),
        name="late" if late else "early",
    )(place, *before, *col_args, *[row_args[name] for name in names])


def shards(showers, geometry, pattern, bins, sources):
    y = lax.axis_index("layer")
    s = lax.axis_index("shower")
    x, z, c = s // (NZ * NC), (s // NC) % NZ, s % NC
    feats = geometry.shape[1]
    blocks = bins.shape[0]

    codes = (bins + BINS * sources + 1).astype(jnp.float32)
    line = lax.broadcasted_iota(jnp.int32, (TAG, feats), 0)
    lane = lax.broadcasted_iota(jnp.int32, (TAG, feats), 1) // PIECE
    which = jnp.where(line == blocks, lane, line)
    tag = jnp.zeros((TAG, feats), jnp.float32)
    for group in range(blocks):
        tag = jnp.where(which == group, codes[group], tag)
    tag = tag.astype(jnp.bfloat16)

    partial_sums = raw_partial(showers, geometry, pattern).reshape(blocks, NY, PIECE, feats)

    def share(turn):
        part = lax.dynamic_index_in_dim(partial_sums, (y + turn) % NY, 1, keepdims=False)
        return part.reshape(BLOCK, feats)

    raw = share(0)
    arrived = [permute(share(turn).astype(jnp.float16), along_y(turn)) for turn in (2, 1, 3)]
    for part in arrived:
        raw = raw + part.astype(jnp.float32)
    scale = lax.rsqrt(jnp.mean(raw * raw, axis=1, keepdims=True) + 1e-05)
    own = jnp.concatenate([tag, (raw * scale).astype(jnp.bfloat16)], axis=0)

    fence = lambda *values: lax.optimization_barrier(values)
    tagged = BLOCK + TAG
    y_way = lambda y, x, z, c: ((y + 1 - 2 * c) % NY, x, z, c)
    own_t = permute(own, swap_core)
    chip = jnp.where(c == 0, jnp.concatenate([own, own_t]), jnp.concatenate([own_t, own]))
    z1 = permute(chip, same_core)
    y1 = permute(chip, y_way)
    x1 = permute(own, swap_x)
    z1, y1, x1 = fence(z1, y1, x1)

    z2 = permute(z1, same_core)
    y2 = permute(jnp.where(c == 0, y1[TAG:tagged], y1[tagged + TAG :]), y_way)
    xa = permute(y1[TAG:tagged], swap_x)
    x1_t = permute(x1, swap_core)
    z1, z2, y2, xa, y1, x1_t = fence(z1, z2, y2, xa, y1, x1_t)

    z3 = permute(z2, same_core)
    xb = permute(y1[tagged + TAG :], swap_x)
    y1_t = permute(y1, swap_core)
    head = TAG + PIECE
    odd_rows = jnp.concatenate([own[TAG:head], y1_t[TAG:head], y2[:PIECE], y1[TAG:head]], axis=0)
    at_start = lambda y, x, z, c: z == 0 and c == 0
    odd_at = [
        permute(
            odd_rows,
            lambda y, x, z, c, to=to: (y, to, z, c),
            keep=lambda *a: a[1] == 2 and at_start(*a),
        )
        for to in (1, 0)
    ]
    y2_t = permute(y2, swap_core)
    xa_t = permute(xa, swap_core)
    z2, z3, y2, xb, y1_t, y2_t, xa_t, odd_at[0] = fence(
        z2, z3, y2, xb, y1_t, y2_t, xa_t, odd_at[0]
    )

    z4 = permute(jnp.where(c == 0, z3[:tagged], z3[tagged:]), same_core)
    held = [chip, z1, z2, z3, z3, z3, z2, z1]
    piece = permute(
        lax.select_n(z, *[value[:head] for value in held]),
        lambda y, x, z, c: (y, 1, z + 1 - c, c),
        keep=lambda y, x, z, c: x == 2 and (z < 4 if c == 0 else z == 0 or z > 4),
    )
    w2 = permute(y2, swap_x)
    xb_t = permute(xb, swap_core)
    col_args = [own, z1, z2, z3]
    col_cuts = [(0, TAG, BLOCK)]
    for arg in (1, 2, 3):
        col_cuts += [(arg, TAG, BLOCK), (arg, tagged + TAG, BLOCK)]
    row_args = dict(own=own, own_t=own_t, y1=y1, y1_t=y1_t, y2=y2, y2_t=y2_t)
    place = jnp.stack([((x < 2) & (z == 0)).astype(jnp.int32), c.astype(jnp.int32)])
    early = pair_sums(place, col_args, row_args, col_cuts, None)
    w2, odd_at[0], odd_at[1], early, piece = fence(w2, odd_at[0], odd_at[1], early, piece)
    w2_t = permute(w2, swap_core)
    odd_rows = odd_at[0] + odd_at[1]
    odd_rows = odd_rows + permute(
        odd_rows, swap_core, keep=lambda *a: a[1] < 2 and at_start(*a)
    )
    row_args |= dict(x1=x1, x1_t=x1_t, xa=xa, xb=xb, xa_t=xa_t, xb_t=xb_t, w2=w2, w2_t=w2_t)
    row_args["odd"] = odd_rows
    col_cuts += [(4, TAG, BLOCK), (5, TAG, PIECE)]
    near, far, theirs, odd_stats = pair_sums(
        place, col_args + [z4, piece], row_args, col_cuts, early
    )

    theirs = permute(theirs, swap_core)
    kept = near + theirs[:, :CHUNK] + permute(far + theirs[:, CHUNK : 2 * CHUNK], swap_x)
    odd_stats = odd_stats + theirs[:, 2 * CHUNK :]
    odd_total = jnp.zeros_like(odd_stats)
    for start in (0, 1):
        odd_total = odd_total + permute(
            odd_stats,
            lambda y, x, z, c: (y, 2, z, c),
            keep=lambda *a, start=start: a[1] == start and at_start(*a),
        )
    odd_total = odd_total.reshape(4, NY, PIECE)
    kept = kept.reshape(4, NY, BLOCK) + jnp.pad(odd_total, ((0, 0), (0, 0), (0, BLOCK - PIECE)))
    total = kept
    for turn in (2, 1, 3):
        total = total + jnp.roll(permute(kept, along_y(turn)), -turn, axis=1)
    weight = 1.0 / (PIECE * 32.0**3)
    proof = (total[0] / total[2] - total[1] / total[3]) * weight
    proof = jnp.concatenate([proof, proof], axis=0)
    proof = lax.dynamic_slice_in_dim(proof, (NY - y) % NY, NY, 0).reshape(NY, blocks, PIECE)
    return jnp.transpose(proof, (1, 0, 2)).reshape(-1)


def solution(mesh):
    placed = (P("shower", "layer"), P("layer", None), P("layer", None), P("shower"), P("shower"))
    return jax.shard_map(shards, mesh=mesh, in_specs=placed, out_specs=P("shower"), check_vma=False)
```

```python
import functools

import jax
import jax.numpy as jnp
from jax import lax
from jax.experimental import pallas as pl
from jax.experimental.pallas import tpu as pltpu
from jax.sharding import PartitionSpec as P

BLOCK = 128
PIECE = 32
TAG = 16
BINS = 8
CHUNK = 512
EARLY = 7
AXES = ("layer", "shower")
NY, NX, NZ, NC = 4, 4, 8, 2


def flat(y, x, z, c):
    return y * (NX * NZ * NC) + (x * NZ + z) * NC + c


def permute(value, move, keep=lambda y, x, z, c: True):
    pairs = [
        (flat(y, x, z, c), flat(*move(y, x, z, c)))
        for y in range(NY)
        for x in range(NX)
        for z in range(NZ)
        for c in range(NC)
        if keep(y, x, z, c)
    ]
    return lax.ppermute(value, AXES, pairs)


def along_y(step):
    return lambda y, x, z, c: ((y + step) % NY, x, z, c)


def along_z(step):
    return lambda y, x, z, c: (y, x, (z + step) % NZ, c)


def flip_z(bit):
    return lambda y, x, z, c: (y, x, z ^ bit, c)


def swap_x(y, x, z, c):
    return (y, x ^ 1, z, c)


def swap_core(y, x, z, c):
    return (y, x, z, 1 - c)


def same_core(y, x, z, c):
    return (y, x, (z + 1 - 2 * c) % NZ, c)


def cross_core(y, x, z, c):
    return (y, x, (z - 1 + 2 * c) % NZ, 1 - c)


def raw_kernel(pattern, showers, geometry, out, masked):
    step = pl.program_id(0)
    layers = pattern.shape[1]
    cells = geometry.shape[0] // layers
    per = geometry.shape[1] // BLOCK
    for layer in range(layers):
        for part in range(per):
            rows = pl.ds(layer * cells, cells)
            cols = pl.ds(part * BLOCK, BLOCK)
            on = pattern[step * per + part, layer].astype(jnp.float32).astype(jnp.bfloat16)
            masked[rows, cols] = geometry[rows, cols] * on
    out[...] = lax.dot_general(
        showers[...], masked[...], (((0,), (0,)), ((), ())), preferred_element_type=jnp.float32
    )


def raw_partial(showers, geometry, pattern):
    rows, depth = showers.shape
    feats = geometry.shape[1]
    width = 512
    return pl.pallas_call(
        raw_kernel,
        grid=(feats // width,),
        in_specs=[
            pl.BlockSpec(memory_space=pltpu.SMEM),
            pl.BlockSpec((depth, rows), lambda i: (0, 0)),
            pl.BlockSpec((depth, width), lambda i: (0, i)),
        ],
        out_specs=pl.BlockSpec((rows, width), lambda i: (0, i)),
        out_shape=jax.ShapeDtypeStruct((rows, feats), jnp.float32),
        scratch_shapes=[pltpu.VMEM((depth, width), jnp.bfloat16)],
        compiler_params=pltpu.CompilerParams(vmem_limit_bytes=60 * 2**20),
        cost_estimate=pl.CostEstimate(
            flops=2 * rows * depth * feats, bytes_accessed=8 * 2**20, transcendentals=0
        ),
        name="raw",
    )(pattern.T, showers.T, geometry)


NAMES = ("own", "own_t", "y1", "y1_t", "y2", "y2_t", "x1", "x1_t", "xa", "xb", "xa_t", "xb_t", "w2", "w2_t", "odd")
TAG_OF = ("own", "x1", "own_t", "x1_t", "own")


def pair_kernel(*refs, col_cuts, n_cols_args, late):
    n_cols = len(col_cuts)
    names = NAMES if late else NAMES[:6]
    place, refs = refs[0], refs[1:]
    before, refs = refs[: 2 * late], refs[2 * late :]
    col_args, refs = refs[:n_cols_args], refs[n_cols_args:]
    held, refs = dict(zip(names, refs)), refs[len(names) :]
    outs, refs = refs[: 4 if late else 2], refs[4 if late else 2 :]
    rows_at, cols_at = refs
    odd_here, core = place[0], place[1]
    tagged = BLOCK + TAG

    starts = [sum(size for _, _, size in col_cuts[:at]) for at in range(n_cols)]
    depth = sum(size for _, _, size in col_cuts)
    for at, (arg, first, size) in enumerate(col_cuts):
        cols_at[pl.ds(starts[at], size), :] = col_args[arg][pl.ds(first, size), :]
    chunks = (0, 2, 1, 3, 4) if late else (0, 2)
    turn = jnp.where(core == 0, 3, 1)
    side = [2 * CHUNK * jnp.where(core == b, 0, 1) for b in range(NC)]

    def rows(name, first, at):
        at = at if isinstance(at, int) else pl.multiple_of(at, BLOCK)
        rows_at[pl.ds(at, BLOCK), :] = held[name][pl.ds(first, BLOCK), :]

    rows("own", TAG, 0)
    rows("y2", 0, 2 * BLOCK)
    for b in range(NC):
        rows("y1", TAG + b * tagged, side[b] + turn * BLOCK)
        rows("y1_t", TAG + b * tagged, side[b] + (NY - turn) * BLOCK)
    rows("own_t", TAG, 2 * CHUNK)
    rows("y2_t", 0, 2 * CHUNK + 2 * BLOCK)
    if late:
        rows("x1", TAG, CHUNK)
        rows("w2", 0, CHUNK + 2 * BLOCK)
        for b in range(NC):
            rows(("xa", "xb")[b], 0, CHUNK + side[b] + turn * BLOCK)
            rows(("xa_t", "xb_t")[b], 0, CHUNK + side[b] + (NY - turn) * BLOCK)
        rows("x1_t", TAG, 3 * CHUNK)
        rows("w2_t", 0, 3 * CHUNK + 2 * BLOCK)
        rows("odd", 0, 4 * CHUNK)

    def bin_of(code):
        source = (code >= BINS).astype(jnp.float32)
        return code - BINS * source, source

    for chunk in chunks:
        first = chunk * CHUNK
        odd = chunk == 4
        size = BLOCK if odd else CHUNK
        tag = held[TAG_OF[chunk]][4:5, pl.ds(0, BLOCK)].astype(jnp.float32) - 1.0
        bins, _ = bin_of(tag)
        if odd:
            bins = jnp.where(odd_here > 0, bins, -2.0)
        bins = jnp.concatenate([bins] * (size // BLOCK), axis=1)
        one = jnp.zeros((8, size), jnp.float32)
        zero = jnp.zeros((8, size), jnp.float32)
        n_one = jnp.zeros((1, size), jnp.float32)
        n_zero = jnp.zeros((1, size), jnp.float32)
        low = EARLY * BLOCK if late and chunk in (0, 2) else 0
        while low < depth:
            high = depth if depth - low < 3 * BLOCK else low + 2 * BLOCK
            products = lax.dot_general(
                cols_at[pl.ds(low, high - low), :],
                rows_at[pl.ds(first, size), :],
                (((1,), (1,)), ((), ())),
                preferred_element_type=jnp.float32,
            )
            shifted = products + 32.0
            cubes = shifted * shifted * shifted
            for group in range(low // PIECE, high // PIECE):
                at = group * PIECE // BLOCK
                if odd and col_cuts[at][2] == PIECE:
                    continue
                block = cubes[group * PIECE - low : (group + 1) * PIECE - low]
                if first == 0 and at == 0:
                    lane = lax.broadcasted_iota(jnp.int32, block.shape, 1)
                    sub = lax.broadcasted_iota(jnp.int32, block.shape, 0)
                    block = jnp.where(lane == sub + group * PIECE, 0.0, block)
                part = (block[0:8] + block[8:16]) + (block[16:24] + block[24:32])
                arg, place_of, _ = col_cuts[at]
                row = place_of - TAG + group % 4
                code = col_args[arg][pl.ds(row, 1), pl.ds(0, size)].astype(jnp.float32) - 1.0
                bin_id, source = bin_of(code)
                match = (bins == bin_id).astype(jnp.float32)
                is_one = match * source
                is_zero = match - is_one
                one += is_one * part
                zero += is_zero * part
                n_one += is_one
                n_zero += is_zero
            low = high
        one = jnp.sum(one, axis=0, keepdims=True)
        zero = jnp.sum(zero, axis=0, keepdims=True)
        if late:
            targets = {0: [(outs[0], 0)], 1: [(outs[1], 0)], 2: [(outs[2], 0)]}
            targets |= {3: [(outs[2], CHUNK)], 4: [(outs[2], 2 * CHUNK), (outs[3], 0)]}
            earlier = {0: before[0], 2: before[1]}.get(chunk)
        else:
            targets, earlier = {0: [(outs[0], 0)], 2: [(outs[1], 0)]}, None
        values = [one, zero, n_one, n_zero]
        if earlier is not None:
            values = [earlier[i : i + 1, :] + value for i, value in enumerate(values)]
        for out, place_at in targets[chunk]:
            for i, value in enumerate(values):
                out[i : i + 1, pl.ds(place_at, size)] = value


def pair_sums(place, col_args, row_args, col_cuts, before):
    late = before is not None
    total = 4 * CHUNK + BLOCK if late else 3 * CHUNK
    used, depth = (5 if late else 2) * CHUNK, sum(size for _, _, size in col_cuts)
    feats = col_args[0].shape[1]
    vmem = pl.BlockSpec(memory_space=pltpu.VMEM)
    widths = [CHUNK, CHUNK, 2 * CHUNK + BLOCK, BLOCK] if late else [CHUNK, CHUNK]
    names = NAMES if late else NAMES[:6]
    before = list(before or [])
    return pl.pallas_call(
        functools.partial(
            pair_kernel, col_cuts=tuple(col_cuts), n_cols_args=len(col_args), late=late
        ),
        in_specs=[pl.BlockSpec(memory_space=pltpu.SMEM)]
        + [vmem] * (len(before) + len(col_args) + len(names)),
        out_specs=[vmem] * len(widths),
        out_shape=[jax.ShapeDtypeStruct((4, width), jnp.float32) for width in widths],
        scratch_shapes=[
            pltpu.VMEM((total, feats), jnp.bfloat16),
            pltpu.VMEM((depth, feats), jnp.bfloat16),
        ],
        compiler_params=pltpu.CompilerParams(vmem_limit_bytes=18 * 2**20),
        cost_estimate=pl.CostEstimate(
            flops=6 * used * depth * feats,
            bytes_accessed=6 * (used + depth) * feats,
            transcendentals=0,
        ),
        name="late" if late else "early",
    )(place, *before, *col_args, *[row_args[name] for name in names])


def shards(showers, geometry, pattern, bins, sources):
    y = lax.axis_index("layer")
    s = lax.axis_index("shower")
    x, z, c = s // (NZ * NC), (s // NC) % NZ, s % NC
    feats = geometry.shape[1]
    blocks = bins.shape[0]

    codes = (bins + BINS * sources + 1).astype(jnp.float32)
    line = lax.broadcasted_iota(jnp.int32, (TAG, feats), 0)
    lane = lax.broadcasted_iota(jnp.int32, (TAG, feats), 1) // PIECE
    which = jnp.where(line == blocks, lane, line)
    tag = jnp.zeros((TAG, feats), jnp.float32)
    for group in range(blocks):
        tag = jnp.where(which == group, codes[group], tag)
    tag = tag.astype(jnp.bfloat16)

    partial_sums = raw_partial(showers, geometry, pattern).reshape(blocks, NY, PIECE, feats)

    def share(sums, turn):
        part = lax.dynamic_index_in_dim(sums, (y + turn) % NY, 1, keepdims=False)
        return part.reshape(BLOCK, feats)

    arrived = []
    for turn in (2, 1, 3):
        part = share(partial_sums, turn).astype(jnp.float16)
        partial_sums, part = lax.optimization_barrier((partial_sums, part))
        arrived.append(permute(part, along_y(turn)))
    raw = share(partial_sums, 0)
    for part in arrived:
        raw = raw + part.astype(jnp.float32)
    scale = lax.rsqrt(jnp.mean(raw * raw, axis=1, keepdims=True) + 1e-05)
    own = jnp.concatenate([tag, (raw * scale).astype(jnp.bfloat16)], axis=0)

    fence = lambda *values: lax.optimization_barrier(values)
    tagged = BLOCK + TAG
    y_way = lambda y, x, z, c: ((y + 1 - 2 * c) % NY, x, z, c)
    own_t = permute(own, swap_core)
    chip = jnp.where(c == 0, jnp.concatenate([own, own_t]), jnp.concatenate([own_t, own]))
    z1 = permute(chip, same_core)
    y1 = permute(chip, y_way)
    x1 = permute(own, swap_x)
    z1, y1, x1 = fence(z1, y1, x1)

    z2 = permute(z1, same_core)
    y2 = permute(jnp.where(c == 0, y1[TAG:tagged], y1[tagged + TAG :]), y_way)
    xa = permute(y1[TAG:tagged], swap_x)
    x1_t = permute(x1, swap_core)
    xb_from = y1[tagged + TAG :]
    z1, z2, y2, xa, y1, x1_t, xb_from = fence(z1, z2, y2, xa, y1, x1_t, xb_from)

    z3 = permute(z2, same_core)
    xb = permute(xb_from, swap_x)
    y1_t = permute(y1, swap_core)
    head = TAG + PIECE
    odd_rows = jnp.concatenate([own[TAG:head], y1_t[TAG:head], y2[:PIECE], y1[TAG:head]], axis=0)
    at_start = lambda y, x, z, c: z == 0 and c == 0
    odd_at = [
        permute(
            odd_rows,
            lambda y, x, z, c, to=to: (y, to, z, c),
            keep=lambda *a: a[1] == 2 and at_start(*a),
        )
        for to in (1, 0)
    ]
    y2_t = permute(y2, swap_core)
    xa_t = permute(xa, swap_core)
    z2, z3, y2, xb, y1_t, y2_t, xa_t, odd_at[0] = fence(
        z2, z3, y2, xb, y1_t, y2_t, xa_t, odd_at[0]
    )

    z4 = permute(jnp.where(c == 0, z3[:tagged], z3[tagged:]), same_core)
    held = [chip, z1, z2, z3, z3, z3, z2, z1]
    piece = permute(
        lax.select_n(z, *[value[:head] for value in held]),
        lambda y, x, z, c: (y, 1, z + 1 - c, c),
        keep=lambda y, x, z, c: x == 2 and (z < 4 if c == 0 else z == 0 or z > 4),
    )
    w2 = permute(y2, swap_x)
    xb_t = permute(xb, swap_core)
    col_args = [own, z1, z2, z3]
    col_cuts = [(0, TAG, BLOCK)]
    for arg in (1, 2, 3):
        col_cuts += [(arg, TAG, BLOCK), (arg, tagged + TAG, BLOCK)]
    row_args = dict(own=own, own_t=own_t, y1=y1, y1_t=y1_t, y2=y2, y2_t=y2_t)
    place = jnp.stack([((x < 2) & (z == 0)).astype(jnp.int32), c.astype(jnp.int32)])
    early = pair_sums(place, col_args, row_args, col_cuts, None)
    w2, odd_at[0], odd_at[1], early, piece = fence(w2, odd_at[0], odd_at[1], early, piece)
    w2_t = permute(w2, swap_core)
    odd_rows = odd_at[0] + odd_at[1]
    odd_rows = odd_rows + permute(
        odd_rows, swap_core, keep=lambda *a: a[1] < 2 and at_start(*a)
    )
    row_args |= dict(x1=x1, x1_t=x1_t, xa=xa, xb=xb, xa_t=xa_t, xb_t=xb_t, w2=w2, w2_t=w2_t)
    row_args["odd"] = odd_rows
    col_cuts += [(4, TAG, BLOCK), (5, TAG, PIECE)]
    near, far, theirs, odd_stats = pair_sums(
        place, col_args + [z4, piece], row_args, col_cuts, early
    )

    theirs = permute(theirs, swap_core)
    kept = near + theirs[:, :CHUNK] + permute(far + theirs[:, CHUNK : 2 * CHUNK], swap_x)
    odd_stats = odd_stats + theirs[:, 2 * CHUNK :]
    odd_total = jnp.zeros_like(odd_stats)
    for start in (0, 1):
        odd_total = odd_total + permute(
            odd_stats,
            lambda y, x, z, c: (y, 2, z, c),
            keep=lambda *a, start=start: a[1] == start and at_start(*a),
        )
    odd_total = odd_total.reshape(4, NY, PIECE)
    kept = kept.reshape(4, NY, BLOCK) + jnp.pad(odd_total, ((0, 0), (0, 0), (0, BLOCK - PIECE)))
    total = kept
    for turn in (2, 1, 3):
        total = total + jnp.roll(permute(kept, along_y(turn)), -turn, axis=1)
    weight = 1.0 / (PIECE * 32.0**3)
    proof = (total[0] / total[2] - total[1] / total[3]) * weight
    proof = jnp.concatenate([proof, proof], axis=0)
    proof = lax.dynamic_slice_in_dim(proof, (NY - y) % NY, NY, 0).reshape(NY, blocks, PIECE)
    return jnp.transpose(proof, (1, 0, 2)).reshape(-1)


def solution(mesh):
    placed = (P("shower", "layer"), P("layer", None), P("layer", None), P("shower"), P("shower"))
    return jax.shard_map(shards, mesh=mesh, in_specs=placed, out_specs=P("shower"), check_vma=False)
```

```python
import functools

import jax
import jax.numpy as jnp
from jax import lax
from jax.experimental import pallas as pl
from jax.experimental.pallas import tpu as pltpu
from jax.sharding import PartitionSpec as P

BLOCK = 128
PIECE = 32
TAG = 16
BINS = 8
CHUNK = 512
EARLY = 7
AXES = ("layer", "shower")
NY, NX, NZ, NC = 4, 4, 8, 2


def flat(y, x, z, c):
    return y * (NX * NZ * NC) + (x * NZ + z) * NC + c


def permute(value, move, keep=lambda y, x, z, c: True):
    pairs = [
        (flat(y, x, z, c), flat(*move(y, x, z, c)))
        for y in range(NY)
        for x in range(NX)
        for z in range(NZ)
        for c in range(NC)
        if keep(y, x, z, c)
    ]
    return lax.ppermute(value, AXES, pairs)


def along_y(step):
    return lambda y, x, z, c: ((y + step) % NY, x, z, c)


def along_z(step):
    return lambda y, x, z, c: (y, x, (z + step) % NZ, c)


def flip_z(bit):
    return lambda y, x, z, c: (y, x, z ^ bit, c)


def swap_x(y, x, z, c):
    return (y, x ^ 1, z, c)


def swap_core(y, x, z, c):
    return (y, x, z, 1 - c)


def same_core(y, x, z, c):
    return (y, x, (z + 1 - 2 * c) % NZ, c)


def cross_core(y, x, z, c):
    return (y, x, (z - 1 + 2 * c) % NZ, 1 - c)


def raw_kernel(pattern, showers, geometry, out, masked):
    step = pl.program_id(0)
    layers = pattern.shape[1]
    cells = geometry.shape[0] // layers
    per = geometry.shape[1] // BLOCK
    for layer in range(layers):
        for part in range(per):
            rows = pl.ds(layer * cells, cells)
            cols = pl.ds(part * BLOCK, BLOCK)
            on = pattern[step * per + part, layer].astype(jnp.float32).astype(jnp.bfloat16)
            masked[rows, cols] = geometry[rows, cols] * on
    out[...] = lax.dot_general(
        showers[...], masked[...], (((0,), (0,)), ((), ())), preferred_element_type=jnp.float32
    )


def raw_partial(showers, geometry, pattern):
    rows, depth = showers.shape
    feats = geometry.shape[1]
    width = 512
    return pl.pallas_call(
        raw_kernel,
        grid=(feats // width,),
        in_specs=[
            pl.BlockSpec(memory_space=pltpu.SMEM),
            pl.BlockSpec((depth, rows), lambda i: (0, 0)),
            pl.BlockSpec((depth, width), lambda i: (0, i)),
        ],
        out_specs=pl.BlockSpec((rows, width), lambda i: (0, i)),
        out_shape=jax.ShapeDtypeStruct((rows, feats), jnp.float32),
        scratch_shapes=[pltpu.VMEM((depth, width), jnp.bfloat16)],
        compiler_params=pltpu.CompilerParams(vmem_limit_bytes=60 * 2**20),
        cost_estimate=pl.CostEstimate(
            flops=2 * rows * depth * feats, bytes_accessed=8 * 2**20, transcendentals=0
        ),
        name="raw",
    )(pattern.T, showers.T, geometry)


NAMES = ("own", "own_t", "y1", "y1_t", "y2", "y2_t", "x1", "x1_t", "xa", "xb", "xa_t", "xb_t", "w2", "w2_t", "odd")
TAG_OF = ("own", "x1", "own_t", "x1_t", "own")


def pair_kernel(*refs, col_cuts, n_cols_args, late):
    n_cols = len(col_cuts)
    names = NAMES if late else NAMES[:6]
    place, refs = refs[0], refs[1:]
    before, refs = refs[: 2 * late], refs[2 * late :]
    col_args, refs = refs[:n_cols_args], refs[n_cols_args:]
    held, refs = dict(zip(names, refs)), refs[len(names) :]
    outs, refs = refs[: 4 if late else 2], refs[4 if late else 2 :]
    rows_at, cols_at = refs
    odd_here, core = place[0], place[1]
    tagged = BLOCK + TAG

    starts = [sum(size for _, _, size in col_cuts[:at]) for at in range(n_cols)]
    depth = sum(size for _, _, size in col_cuts)
    for at, (arg, first, size) in enumerate(col_cuts):
        cols_at[pl.ds(starts[at], size), :] = col_args[arg][pl.ds(first, size), :]
    chunks = (0, 2, 1, 3, 4) if late else (0, 2)
    turn = jnp.where(core == 0, 3, 1)
    side = [2 * CHUNK * jnp.where(core == b, 0, 1) for b in range(NC)]

    def rows(name, first, at):
        at = at if isinstance(at, int) else pl.multiple_of(at, BLOCK)
        rows_at[pl.ds(at, BLOCK), :] = held[name][pl.ds(first, BLOCK), :]

    rows("own", TAG, 0)
    rows("y2", 0, 2 * BLOCK)
    for b in range(NC):
        rows("y1", TAG + b * tagged, side[b] + turn * BLOCK)
        rows("y1_t", TAG + b * tagged, side[b] + (NY - turn) * BLOCK)
    rows("own_t", TAG, 2 * CHUNK)
    rows("y2_t", 0, 2 * CHUNK + 2 * BLOCK)
    if late:
        rows("x1", TAG, CHUNK)
        rows("w2", 0, CHUNK + 2 * BLOCK)
        rows("xa", 0, CHUNK + turn * BLOCK)
        rows("xb", 0, 3 * CHUNK + turn * BLOCK)
        rows("xa_t", 0, 3 * CHUNK + (NY - turn) * BLOCK)
        rows("xb_t", 0, CHUNK + (NY - turn) * BLOCK)
        rows("x1_t", TAG, 3 * CHUNK)
        rows("w2_t", 0, 3 * CHUNK + 2 * BLOCK)
        rows("odd", 0, 4 * CHUNK)

    def bin_of(code):
        source = (code >= BINS).astype(jnp.float32)
        return code - BINS * source, source

    for chunk in chunks:
        first = chunk * CHUNK
        odd = chunk == 4
        size = BLOCK if odd else CHUNK
        tag = held[TAG_OF[chunk]][4:5, pl.ds(0, BLOCK)].astype(jnp.float32) - 1.0
        bins, _ = bin_of(tag)
        if odd:
            bins = jnp.where(odd_here > 0, bins, -2.0)
        bins = jnp.concatenate([bins] * (size // BLOCK), axis=1)
        one = jnp.zeros((8, size), jnp.float32)
        zero = jnp.zeros((8, size), jnp.float32)
        n_one = jnp.zeros((1, size), jnp.float32)
        n_zero = jnp.zeros((1, size), jnp.float32)
        low = EARLY * BLOCK if late and chunk in (0, 2) else 0
        while low < depth:
            high = depth if depth - low < 3 * BLOCK else low + 2 * BLOCK
            products = lax.dot_general(
                cols_at[pl.ds(low, high - low), :],
                rows_at[pl.ds(first, size), :],
                (((1,), (1,)), ((), ())),
                preferred_element_type=jnp.float32,
            )
            shifted = products + 32.0
            cubes = shifted * shifted * shifted
            for group in range(low // PIECE, high // PIECE):
                at = group * PIECE // BLOCK
                if odd and col_cuts[at][2] == PIECE:
                    continue
                block = cubes[group * PIECE - low : (group + 1) * PIECE - low]
                if first == 0 and at == 0:
                    lane = lax.broadcasted_iota(jnp.int32, block.shape, 1)
                    sub = lax.broadcasted_iota(jnp.int32, block.shape, 0)
                    block = jnp.where(lane == sub + group * PIECE, 0.0, block)
                part = (block[0:8] + block[8:16]) + (block[16:24] + block[24:32])
                arg, place_of, _ = col_cuts[at]
                row = place_of - TAG + group % 4
                code = col_args[arg][pl.ds(row, 1), pl.ds(0, size)].astype(jnp.float32) - 1.0
                bin_id, source = bin_of(code)
                match = (bins == bin_id).astype(jnp.float32)
                is_one = match * source
                is_zero = match - is_one
                one += is_one * part
                zero += is_zero * part
                n_one += is_one
                n_zero += is_zero
            low = high
        one = jnp.sum(one, axis=0, keepdims=True)
        zero = jnp.sum(zero, axis=0, keepdims=True)
        if late:
            targets = {0: [(outs[0], 0)], 1: [(outs[1], 0)], 2: [(outs[2], 0)]}
            targets |= {3: [(outs[2], CHUNK)], 4: [(outs[2], 2 * CHUNK), (outs[3], 0)]}
            earlier = {0: before[0], 2: before[1]}.get(chunk)
        else:
            targets, earlier = {0: [(outs[0], 0)], 2: [(outs[1], 0)]}, None
        values = [one, zero, n_one, n_zero]
        if earlier is not None:
            values = [earlier[i : i + 1, :] + value for i, value in enumerate(values)]
        for out, place_at in targets[chunk]:
            for i, value in enumerate(values):
                out[i : i + 1, pl.ds(place_at, size)] = value


def pair_sums(place, col_args, row_args, col_cuts, before):
    late = before is not None
    total = 4 * CHUNK + BLOCK if late else 3 * CHUNK
    used, depth = (5 if late else 2) * CHUNK, sum(size for _, _, size in col_cuts)
    feats = col_args[0].shape[1]
    vmem = pl.BlockSpec(memory_space=pltpu.VMEM)
    widths = [CHUNK, CHUNK, 2 * CHUNK + BLOCK, BLOCK] if late else [CHUNK, CHUNK]
    names = NAMES if late else NAMES[:6]
    before = list(before or [])
    return pl.pallas_call(
        functools.partial(
            pair_kernel, col_cuts=tuple(col_cuts), n_cols_args=len(col_args), late=late
        ),
        in_specs=[pl.BlockSpec(memory_space=pltpu.SMEM)]
        + [vmem] * (len(before) + len(col_args) + len(names)),
        out_specs=[vmem] * len(widths),
        out_shape=[jax.ShapeDtypeStruct((4, width), jnp.float32) for width in widths],
        scratch_shapes=[
            pltpu.VMEM((total, feats), jnp.bfloat16),
            pltpu.VMEM((depth, feats), jnp.bfloat16),
        ],
        compiler_params=pltpu.CompilerParams(vmem_limit_bytes=18 * 2**20),
        cost_estimate=pl.CostEstimate(
            flops=6 * used * depth * feats,
            bytes_accessed=6 * (used + depth) * feats,
            transcendentals=0,
        ),
        name="late" if late else "early",
    )(place, *before, *col_args, *[row_args[name] for name in names])


def shards(showers, geometry, pattern, bins, sources):
    y = lax.axis_index("layer")
    s = lax.axis_index("shower")
    x, z, c = s // (NZ * NC), (s // NC) % NZ, s % NC
    feats = geometry.shape[1]
    blocks = bins.shape[0]

    codes = (bins + BINS * sources + 1).astype(jnp.float32)
    line = lax.broadcasted_iota(jnp.int32, (TAG, feats), 0)
    lane = lax.broadcasted_iota(jnp.int32, (TAG, feats), 1) // PIECE
    which = jnp.where(line == blocks, lane, line)
    tag = jnp.zeros((TAG, feats), jnp.float32)
    for group in range(blocks):
        tag = jnp.where(which == group, codes[group], tag)
    tag = tag.astype(jnp.bfloat16)

    partial_sums = raw_partial(showers, geometry, pattern).reshape(blocks, NY, PIECE, feats)

    def share(turn):
        part = lax.dynamic_index_in_dim(partial_sums, (y + turn) % NY, 1, keepdims=False)
        return part.reshape(BLOCK, feats)

    raw = share(0)
    arrived = [permute(share(turn).astype(jnp.float16), along_y(turn)) for turn in (2, 1, 3)]
    for part in arrived:
        raw = raw + part.astype(jnp.float32)
    scale = lax.rsqrt(jnp.mean(raw * raw, axis=1, keepdims=True) + 1e-05)
    own = jnp.concatenate([tag, (raw * scale).astype(jnp.bfloat16)], axis=0)

    fence = lambda *values: lax.optimization_barrier(values)
    tagged = BLOCK + TAG
    y_way = lambda y, x, z, c: ((y + 1 - 2 * c) % NY, x, z, c)
    own_t = permute(own, swap_core)
    chip = jnp.where(c == 0, jnp.concatenate([own, own_t]), jnp.concatenate([own_t, own]))
    z1 = permute(chip, same_core)
    y1 = permute(chip, y_way)
    x1 = permute(own, swap_x)
    z1, y1, x1 = fence(z1, y1, x1)

    z2 = permute(z1, same_core)
    near_one, far_one = y1[TAG:tagged], y1[tagged + TAG :]
    y1_mine = jnp.where(c == 0, near_one, far_one)
    y1_other = jnp.where(c == 0, far_one, near_one)
    y1_mine, y1_other = fence(y1_mine, y1_other)
    y2 = permute(y1_mine, y_way)
    xa = permute(y1_mine, swap_x)
    x1_t = permute(x1, swap_core)
    z1, z2, y2, xa, y1, x1_t = fence(z1, z2, y2, xa, y1, x1_t)

    z3 = permute(z2, same_core)
    xb = permute(y1_other, swap_x)
    y1_t = permute(y1, swap_core)
    head = TAG + PIECE
    odd_rows = jnp.concatenate([own[TAG:head], y1_t[TAG:head], y2[:PIECE], y1[TAG:head]], axis=0)
    at_start = lambda y, x, z, c: z == 0 and c == 0
    odd_at = [
        permute(
            odd_rows,
            lambda y, x, z, c, to=to: (y, to, z, c),
            keep=lambda *a: a[1] == 2 and at_start(*a),
        )
        for to in (1, 0)
    ]
    y2_t = permute(y2, swap_core)
    xa_t = permute(xa, swap_core)
    z2, z3, y2, xb, y1_t, y2_t, xa_t, odd_at[0] = fence(
        z2, z3, y2, xb, y1_t, y2_t, xa_t, odd_at[0]
    )

    z4 = permute(jnp.where(c == 0, z3[:tagged], z3[tagged:]), same_core)
    held = [chip, z1, z2, z3, z3, z3, z2, z1]
    piece = permute(
        lax.select_n(z, *[value[:head] for value in held]),
        lambda y, x, z, c: (y, 1, z + 1 - c, c),
        keep=lambda y, x, z, c: x == 2 and (z < 4 if c == 0 else z == 0 or z > 4),
    )
    w2 = permute(y2, swap_x)
    xb_t = permute(xb, swap_core)
    col_args = [own, z1, z2, z3]
    col_cuts = [(0, TAG, BLOCK)]
    for arg in (1, 2, 3):
        col_cuts += [(arg, TAG, BLOCK), (arg, tagged + TAG, BLOCK)]
    row_args = dict(own=own, own_t=own_t, y1=y1, y1_t=y1_t, y2=y2, y2_t=y2_t)
    place = jnp.stack([((x < 2) & (z == 0)).astype(jnp.int32), c.astype(jnp.int32)])
    early = pair_sums(place, col_args, row_args, col_cuts, None)
    w2, odd_at[0], odd_at[1], early, piece = fence(w2, odd_at[0], odd_at[1], early, piece)
    w2_t = permute(w2, swap_core)
    odd_rows = odd_at[0] + odd_at[1]
    odd_rows = odd_rows + permute(
        odd_rows, swap_core, keep=lambda *a: a[1] < 2 and at_start(*a)
    )
    row_args |= dict(x1=x1, x1_t=x1_t, xa=xa, xb=xb, xa_t=xa_t, xb_t=xb_t, w2=w2, w2_t=w2_t)
    row_args["odd"] = odd_rows
    col_cuts += [(4, TAG, BLOCK), (5, TAG, PIECE)]
    near, far, theirs, odd_stats = pair_sums(
        place, col_args + [z4, piece], row_args, col_cuts, early
    )

    theirs = permute(theirs, swap_core)
    kept = near + theirs[:, :CHUNK] + permute(far + theirs[:, CHUNK : 2 * CHUNK], swap_x)
    odd_stats = odd_stats + theirs[:, 2 * CHUNK :]
    odd_total = jnp.zeros_like(odd_stats)
    for start in (0, 1):
        odd_total = odd_total + permute(
            odd_stats,
            lambda y, x, z, c: (y, 2, z, c),
            keep=lambda *a, start=start: a[1] == start and at_start(*a),
        )
    odd_total = odd_total.reshape(4, NY, PIECE)
    kept = kept.reshape(4, NY, BLOCK) + jnp.pad(odd_total, ((0, 0), (0, 0), (0, BLOCK - PIECE)))
    total = kept
    for turn in (2, 1, 3):
        total = total + jnp.roll(permute(kept, along_y(turn)), -turn, axis=1)
    weight = 1.0 / (PIECE * 32.0**3)
    proof = (total[0] / total[2] - total[1] / total[3]) * weight
    proof = jnp.concatenate([proof, proof], axis=0)
    proof = lax.dynamic_slice_in_dim(proof, (NY - y) % NY, NY, 0).reshape(NY, blocks, PIECE)
    return jnp.transpose(proof, (1, 0, 2)).reshape(-1)


def solution(mesh):
    placed = (P("shower", "layer"), P("layer", None), P("layer", None), P("shower"), P("shower"))
    return jax.shard_map(shards, mesh=mesh, in_specs=placed, out_specs=P("shower"), check_vma=False)
```

```python
import functools

import jax
import jax.numpy as jnp
from jax import lax
from jax.experimental import pallas as pl
from jax.experimental.pallas import tpu as pltpu
from jax.sharding import PartitionSpec as P

BLOCK = 128
PIECE = 32
TAG = 16
BINS = 8
CHUNK = 512
EARLY = 7
AXES = ("layer", "shower")
NY, NX, NZ, NC = 4, 4, 8, 2


def flat(y, x, z, c):
    return y * (NX * NZ * NC) + (x * NZ + z) * NC + c


def permute(value, move, keep=lambda y, x, z, c: True):
    pairs = [
        (flat(y, x, z, c), flat(*move(y, x, z, c)))
        for y in range(NY)
        for x in range(NX)
        for z in range(NZ)
        for c in range(NC)
        if keep(y, x, z, c)
    ]
    return lax.ppermute(value, AXES, pairs)


def along_y(step):
    return lambda y, x, z, c: ((y + step) % NY, x, z, c)


def along_z(step):
    return lambda y, x, z, c: (y, x, (z + step) % NZ, c)


def flip_z(bit):
    return lambda y, x, z, c: (y, x, z ^ bit, c)


def swap_x(y, x, z, c):
    return (y, x ^ 1, z, c)


def swap_core(y, x, z, c):
    return (y, x, z, 1 - c)


def same_core(y, x, z, c):
    return (y, x, (z + 1 - 2 * c) % NZ, c)


def cross_core(y, x, z, c):
    return (y, x, (z - 1 + 2 * c) % NZ, 1 - c)


def raw_kernel(pattern, showers, geometry, out, masked):
    step = pl.program_id(0)
    layers = pattern.shape[1]
    cells = geometry.shape[0] // layers
    per = geometry.shape[1] // BLOCK
    for layer in range(layers):
        for part in range(per):
            rows = pl.ds(layer * cells, cells)
            cols = pl.ds(part * BLOCK, BLOCK)
            on = pattern[step * per + part, layer].astype(jnp.float32).astype(jnp.bfloat16)
            masked[rows, cols] = geometry[rows, cols] * on
    out[...] = lax.dot_general(
        showers[...], masked[...], (((0,), (0,)), ((), ())), preferred_element_type=jnp.float32
    )


def raw_partial(showers, geometry, pattern):
    rows, depth = showers.shape
    feats = geometry.shape[1]
    width = 512
    return pl.pallas_call(
        raw_kernel,
        grid=(feats // width,),
        in_specs=[
            pl.BlockSpec(memory_space=pltpu.SMEM),
            pl.BlockSpec((depth, rows), lambda i: (0, 0)),
            pl.BlockSpec((depth, width), lambda i: (0, i)),
        ],
        out_specs=pl.BlockSpec((rows, width), lambda i: (0, i)),
        out_shape=jax.ShapeDtypeStruct((rows, feats), jnp.float32),
        scratch_shapes=[pltpu.VMEM((depth, width), jnp.bfloat16)],
        compiler_params=pltpu.CompilerParams(vmem_limit_bytes=60 * 2**20),
        cost_estimate=pl.CostEstimate(
            flops=2 * rows * depth * feats, bytes_accessed=8 * 2**20, transcendentals=0
        ),
        name="raw",
    )(pattern.T, showers.T, geometry)


NAMES = ("own", "own_t", "y1", "y1_t", "y2", "y2_t", "x1", "x1_t", "xa", "xb", "xa_t", "xb_t", "w2", "w2_t", "odd")
TAG_OF = ("own", "x1", "own_t", "x1_t", "own")


def pair_kernel(*refs, col_cuts, n_cols_args, late):
    n_cols = len(col_cuts)
    names = NAMES if late else NAMES[:6]
    place, refs = refs[0], refs[1:]
    before, refs = refs[: 2 * late], refs[2 * late :]
    col_args, refs = refs[:n_cols_args], refs[n_cols_args:]
    held, refs = dict(zip(names, refs)), refs[len(names) :]
    outs, refs = refs[: 4 if late else 2], refs[4 if late else 2 :]
    rows_at, cols_at = refs
    odd_here, core = place[0], place[1]
    tagged = BLOCK + TAG

    starts = [sum(size for _, _, size in col_cuts[:at]) for at in range(n_cols)]
    depth = sum(size for _, _, size in col_cuts)
    for at, (arg, first, size) in enumerate(col_cuts):
        cols_at[pl.ds(starts[at], size), :] = col_args[arg][pl.ds(first, size), :]
    chunks = (0, 2, 1, 3, 4) if late else (0, 2)
    turn = jnp.where(core == 0, 3, 1)
    side = [2 * CHUNK * jnp.where(core == b, 0, 1) for b in range(NC)]

    def rows(name, first, at):
        at = at if isinstance(at, int) else pl.multiple_of(at, BLOCK)
        rows_at[pl.ds(at, BLOCK), :] = held[name][pl.ds(first, BLOCK), :]

    rows("own", TAG, 0)
    rows("y2", 0, 2 * BLOCK)
    for b in range(NC):
        rows("y1", TAG + b * tagged, side[b] + turn * BLOCK)
        rows("y1_t", TAG + b * tagged, side[b] + (NY - turn) * BLOCK)
    rows("own_t", TAG, 2 * CHUNK)
    rows("y2_t", 0, 2 * CHUNK + 2 * BLOCK)
    if late:
        rows("x1", TAG, CHUNK)
        rows("w2", 0, CHUNK + 2 * BLOCK)
        rows("xa", 0, CHUNK + turn * BLOCK)
        rows("xb", 0, 3 * CHUNK + turn * BLOCK)
        rows("xa_t", 0, 3 * CHUNK + (NY - turn) * BLOCK)
        rows("xb_t", 0, CHUNK + (NY - turn) * BLOCK)
        rows("x1_t", TAG, 3 * CHUNK)
        rows("w2_t", 0, 3 * CHUNK + 2 * BLOCK)
        rows("odd", 0, 4 * CHUNK)

    def bin_of(code):
        source = (code >= BINS).astype(jnp.float32)
        return code - BINS * source, source

    for chunk in chunks:
        first = chunk * CHUNK
        odd = chunk == 4
        size = BLOCK if odd else CHUNK
        tag = held[TAG_OF[chunk]][4:5, pl.ds(0, BLOCK)].astype(jnp.float32) - 1.0
        bins, _ = bin_of(tag)
        if odd:
            bins = jnp.where(odd_here > 0, bins, -2.0)
        bins = jnp.concatenate([bins] * (size // BLOCK), axis=1)
        one = jnp.zeros((8, size), jnp.float32)
        zero = jnp.zeros((8, size), jnp.float32)
        n_one = jnp.zeros((1, size), jnp.float32)
        n_zero = jnp.zeros((1, size), jnp.float32)
        low = EARLY * BLOCK if late and chunk in (0, 2) else 0
        while low < depth:
            high = depth if depth - low < 3 * BLOCK else low + 2 * BLOCK
            products = lax.dot_general(
                cols_at[pl.ds(low, high - low), :],
                rows_at[pl.ds(first, size), :],
                (((1,), (1,)), ((), ())),
                preferred_element_type=jnp.float32,
            )
            shifted = products + 32.0
            cubes = shifted * shifted * shifted
            for group in range(low // PIECE, high // PIECE):
                at = group * PIECE // BLOCK
                if odd and col_cuts[at][2] == PIECE:
                    continue
                block = cubes[group * PIECE - low : (group + 1) * PIECE - low]
                if first == 0 and at == 0:
                    lane = lax.broadcasted_iota(jnp.int32, block.shape, 1)
                    sub = lax.broadcasted_iota(jnp.int32, block.shape, 0)
                    block = jnp.where(lane == sub + group * PIECE, 0.0, block)
                part = (block[0:8] + block[8:16]) + (block[16:24] + block[24:32])
                arg, place_of, _ = col_cuts[at]
                row = place_of - TAG + group % 4
                code = col_args[arg][pl.ds(row, 1), pl.ds(0, size)].astype(jnp.float32) - 1.0
                bin_id, source = bin_of(code)
                match = (bins == bin_id).astype(jnp.float32)
                is_one = match * source
                is_zero = match - is_one
                one += is_one * part
                zero += is_zero * part
                n_one += is_one
                n_zero += is_zero
            low = high
        one = jnp.sum(one, axis=0, keepdims=True)
        zero = jnp.sum(zero, axis=0, keepdims=True)
        if late:
            targets = {0: [(outs[0], 0)], 1: [(outs[1], 0)], 2: [(outs[2], 0)]}
            targets |= {3: [(outs[2], CHUNK)], 4: [(outs[2], 2 * CHUNK), (outs[3], 0)]}
            earlier = {0: before[0], 2: before[1]}.get(chunk)
        else:
            targets, earlier = {0: [(outs[0], 0)], 2: [(outs[1], 0)]}, None
        values = [one, zero, n_one, n_zero]
        if earlier is not None:
            values = [earlier[i : i + 1, :] + value for i, value in enumerate(values)]
        for out, place_at in targets[chunk]:
            for i, value in enumerate(values):
                out[i : i + 1, pl.ds(place_at, size)] = value


def pair_sums(place, col_args, row_args, col_cuts, before):
    late = before is not None
    total = 4 * CHUNK + BLOCK if late else 3 * CHUNK
    used, depth = (5 if late else 2) * CHUNK, sum(size for _, _, size in col_cuts)
    feats = col_args[0].shape[1]
    vmem = pl.BlockSpec(memory_space=pltpu.VMEM)
    widths = [CHUNK, CHUNK, 2 * CHUNK + BLOCK, BLOCK] if late else [CHUNK, CHUNK]
    names = NAMES if late else NAMES[:6]
    before = list(before or [])
    return pl.pallas_call(
        functools.partial(
            pair_kernel, col_cuts=tuple(col_cuts), n_cols_args=len(col_args), late=late
        ),
        in_specs=[pl.BlockSpec(memory_space=pltpu.SMEM)]
        + [vmem] * (len(before) + len(col_args) + len(names)),
        out_specs=[vmem] * len(widths),
        out_shape=[jax.ShapeDtypeStruct((4, width), jnp.float32) for width in widths],
        scratch_shapes=[
            pltpu.VMEM((total, feats), jnp.bfloat16),
            pltpu.VMEM((depth, feats), jnp.bfloat16),
        ],
        compiler_params=pltpu.CompilerParams(vmem_limit_bytes=18 * 2**20),
        cost_estimate=pl.CostEstimate(
            flops=6 * used * depth * feats,
            bytes_accessed=6 * (used + depth) * feats,
            transcendentals=0,
        ),
        name="late" if late else "early",
    )(place, *before, *col_args, *[row_args[name] for name in names])


def shards(showers, geometry, pattern, bins, sources):
    y = lax.axis_index("layer")
    s = lax.axis_index("shower")
    x, z, c = s // (NZ * NC), (s // NC) % NZ, s % NC
    feats = geometry.shape[1]
    blocks = bins.shape[0]

    codes = (bins + BINS * sources + 1).astype(jnp.float32)
    line = lax.broadcasted_iota(jnp.int32, (TAG, feats), 0)
    lane = lax.broadcasted_iota(jnp.int32, (TAG, feats), 1) // PIECE
    which = jnp.where(line == blocks, lane, line)
    tag = jnp.zeros((TAG, feats), jnp.float32)
    for group in range(blocks):
        tag = jnp.where(which == group, codes[group], tag)
    tag = tag.astype(jnp.bfloat16)

    partial_sums = raw_partial(showers, geometry, pattern).reshape(blocks, NY, PIECE, feats)

    def share(turn):
        part = lax.dynamic_index_in_dim(partial_sums, (y + turn) % NY, 1, keepdims=False)
        return part.reshape(BLOCK, feats)

    raw = share(0)
    arrived = [permute(share(turn).astype(jnp.float16), along_y(turn)) for turn in (2, 1, 3)]
    for part in arrived:
        raw = raw + part.astype(jnp.float32)
    scale = lax.rsqrt(jnp.mean(raw * raw, axis=1, keepdims=True) + 1e-05)
    own = jnp.concatenate([tag, (raw * scale).astype(jnp.bfloat16)], axis=0)

    fence = lambda *values: lax.optimization_barrier(values)
    tagged = BLOCK + TAG
    y_way = lambda y, x, z, c: ((y + 1 - 2 * c) % NY, x, z, c)
    own_t = permute(own, swap_core)
    chip = jnp.where(c == 0, jnp.concatenate([own, own_t]), jnp.concatenate([own_t, own]))
    z1 = permute(chip, same_core)
    y1 = permute(chip, y_way)
    x1 = permute(own, swap_x)
    z1, x1 = fence(z1, x1)

    z2 = permute(z1, same_core)
    near_one, far_one = y1[TAG:tagged], y1[tagged + TAG :]
    y1_mine = jnp.where(c == 0, near_one, far_one)
    y1_other = jnp.where(c == 0, far_one, near_one)
    y1_mine, y1_other = fence(y1_mine, y1_other)
    y2 = permute(y1_mine, y_way)
    xa = permute(y1_mine, swap_x)
    x1_t = permute(x1, swap_core)
    z1, z2, y2, xa, y1, x1_t = fence(z1, z2, y2, xa, y1, x1_t)

    z3 = permute(z2, same_core)
    xb = permute(y1_other, swap_x)
    y1_t = permute(y1, swap_core)
    head = TAG + PIECE
    odd_rows = jnp.concatenate([own[TAG:head], y1_t[TAG:head], y2[:PIECE], y1[TAG:head]], axis=0)
    at_start = lambda y, x, z, c: z == 0 and c == 0
    odd_at = [
        permute(
            odd_rows,
            lambda y, x, z, c, to=to: (y, to, z, c),
            keep=lambda *a: a[1] == 2 and at_start(*a),
        )
        for to in (1, 0)
    ]
    y2_t = permute(y2, swap_core)
    xa_t = permute(xa, swap_core)
    z2, z3, y2, xb, y1_t, y2_t, xa_t, odd_at[0] = fence(
        z2, z3, y2, xb, y1_t, y2_t, xa_t, odd_at[0]
    )

    z4 = permute(jnp.where(c == 0, z3[:tagged], z3[tagged:]), same_core)
    held = [chip, z1, z2, z3, z3, z3, z2, z1]
    piece = permute(
        lax.select_n(z, *[value[:head] for value in held]),
        lambda y, x, z, c: (y, 1, z + 1 - c, c),
        keep=lambda y, x, z, c: x == 2 and (z < 4 if c == 0 else z == 0 or z > 4),
    )
    w2 = permute(y2, swap_x)
    xb_t = permute(xb, swap_core)
    col_args = [own, z1, z2, z3]
    col_cuts = [(0, TAG, BLOCK)]
    for arg in (1, 2, 3):
        col_cuts += [(arg, TAG, BLOCK), (arg, tagged + TAG, BLOCK)]
    row_args = dict(own=own, own_t=own_t, y1=y1, y1_t=y1_t, y2=y2, y2_t=y2_t)
    place = jnp.stack([((x < 2) & (z == 0)).astype(jnp.int32), c.astype(jnp.int32)])
    early = pair_sums(place, col_args, row_args, col_cuts, None)
    w2, odd_at[0], odd_at[1], early, piece = fence(w2, odd_at[0], odd_at[1], early, piece)
    w2_t = permute(w2, swap_core)
    odd_rows = odd_at[0] + odd_at[1]
    odd_rows = odd_rows + permute(
        odd_rows, swap_core, keep=lambda *a: a[1] < 2 and at_start(*a)
    )
    row_args |= dict(x1=x1, x1_t=x1_t, xa=xa, xb=xb, xa_t=xa_t, xb_t=xb_t, w2=w2, w2_t=w2_t)
    row_args["odd"] = odd_rows
    col_cuts += [(4, TAG, BLOCK), (5, TAG, PIECE)]
    near, far, theirs, odd_stats = pair_sums(
        place, col_args + [z4, piece], row_args, col_cuts, early
    )

    theirs = permute(theirs, swap_core)
    kept = near + theirs[:, :CHUNK] + permute(far + theirs[:, CHUNK : 2 * CHUNK], swap_x)
    odd_stats = odd_stats + theirs[:, 2 * CHUNK :]
    odd_total = jnp.zeros_like(odd_stats)
    for start in (0, 1):
        odd_total = odd_total + permute(
            odd_stats,
            lambda y, x, z, c: (y, 2, z, c),
            keep=lambda *a, start=start: a[1] == start and at_start(*a),
        )
    odd_total = odd_total.reshape(4, NY, PIECE)
    kept = kept.reshape(4, NY, BLOCK) + jnp.pad(odd_total, ((0, 0), (0, 0), (0, BLOCK - PIECE)))
    total = kept
    for turn in (2, 1, 3):
        total = total + jnp.roll(permute(kept, along_y(turn)), -turn, axis=1)
    weight = 1.0 / (PIECE * 32.0**3)
    proof = (total[0] / total[2] - total[1] / total[3]) * weight
    proof = jnp.concatenate([proof, proof], axis=0)
    proof = lax.dynamic_slice_in_dim(proof, (NY - y) % NY, NY, 0).reshape(NY, blocks, PIECE)
    return jnp.transpose(proof, (1, 0, 2)).reshape(-1)


def solution(mesh):
    placed = (P("shower", "layer"), P("layer", None), P("layer", None), P("shower"), P("shower"))
    return jax.shard_map(shards, mesh=mesh, in_specs=placed, out_specs=P("shower"), check_vma=False)
```

```python
import functools

import jax
import jax.numpy as jnp
from jax import lax
from jax.experimental import pallas as pl
from jax.experimental.pallas import tpu as pltpu
from jax.sharding import PartitionSpec as P

BLOCK = 128
PIECE = 32
TAG = 16
BINS = 8
CHUNK = 512
EARLY = 7
AXES = ("layer", "shower")
NY, NX, NZ, NC = 4, 4, 8, 2


def flat(y, x, z, c):
    return y * (NX * NZ * NC) + (x * NZ + z) * NC + c


def permute(value, move, keep=lambda y, x, z, c: True):
    pairs = [
        (flat(y, x, z, c), flat(*move(y, x, z, c)))
        for y in range(NY)
        for x in range(NX)
        for z in range(NZ)
        for c in range(NC)
        if keep(y, x, z, c)
    ]
    return lax.ppermute(value, AXES, pairs)


def along_y(step):
    return lambda y, x, z, c: ((y + step) % NY, x, z, c)


def along_z(step):
    return lambda y, x, z, c: (y, x, (z + step) % NZ, c)


def flip_z(bit):
    return lambda y, x, z, c: (y, x, z ^ bit, c)


def swap_x(y, x, z, c):
    return (y, x ^ 1, z, c)


def swap_core(y, x, z, c):
    return (y, x, z, 1 - c)


def same_core(y, x, z, c):
    return (y, x, (z + 1 - 2 * c) % NZ, c)


def cross_core(y, x, z, c):
    return (y, x, (z - 1 + 2 * c) % NZ, 1 - c)


def raw_kernel(pattern, showers, geometry, out, masked):
    step = pl.program_id(0)
    layers = pattern.shape[1]
    cells = geometry.shape[0] // layers
    per = geometry.shape[1] // BLOCK
    for layer in range(layers):
        for part in range(per):
            rows = pl.ds(layer * cells, cells)
            cols = pl.ds(part * BLOCK, BLOCK)
            on = pattern[step * per + part, layer].astype(jnp.float32).astype(jnp.bfloat16)
            masked[rows, cols] = geometry[rows, cols] * on
    out[...] = lax.dot_general(
        showers[...], masked[...], (((0,), (0,)), ((), ())), preferred_element_type=jnp.float32
    )


def raw_partial(showers, geometry, pattern):
    rows, depth = showers.shape
    feats = geometry.shape[1]
    width = 512
    return pl.pallas_call(
        raw_kernel,
        grid=(feats // width,),
        in_specs=[
            pl.BlockSpec(memory_space=pltpu.SMEM),
            pl.BlockSpec((depth, rows), lambda i: (0, 0)),
            pl.BlockSpec((depth, width), lambda i: (0, i)),
        ],
        out_specs=pl.BlockSpec((rows, width), lambda i: (0, i)),
        out_shape=jax.ShapeDtypeStruct((rows, feats), jnp.float32),
        scratch_shapes=[pltpu.VMEM((depth, width), jnp.bfloat16)],
        compiler_params=pltpu.CompilerParams(vmem_limit_bytes=60 * 2**20),
        cost_estimate=pl.CostEstimate(
            flops=2 * rows * depth * feats, bytes_accessed=8 * 2**20, transcendentals=0
        ),
        name="raw",
    )(pattern.T, showers.T, geometry)


NAMES = ("own", "own_t", "y1", "y1_t", "y2", "y2_t", "x1", "x1_t", "xa", "xb", "xa_t", "xb_t", "w2", "w2_t", "odd")
TAG_OF = ("own", "x1", "own_t", "x1_t", "own")


def pair_kernel(*refs, col_cuts, n_cols_args, late):
    n_cols = len(col_cuts)
    names = NAMES if late else NAMES[:6]
    place, refs = refs[0], refs[1:]
    before, refs = refs[: 2 * late], refs[2 * late :]
    col_args, refs = refs[:n_cols_args], refs[n_cols_args:]
    held, refs = dict(zip(names, refs)), refs[len(names) :]
    outs, refs = refs[: 4 if late else 2], refs[4 if late else 2 :]
    rows_at, cols_at = refs
    odd_here, core = place[0], place[1]
    tagged = BLOCK + TAG

    starts = [sum(size for _, _, size in col_cuts[:at]) for at in range(n_cols)]
    depth = sum(size for _, _, size in col_cuts)
    for at, (arg, first, size) in enumerate(col_cuts):
        cols_at[pl.ds(starts[at], size), :] = col_args[arg][pl.ds(first, size), :]
    chunks = (0, 2, 1, 3, 4) if late else (0, 2)
    turn = jnp.where(core == 0, 3, 1)
    side = [2 * CHUNK * jnp.where(core == b, 0, 1) for b in range(NC)]

    def rows(name, first, at):
        at = at if isinstance(at, int) else pl.multiple_of(at, BLOCK)
        rows_at[pl.ds(at, BLOCK), :] = held[name][pl.ds(first, BLOCK), :]

    rows("own", TAG, 0)
    rows("y2", 0, 2 * BLOCK)
    for b in range(NC):
        rows("y1", TAG + b * tagged, side[b] + turn * BLOCK)
        rows("y1_t", TAG + b * tagged, side[b] + (NY - turn) * BLOCK)
    rows("own_t", TAG, 2 * CHUNK)
    rows("y2_t", 0, 2 * CHUNK + 2 * BLOCK)
    if late:
        rows("x1", TAG, CHUNK)
        rows("w2", 0, CHUNK + 2 * BLOCK)
        rows("xa", 0, CHUNK + turn * BLOCK)
        rows("xb", 0, 3 * CHUNK + turn * BLOCK)
        rows("xa_t", 0, 3 * CHUNK + (NY - turn) * BLOCK)
        rows("xb_t", 0, CHUNK + (NY - turn) * BLOCK)
        rows("x1_t", TAG, 3 * CHUNK)
        rows("w2_t", 0, 3 * CHUNK + 2 * BLOCK)
        rows("odd", 0, 4 * CHUNK)

    def bin_of(code):
        source = (code >= BINS).astype(jnp.float32)
        return code - BINS * source, source

    for chunk in chunks:
        first = chunk * CHUNK
        odd = chunk == 4
        size = BLOCK if odd else CHUNK
        tag = held[TAG_OF[chunk]][4:5, pl.ds(0, BLOCK)].astype(jnp.float32) - 1.0
        bins, _ = bin_of(tag)
        if odd:
            bins = jnp.where(odd_here > 0, bins, -2.0)
        bins = jnp.concatenate([bins] * (size // BLOCK), axis=1)
        one = jnp.zeros((8, size), jnp.float32)
        zero = jnp.zeros((8, size), jnp.float32)
        n_one = jnp.zeros((1, size), jnp.float32)
        n_zero = jnp.zeros((1, size), jnp.float32)
        low = EARLY * BLOCK if late and chunk in (0, 2) else 0
        while low < depth:
            high = depth if depth - low < 3 * BLOCK else low + 2 * BLOCK
            products = lax.dot_general(
                cols_at[pl.ds(low, high - low), :],
                rows_at[pl.ds(first, size), :],
                (((1,), (1,)), ((), ())),
                preferred_element_type=jnp.float32,
            )
            shifted = products + 32.0
            cubes = shifted * shifted * shifted
            for group in range(low // PIECE, high // PIECE):
                at = group * PIECE // BLOCK
                if odd and col_cuts[at][2] == PIECE:
                    continue
                block = cubes[group * PIECE - low : (group + 1) * PIECE - low]
                if first == 0 and at == 0:
                    lane = lax.broadcasted_iota(jnp.int32, block.shape, 1)
                    sub = lax.broadcasted_iota(jnp.int32, block.shape, 0)
                    block = jnp.where(lane == sub + group * PIECE, 0.0, block)
                part = (block[0:8] + block[8:16]) + (block[16:24] + block[24:32])
                arg, place_of, _ = col_cuts[at]
                row = place_of - TAG + group % 4
                code = col_args[arg][pl.ds(row, 1), pl.ds(0, size)].astype(jnp.float32) - 1.0
                bin_id, source = bin_of(code)
                match = (bins == bin_id).astype(jnp.float32)
                is_one = match * source
                is_zero = match - is_one
                one += is_one * part
                zero += is_zero * part
                n_one += is_one
                n_zero += is_zero
            low = high
        one = jnp.sum(one, axis=0, keepdims=True)
        zero = jnp.sum(zero, axis=0, keepdims=True)
        if late:
            targets = {0: [(outs[0], 0)], 1: [(outs[1], 0)], 2: [(outs[2], 0)]}
            targets |= {3: [(outs[2], CHUNK)], 4: [(outs[2], 2 * CHUNK), (outs[3], 0)]}
            earlier = {0: before[0], 2: before[1]}.get(chunk)
        else:
            targets, earlier = {0: [(outs[0], 0)], 2: [(outs[1], 0)]}, None
        values = [one, zero, n_one, n_zero]
        if earlier is not None:
            values = [earlier[i : i + 1, :] + value for i, value in enumerate(values)]
        for out, place_at in targets[chunk]:
            for i, value in enumerate(values):
                out[i : i + 1, pl.ds(place_at, size)] = value


def pair_sums(place, col_args, row_args, col_cuts, before):
    late = before is not None
    total = 4 * CHUNK + BLOCK if late else 3 * CHUNK
    used, depth = (5 if late else 2) * CHUNK, sum(size for _, _, size in col_cuts)
    feats = col_args[0].shape[1]
    vmem = pl.BlockSpec(memory_space=pltpu.VMEM)
    widths = [CHUNK, CHUNK, 2 * CHUNK + BLOCK, BLOCK] if late else [CHUNK, CHUNK]
    names = NAMES if late else NAMES[:6]
    before = list(before or [])
    return pl.pallas_call(
        functools.partial(
            pair_kernel, col_cuts=tuple(col_cuts), n_cols_args=len(col_args), late=late
        ),
        in_specs=[pl.BlockSpec(memory_space=pltpu.SMEM)]
        + [vmem] * (len(before) + len(col_args) + len(names)),
        out_specs=[vmem] * len(widths),
        out_shape=[jax.ShapeDtypeStruct((4, width), jnp.float32) for width in widths],
        scratch_shapes=[
            pltpu.VMEM((total, feats), jnp.bfloat16),
            pltpu.VMEM((depth, feats), jnp.bfloat16),
        ],
        compiler_params=pltpu.CompilerParams(vmem_limit_bytes=18 * 2**20),
        cost_estimate=pl.CostEstimate(
            flops=6 * used * depth * feats,
            bytes_accessed=6 * (used + depth) * feats,
            transcendentals=0,
        ),
        name="late" if late else "early",
    )(place, *before, *col_args, *[row_args[name] for name in names])


def shards(showers, geometry, pattern, bins, sources):
    y = lax.axis_index("layer")
    s = lax.axis_index("shower")
    x, z, c = s // (NZ * NC), (s // NC) % NZ, s % NC
    feats = geometry.shape[1]
    blocks = bins.shape[0]

    codes = (bins + BINS * sources + 1).astype(jnp.float32)
    line = lax.broadcasted_iota(jnp.int32, (TAG, feats), 0)
    lane = lax.broadcasted_iota(jnp.int32, (TAG, feats), 1) // PIECE
    which = jnp.where(line == blocks, lane, line)
    tag = jnp.zeros((TAG, feats), jnp.float32)
    for group in range(blocks):
        tag = jnp.where(which == group, codes[group], tag)
    tag = tag.astype(jnp.bfloat16)

    partial_sums = raw_partial(showers, geometry, pattern).reshape(blocks, NY, PIECE, feats)

    def share(turn):
        part = lax.dynamic_index_in_dim(partial_sums, (y + turn) % NY, 1, keepdims=False)
        return part.reshape(BLOCK, feats)

    raw = share(0)
    arrived = [permute(share(turn).astype(jnp.float16), along_y(turn)) for turn in (2, 1, 3)]
    for part in arrived:
        raw = raw + part.astype(jnp.float32)
    scale = lax.rsqrt(jnp.mean(raw * raw, axis=1, keepdims=True) + 1e-05)
    own = jnp.concatenate([tag, (raw * scale).astype(jnp.bfloat16)], axis=0)

    fence = lambda *values: lax.optimization_barrier(values)
    tagged = BLOCK + TAG
    y_way = lambda y, x, z, c: ((y + 1 - 2 * c) % NY, x, z, c)
    own_t = permute(own, swap_core)
    chip = jnp.where(c == 0, jnp.concatenate([own, own_t]), jnp.concatenate([own_t, own]))
    z1 = permute(chip, same_core)
    y1 = permute(chip, y_way)
    x1 = permute(own, swap_x)
    z1, x1 = fence(z1, x1)

    z2 = permute(z1, same_core)
    near_one, far_one = y1[TAG:tagged], y1[tagged + TAG :]
    y1_mine = jnp.where(c == 0, near_one, far_one)
    y1_other = jnp.where(c == 0, far_one, near_one)
    y1_mine, y1_other = fence(y1_mine, y1_other)
    y2 = permute(y1_mine, y_way)
    xa = permute(y1_mine, swap_x)
    x1_t = permute(x1, swap_core)
    z1, z2, y2, xa, y1, x1_t = fence(z1, z2, y2, xa, y1, x1_t)

    z3 = permute(z2, same_core)
    xb = permute(y1_other, swap_x)
    y1_t = permute(y1, swap_core)
    head = TAG + PIECE
    odd_rows = jnp.concatenate([own[TAG:head], y1_t[TAG:head], y2[:PIECE], y1[TAG:head]], axis=0)
    at_start = lambda y, x, z, c: z == 0 and c == 0
    odd_at = [
        permute(
            odd_rows,
            lambda y, x, z, c, to=to: (y, to, z, c),
            keep=lambda *a: a[1] == 2 and at_start(*a),
        )
        for to in (1, 0)
    ]
    y2_t = permute(y2, swap_core)
    xa_t = permute(xa, swap_core)
    z2, z3, y2, y1_t, y2_t, xa_t, odd_at[0] = fence(
        z2, z3, y2, y1_t, y2_t, xa_t, odd_at[0]
    )

    z4 = permute(jnp.where(c == 0, z3[:tagged], z3[tagged:]), same_core)
    held = [chip, z1, z2, z3, z3, z3, z2, z1]
    piece = permute(
        lax.select_n(z, *[value[:head] for value in held]),
        lambda y, x, z, c: (y, 1, z + 1 - c, c),
        keep=lambda y, x, z, c: x == 2 and (z < 4 if c == 0 else z == 0 or z > 4),
    )
    w2 = permute(y2, swap_x)
    xb_t = permute(xb, swap_core)
    col_args = [own, z1, z2, z3]
    col_cuts = [(0, TAG, BLOCK)]
    for arg in (1, 2, 3):
        col_cuts += [(arg, TAG, BLOCK), (arg, tagged + TAG, BLOCK)]
    row_args = dict(own=own, own_t=own_t, y1=y1, y1_t=y1_t, y2=y2, y2_t=y2_t)
    place = jnp.stack([((x < 2) & (z == 0)).astype(jnp.int32), c.astype(jnp.int32)])
    early = pair_sums(place, col_args, row_args, col_cuts, None)
    w2, odd_at[0], odd_at[1], early, piece = fence(w2, odd_at[0], odd_at[1], early, piece)
    w2_t = permute(w2, swap_core)
    odd_rows = odd_at[0] + odd_at[1]
    odd_rows = odd_rows + permute(
        odd_rows, swap_core, keep=lambda *a: a[1] < 2 and at_start(*a)
    )
    row_args |= dict(x1=x1, x1_t=x1_t, xa=xa, xb=xb, xa_t=xa_t, xb_t=xb_t, w2=w2, w2_t=w2_t)
    row_args["odd"] = odd_rows
    col_cuts += [(4, TAG, BLOCK), (5, TAG, PIECE)]
    near, far, theirs, odd_stats = pair_sums(
        place, col_args + [z4, piece], row_args, col_cuts, early
    )

    theirs = permute(theirs, swap_core)
    kept = near + theirs[:, :CHUNK] + permute(far + theirs[:, CHUNK : 2 * CHUNK], swap_x)
    odd_stats = odd_stats + theirs[:, 2 * CHUNK :]
    odd_total = jnp.zeros_like(odd_stats)
    for start in (0, 1):
        odd_total = odd_total + permute(
            odd_stats,
            lambda y, x, z, c: (y, 2, z, c),
            keep=lambda *a, start=start: a[1] == start and at_start(*a),
        )
    odd_total = odd_total.reshape(4, NY, PIECE)
    kept = kept.reshape(4, NY, BLOCK) + jnp.pad(odd_total, ((0, 0), (0, 0), (0, BLOCK - PIECE)))
    total = kept
    for turn in (2, 1, 3):
        total = total + jnp.roll(permute(kept, along_y(turn)), -turn, axis=1)
    weight = 1.0 / (PIECE * 32.0**3)
    proof = (total[0] / total[2] - total[1] / total[3]) * weight
    proof = jnp.concatenate([proof, proof], axis=0)
    proof = lax.dynamic_slice_in_dim(proof, (NY - y) % NY, NY, 0).reshape(NY, blocks, PIECE)
    return jnp.transpose(proof, (1, 0, 2)).reshape(-1)


def solution(mesh):
    placed = (P("shower", "layer"), P("layer", None), P("layer", None), P("shower"), P("shower"))
    return jax.shard_map(shards, mesh=mesh, in_specs=placed, out_specs=P("shower"), check_vma=False)
```
